128 devices in a mesh: row: 8 (over x, core), col: 16 (over z, y).
Axes of the slice: x: 4, y: 4, z: 4, core: 2. Of those that a mesh axis runs over, the one named last changes fastest.
Arguments:
- table: bfloat16 [131072, 256], P(('row', 'col')), may hold values from -6 to 6
- home: int32 [65536], P(('row', 'col')), may hold values from 0 to 65535, as said below
- degree: int32 [131072], P(('row', 'col')), may hold values from 2 to 8
- tile_rows: int32 [8, 16, 704], P('row', 'col'), may hold values from 0 to 63, as said below
- tile_cols: int32 [8, 16, 704], P('row', 'col'), may hold values from 0 to 127
- tile_count: int32 [8, 16], P('row', 'col'), may hold values from 88 to 704, as said below
- tile_values: bfloat16 [8, 16, 704, 128, 128], P('row', 'col'), may hold values from 0 to 1
- w_self: bfloat16 [256, 256], replicated, may hold values from -0.375 to 0.375
- w_neigh: bfloat16 [256, 256], replicated, may hold values from -0.375 to 0.375
- bias: bfloat16 [256], replicated, may hold values from -3 to 3
Outputs:
- layer_out: bfloat16 [131072, 256], P(('row', 'col'))
The draws below stay inside these ranges and needn't reach their ends.
Inputs may be any that keep to these rules, and one draw needn't show every extreme that they name: home is a permutation of the node blocks. Device d in row-major order of (row, col) owns node blocks d * 512 to (d + 1) * 512 - 1. Of the hash blocks of one device's shard at most 6 belong to one owner, and some pair of devices reaches 6 in every draw. Within one grid cell the live slots name distinct (tile_rows, tile_cols) pairs. `tile_count`: one grid cell has exactly 704 live slots; the others have from 88 to 352.
All inputs are finite; a program needn't handle non-finite values.
Results may differ from the reference program's by a relative error of at most 0.02.
Values may be sent and summed in bfloat16 or wider, within the bound.
No kernel may reach another device: no remote copies, remote signals or barrier semaphores. Data moves between devices by JAX's collectives and lax.ppermute only.
A program may use at most 192 MiB of HBM per device.

```python
import jax
import jax.numpy as jnp
from jax import lax

FEAT = 256
TILE = 128
ROWS_DEV = 1024
NNZ_MAX = 704
NODES = 131072
BLOCKS_DEV = 512
CAP = 6
N_ROW = 8
N_COL = 16


def draw_home(key, part):
    key = jax.random.fold_in(key, 11)
    devices = N_ROW * N_COL
    keys = jax.random.split(key, 5)
    shuffle = jax.random.permutation(keys[0], devices).astype(jnp.int32)
    heavy = jax.random.randint(keys[1], (), 0, devices)
    units = jax.random.permutation(keys[2], (devices - 1) * CAP)[:BLOCKS_DEV - CAP].astype(jnp.int32) // CAP
    others = jnp.zeros((devices - 1,), jnp.int32).at[units].add(1)
    shifts = jnp.arange(devices, dtype=jnp.int32)
    other_pos = jnp.clip(jnp.where(shifts < heavy, shifts, shifts - 1), 0, devices - 2)
    counts = jnp.where(shifts == heavy, CAP, others[other_pos]).astype(jnp.int32)
    ends = jnp.cumsum(counts).astype(jnp.int32)
    slots = jnp.arange(BLOCKS_DEV, dtype=jnp.int32)
    segment = jnp.sum((ends[None, :] <= slots[:, None]).astype(jnp.int32), axis=1)
    sigma = jax.vmap(lambda k: jax.random.permutation(k, BLOCKS_DEV))(jax.random.split(keys[3], devices)).astype(jnp.int32)
    rho = jax.vmap(lambda k: jax.random.permutation(k, BLOCKS_DEV))(jax.random.split(keys[4], devices)).astype(jnp.int32)
    receiver = (shuffle[:, None] + segment[None, :]) % devices
    table_pos = shifts[:, None] * BLOCKS_DEV + sigma
    node_block = receiver * BLOCKS_DEV + rho[receiver, slots[None, :]]
    result = jnp.zeros((devices * BLOCKS_DEV,), jnp.int32)
    return result.at[table_pos.reshape(-1)].set(node_block.reshape(-1))


def tile_layout(key):
    cells = N_ROW * N_COL
    per_row = N_COL * ROWS_DEV // TILE
    grid_slots = N_ROW * ROWS_DEV // TILE * per_row
    chosen = jax.vmap(lambda k: jax.random.permutation(k, grid_slots)[:NNZ_MAX])(jax.random.split(key, cells)).astype(jnp.int32)
    return ((chosen // per_row).reshape(N_ROW, N_COL, NNZ_MAX), (chosen % per_row).reshape(N_ROW, N_COL, NNZ_MAX))


def draw_tile_rows(key, part):
    rows_part, cols_part = tile_layout(key)
    return rows_part


def draw_tile_cols(key, part):
    rows_part, cols_part = tile_layout(key)
    return cols_part


def draw_tile_count(key, part):
    key = jax.random.fold_in(key, 23)
    keys = jax.random.split(key, 2)
    counts = jax.random.randint(keys[0], (N_ROW * N_COL,), NNZ_MAX // 8, NNZ_MAX // 2 + 1).astype(jnp.int32)
    heavy = jax.random.randint(keys[1], (), 0, N_ROW * N_COL)
    counts = counts.at[heavy].set(NNZ_MAX)
    return counts.reshape(N_ROW, N_COL)


def set_ends(array, own_key, least, largest):
    spot = [jax.random.randint(jax.random.fold_in(own_key, axis), (), 0, length) for axis, length in enumerate(array.shape)]
    widest = array.shape.index(max(array.shape))
    beside = spot[:widest] + [(spot[widest] + 1) % array.shape[widest]] + spot[widest + 1:]
    return array.at[tuple(spot)].set(least).at[tuple(beside)].set(largest)


def level_of(stream_key, extent, cuts, least, top_value):
    def one(axis_at, parts):
        draws = jax.random.uniform(jax.random.fold_in(jax.random.fold_in(stream_key, 6), axis_at), (parts,), jnp.float32, least / len(cuts), top_value / len(cuts))
        return jnp.repeat(jnp.exp(draws), extent[axis_at] // parts).reshape((-1,) + (1,) * (len(extent) - axis_at - 1))

    factor_of = one(*cuts[0])
    for cut in cuts[1:]:
        factor_of = factor_of * one(*cut)
    return factor_of


def noise(stream_key, dims, deviation, reach, pieces=(), kind=jnp.bfloat16):
    gain = level_of(stream_key, dims, pieces, -0.22, 0.18) if pieces else 1.0
    entries = jax.random.normal(stream_key, dims, jnp.float32) * deviation * gain
    return jnp.minimum(jnp.maximum(entries, -reach), reach).astype(kind)


def setup_inputs(seed: int = 0) -> dict:
    key_list = jax.random.split(jax.random.key(seed), 11)
    return {
        "table": noise(key_list[0], (NODES, FEAT), 1.0, 6.0, ((0, 128),)),
        "home": draw_home(jax.random.fold_in(key_list[10], 71), 0),
        "degree": set_ends(jax.random.randint(key_list[2], (NODES,), 2, 9), jax.random.fold_in(key_list[2], 1), 2, 8).astype(jnp.int32),
        "tile_rows": draw_tile_rows(jax.random.fold_in(key_list[10], 71), 0),
        "tile_cols": draw_tile_cols(jax.random.fold_in(key_list[10], 71), 0),
        "tile_count": draw_tile_count(jax.random.fold_in(key_list[10], 71), 0),
        "tile_values": jnp.clip(1.0 * jax.random.uniform(key_list[6], (N_ROW, N_COL, NNZ_MAX, TILE, TILE), jnp.float32) ** level_of(key_list[6], (N_ROW, N_COL, NNZ_MAX, TILE, TILE), ((0, 8), (1, 16)), -0.2, 0.2), 0.0, 1.0).astype(jnp.bfloat16),
        "w_self": noise(key_list[7], (FEAT, FEAT), FEAT ** -0.5, 0.375),
        "w_neigh": noise(key_list[8], (FEAT, FEAT), FEAT ** -0.5, 0.375),
        "bias": noise(key_list[9], (FEAT,), 0.5, 3.0),
    }


def reference(table, home, degree, tile_rows, tile_cols, tile_count, tile_values, w_self, w_neigh, bias):
    nodes, feature_width = table.shape
    block_count = home.shape[0]
    block_rows = nodes // block_count
    features = jnp.zeros((block_count, block_rows * feature_width), table.dtype)
    features = features.at[home].set(table.reshape(block_count, block_rows * feature_width))
    features = features.reshape(nodes, feature_width)
    grid_rows, grid_cols = tile_count.shape
    rows_per = nodes // (grid_rows * grid_cols)
    tile_size = tile_values.shape[-1]
    slot_count = tile_values.shape[2]
    dest_tiles = grid_rows * rows_per // tile_size

    def cell_partial(grid_row, grid_col):
        panel_rows = lax.dynamic_slice_in_dim(features, grid_row * grid_cols * rows_per, grid_cols * rows_per, 0)
        panel_rows = panel_rows.reshape(-1, tile_size, feature_width).astype(jnp.float32)
        weights = tile_values[grid_row, grid_col].astype(jnp.float32)
        sources = panel_rows[tile_cols[grid_row, grid_col]]
        products = jnp.einsum("gab,gbf->gaf", weights, sources)
        is_live = jnp.arange(slot_count, dtype=jnp.int32) < tile_count[grid_row, grid_col]
        products = jnp.where(is_live[:, None, None], products, jnp.float32(0.0))
        accumulated = jnp.zeros((dest_tiles, tile_size, feature_width), jnp.float32)
        accumulated = accumulated.at[tile_rows[grid_row, grid_col]].add(products)
        rounded = lax.optimization_barrier(accumulated.reshape(grid_rows * rows_per, feature_width).astype(jnp.bfloat16))
        return rounded.astype(jnp.float32)

    def column_sum(grid_col):
        def add_cell(carry, grid_row):
            return carry + cell_partial(grid_row, grid_col), None
        start = jnp.zeros((grid_rows * rows_per, feature_width), jnp.float32)
        return lax.scan(add_cell, start, jnp.arange(grid_rows, dtype=jnp.int32))[0]

    sums = lax.map(column_sum, jnp.arange(grid_cols, dtype=jnp.int32))
    neighbor_sum = sums.reshape(grid_cols, grid_rows, rows_per, feature_width).transpose(1, 0, 2, 3).reshape(nodes, feature_width)
    neighbor_mean = (neighbor_sum / degree.astype(jnp.float32)[:, None]).astype(jnp.bfloat16)
    total = jnp.dot(features, w_self, preferred_element_type=jnp.float32)
    total = total + jnp.dot(neighbor_mean, w_neigh, preferred_element_type=jnp.float32)
    total = total + bias.astype(jnp.float32)[None, :]
    return jnp.maximum(total, jnp.float32(0.0)).astype(jnp.bfloat16)
```

```python
import functools

import jax
import jax.numpy as jnp
from jax import lax
from jax.experimental import pallas as pl
from jax.experimental.pallas import tpu as pltpu
from jax.sharding import PartitionSpec as P

SLOT_ROWS = 16
POS_ROW = 12
PAIRS = 8
BLOCK = 2 * PAIRS
BUFS = 4
LIST = 1152
MB = 1 << 20


def iota(shape, dim):
    return lax.broadcasted_iota(jnp.int32, shape, dim)


def onehot(mask):
    return jnp.where(mask, 1.0, 0.0).astype(jnp.bfloat16)


def pack_kernel(home_ref, table_ref, out_ref):
    rows = table_ref.shape[0]
    home = home_ref[...]
    dest = home >> 9
    pos = home & 511
    dest_f = dest.astype(jnp.float32)
    dest_col = jnp.broadcast_to(dest_f, (128, rows)).T[:, :1]
    before = (dest_col == dest_f) & (iota((rows, rows), 0) < iota((rows, rows), 1))
    rank = jnp.sum(jnp.where(before, 1.0, 0.0), axis=0, keepdims=True).astype(jnp.int32)
    place = dest * SLOT_ROWS + rank
    outs = out_ref.shape[0]
    spread = onehot(iota((outs, rows), 0) == place)
    data = jnp.dot(spread, table_ref[...], preferred_element_type=jnp.float32)
    lane = iota((256, rows), 0)
    high = jnp.broadcast_to(((pos >> 1) + 1).astype(jnp.float32), (256, rows))
    low = jnp.broadcast_to((pos & 1).astype(jnp.float32), (256, rows))
    marks = jnp.where(lane == rank, high, jnp.where(lane == rank + 128, low, 0.0)).astype(
        jnp.bfloat16
    )
    owner = onehot(iota((128, rows), 0) == dest)
    pos_rows = lax.dot_general(
        owner, marks, (((1,), (1,)), ((), ())), preferred_element_type=jnp.float32
    ).astype(jnp.bfloat16)
    lift = onehot(iota((outs, 128), 0) == iota((outs, 128), 1) * SLOT_ROWS + POS_ROW)
    data = data + jnp.dot(lift, pos_rows, preferred_element_type=jnp.float32)
    out_ref[...] = data.astype(jnp.bfloat16)


def unpack_kernel(in_ref, out_ref):
    ins = in_ref.shape[0]
    rows = out_ref.shape[0]
    data = in_ref[...]
    drop = onehot(iota((128, ins), 1) == iota((128, ins), 0) * SLOT_ROWS + POS_ROW)
    pos_rows = jnp.dot(drop, data, preferred_element_type=jnp.float32).astype(jnp.bfloat16)
    within = onehot(iota((128, ins), 0) == (iota((128, ins), 1) & (SLOT_ROWS - 1)))
    mine = (iota((128, ins), 1) >> 4) == iota((128, ins), 0)

    def lanes(part):
        spread = jnp.dot(part, within, preferred_element_type=jnp.float32)
        return jnp.sum(jnp.where(mine, spread, 0.0), axis=0, keepdims=True).astype(jnp.int32)

    high = lanes(pos_rows[:, :128])
    low = lanes(pos_rows[:, 128:])
    target = 4 * (high - 1) + 2 * low + (iota((1, ins), 1) & 1)
    pick = onehot(iota((rows, ins), 0) == target)
    out_ref[...] = jnp.dot(pick, data, preferred_element_type=jnp.float32).astype(jnp.bfloat16)


def ring_order(step):
    return jnp.where(step == 0, 0, jnp.where(step == 3, 1, jnp.where(step == 1, 2, 3)))


def plan_kernel(where_ref, count_ref, rows_ref, cols_ref, code_ref, start_ref):
    slots = rows_ref.shape[1]
    count = count_ref[0]
    x, core, z, y = where_ref[0], where_ref[1], where_ref[2], where_ref[3]
    row = rows_ref[...]
    col = cols_ref[...]
    source = col >> 3
    order_z = ring_order(((source >> 2) - z) & 3)
    order_y = ring_order(((source & 3) - y) & 3)
    half = (col >> 2) & 1
    outer = jnp.where(half == 0, order_z, order_y)
    inner = jnp.where(half == 0, order_y, order_z)
    late = jnp.where(outer == 3, 1, 0)
    tile = inner * 4 + (col & 3) + jnp.where(late == 1, half * 16, half * 48 + outer * 16)
    owner = row >> 3
    dx = ((owner >> 1) - x) & 3
    order_x = jnp.where(dx == 2, 0, jnp.where(dx == 1, 1, jnp.where(dx == 3, 2, 3)))
    chunk = jnp.where((owner & 1) == core, 4, 0) + order_x
    key = late * 64 + chunk * 8 + (row & 7)
    slot = iota((1, slots), 1)
    key = jnp.where(slot < count, key, 255)
    code = ((row & 7) << 18) + (slot << 8) + tile + 1

    def column(v):
        return jnp.broadcast_to(v.astype(jnp.float32), (128, slots)).T

    key_row = key.astype(jnp.float32)
    key_col = column(key)[:, :1]
    code_col = column(code)[:, :1]
    same = (key_col == key_row) & (iota((slots, slots), 1) < iota((slots, slots), 0))
    rank = jnp.sum(jnp.where(same, 1.0, 0.0), axis=1, keepdims=True)
    bucket = iota((slots, 256), 1).astype(jnp.float32)
    member = (key_col == bucket) & (bucket < 128)
    cnt = jnp.sum(jnp.where(member, 1.0, 0.0), axis=0, keepdims=True).astype(jnp.int32)
    pairs = jnp.broadcast_to((cnt + 1) >> 1, (16, 256)).astype(jnp.float32).astype(jnp.bfloat16)
    a, b = iota((256, 256), 0), iota((256, 256), 1)
    same_chunk = (a >> 3) == (b >> 3)
    inside = jnp.dot(pairs, onehot(same_chunk & (a < b)), preferred_element_type=jnp.float32)
    total = jnp.dot(pairs, onehot(same_chunk), preferred_element_type=jnp.float32)
    blocks = ((total.astype(jnp.int32) + (PAIRS - 1)) >> 3).astype(jnp.float32)
    blocks = blocks.astype(jnp.bfloat16)
    ahead = jnp.dot(
        blocks, onehot(((a & 7) == 0) & ((a >> 3) < (b >> 3))), preferred_element_type=jnp.float32
    )
    begin = (ahead * BLOCK + inside * 2.0)[:1]
    base = jnp.sum(jnp.where(member, begin, 0.0), axis=1, keepdims=True)
    live = iota((slots, 1), 0) < count
    place = jnp.where(live, base + rank, -1.0)
    lists = code_ref.shape[1]
    hit = place == iota((slots, lists), 1).astype(jnp.float32)
    code_ref[...] = jnp.sum(jnp.where(hit, code_col, 0.0), axis=0, keepdims=True).astype(jnp.int32)
    start_ref[...] = ahead[:1].astype(jnp.int32)


def tiles_kernel(late, n_pieces, chunks, *refs):
    code_ref, start_ref, weights = refs[:3]
    pieces = refs[3 : 3 + n_pieces]
    k = 3 + n_pieces
    if late:
        sum_in = refs[k]
        k += 1
    out = refs[k]
    panel, wbuf, acc, stage, wsem, psem, isem, osem = refs[k + 1 :]
    lo, n_chunks = chunks
    base = 64 if late else 0
    first = start_ref[base + 8 * lo]
    last = start_ref[base + 8 * (lo + n_chunks)]

    offset = 1
    copies = []
    for i, piece in enumerate(pieces):
        n = piece.shape[0]
        copies.append(pltpu.make_async_copy(piece, panel.at[pl.ds(offset, n)], psem.at[i]))
        offset += n
    for c in copies:
        c.start()

    def fetch(block):
        slot = lax.rem(block, BUFS)
        for i in range(BLOCK):
            s = (code_ref[block * BLOCK + i] >> 8) & 1023
            pltpu.make_async_copy(weights.at[s], wbuf.at[slot, i], wsem.at[slot]).start()

    def sum_copy(q):
        return pltpu.make_async_copy(sum_in.at[lo + q], acc.at[lax.rem(q, 2)], isem.at[lax.rem(q, 2)])

    def out_copy(q):
        src = (stage if late else acc).at[lax.rem(q, 2)]
        return pltpu.make_async_copy(src, out.at[q], osem.at[lax.rem(q, 2)])

    if late:
        sum_copy(0).start()
    for i in range(BUFS - 1):
        pl.when(first + i < last)(functools.partial(fetch, first + i))
    panel[0] = jnp.zeros(panel.shape[1:], panel.dtype)
    for c in copies:
        c.wait()

    def run_chunk(q, _):
        par = lax.rem(q, 2)
        if late:
            @pl.when(q + 1 < n_chunks)
            def _():
                sum_copy(q + 1).start()

            sum_copy(q).wait()
        else:
            @pl.when(q >= 2)
            def _():
                out_copy(q - 2).wait()

            acc[par] = jnp.zeros(acc.shape[1:], acc.dtype)

        def run_block(block, _):
            @pl.when(block + (BUFS - 1) < last)
            def _():
                fetch(block + (BUFS - 1))

            slot = lax.rem(block, BUFS)
            pltpu.make_async_copy(weights.at[pl.ds(0, BLOCK)], wbuf.at[slot], wsem.at[slot]).wait()
            for u in range(PAIRS):
                c0 = code_ref[block * BLOCK + 2 * u]
                c1 = code_ref[block * BLOCK + 2 * u + 1]
                w = jnp.concatenate([wbuf[slot, 2 * u], wbuf[slot, 2 * u + 1]], axis=1)
                f = jnp.concatenate([panel[c0 & 255], panel[c1 & 255]], axis=0)
                acc[par, c0 >> 18] += jnp.dot(w, f, preferred_element_type=jnp.float32)
            return 0

        lax.fori_loop(start_ref[base + 8 * (lo + q)], start_ref[base + 8 * (lo + q) + 8], run_block, 0)
        if late:
            @pl.when(q >= 2)
            def _():
                out_copy(q - 2).wait()

            stage[par] = acc[par].astype(jnp.bfloat16)
        out_copy(q).start()
        return 0

    lax.fori_loop(0, n_chunks, run_chunk, 0)
    for q in range(max(0, n_chunks - 2), n_chunks):
        out_copy(q).wait()


def run_tiles(late, chunks, code, start, weights, pieces, sums=None):
    any_spec = pl.BlockSpec(memory_space=pl.ANY)
    smem = pl.BlockSpec(memory_space=pltpu.SMEM)
    n = len(pieces)
    tiles = sum(p.shape[0] for p in pieces) + 1
    t, f = pieces[0].shape[1:]
    dtype = jnp.bfloat16 if late else jnp.float32
    args = [code, start, weights, *pieces] + ([sums] if late else [])
    return pl.pallas_call(
        functools.partial(tiles_kernel, late, n, chunks),
        out_shape=jax.ShapeDtypeStruct((chunks[1], 8, t, f), dtype),
        in_specs=[smem, smem] + [any_spec] * (len(args) - 2),
        out_specs=any_spec,
        scratch_shapes=[
            pltpu.VMEM((tiles, t, f), jnp.bfloat16),
            pltpu.VMEM((BUFS, BLOCK, t, t), jnp.bfloat16),
            pltpu.VMEM((2, 8, t, f), jnp.float32),
            pltpu.VMEM((2, 8, t, f) if late else (2, 8, 128), jnp.bfloat16),
            pltpu.SemaphoreType.DMA((BUFS,)),
            pltpu.SemaphoreType.DMA((n,)),
            pltpu.SemaphoreType.DMA((2,)),
            pltpu.SemaphoreType.DMA((2,)),
        ],
        compiler_params=pltpu.CompilerParams(vmem_limit_bytes=24 * MB),
        name="late_tiles" if late else "early_tiles",
    )(*args)


def col_perm(dz, dy):
    return [(z * 4 + y, (z + dz) % 4 * 4 + (y + dy) % 4) for z in range(4) for y in range(4)]


def row_perm(dx, flip=0):
    return [(x * 2 + c, (x + dx) % 4 * 2 + (c ^ flip)) for x in range(4) for c in range(2)]


def per_device(
    table, home, degree, tile_rows, tile_cols, tile_count, tile_values, w_self, w_neigh, bias
):
    rows, width = table.shape
    devices = lax.axis_size("row") * lax.axis_size("col")
    slots, tile = tile_values.shape[2:4]
    row_index = lax.axis_index("row")
    col_index = lax.axis_index("col")
    where = jnp.stack([row_index // 2, row_index % 2, col_index // 4, col_index % 4]).astype(
        jnp.int32
    )
    vmem = pl.BlockSpec(memory_space=pltpu.VMEM)
    smem = pl.BlockSpec(memory_space=pltpu.SMEM)
    big = pltpu.CompilerParams(vmem_limit_bytes=48 * MB)

    outgoing = pl.pallas_call(
        pack_kernel,
        out_shape=jax.ShapeDtypeStruct((devices * SLOT_ROWS, width), jnp.bfloat16),
        in_specs=[vmem, vmem],
        out_specs=vmem,
        compiler_params=big,
        name="pack",
    )(jnp.repeat(home, 2).reshape(1, rows), table)
    incoming = lax.all_to_all(
        outgoing.reshape(devices, SLOT_ROWS, width),
        ("row", "col"),
        split_axis=0,
        concat_axis=0,
        tiled=True,
    )
    owned = pl.pallas_call(
        unpack_kernel,
        out_shape=jax.ShapeDtypeStruct((rows, width), jnp.bfloat16),
        in_specs=[vmem],
        out_specs=vmem,
        compiler_params=big,
        name="unpack",
    )(incoming.reshape(devices * SLOT_ROWS, width))

    code, start = pl.pallas_call(
        plan_kernel,
        out_shape=(
            jax.ShapeDtypeStruct((1, LIST), jnp.int32),
            jax.ShapeDtypeStruct((1, 256), jnp.int32),
        ),
        in_specs=[smem, smem, vmem, vmem],
        out_specs=(vmem, vmem),
        compiler_params=big,
        name="plan",
    )(where, tile_count.reshape(1), tile_rows.reshape(1, slots), tile_cols.reshape(1, slots))
    code = code.reshape(LIST)
    start = start.reshape(256)
    weights = tile_values.reshape(slots, tile, tile)

    def send(v, dz, dy):
        return lax.ppermute(v, "col", col_perm(dz, dy))

    def far(plus, minus, dz, dy):
        h = plus.shape[0] // 2
        return send(plus[:h], dz, dy), send(minus[h:], -dz, -dy)

    half = rows // 2
    a0, b0 = owned[:half], owned[half:]
    ap, am = send(a0, 0, 1), send(a0, 0, -1)
    bp, bm = send(b0, 1, 0), send(b0, -1, 0)
    a3 = jnp.concatenate([a0, ap, am, *far(ap, am, 0, 1)], axis=0)
    b3 = jnp.concatenate([b0, bp, bm, *far(bp, bm, 1, 0)], axis=0)
    a_p, a_m = send(a3, 1, 0), send(a3, -1, 0)
    b_p, b_m = send(b3, 0, 1), send(b3, 0, -1)
    late_pieces = [*far(a_p, a_m, 1, 0), *far(b_p, b_m, 0, 1)]
    pieces = [v.reshape(-1, tile, width) for v in (a3, a_p, a_m, b3, b_p, b_m)]
    late_pieces = [v.reshape(-1, tile, width) for v in late_pieces]

    sums = run_tiles(False, (0, 8), code, start, weights, pieces)
    other = run_tiles(True, (0, 4), code, start, weights, late_pieces, sums)
    mine = run_tiles(True, (4, 4), code, start, weights, late_pieces, sums)
    other = other.reshape(4, rows, width)
    mine = mine.reshape(4, rows, width)

    f32 = jnp.float32
    got = lax.ppermute(other, "row", row_perm(0, 1))
    both = [(mine[i].astype(f32) + got[i].astype(f32)) for i in range(4)]
    across = both[0].astype(jnp.bfloat16)
    from_minus = lax.ppermute(across[:half], "row", row_perm(1))
    from_plus = lax.ppermute(across[half:], "row", row_perm(-1))
    to_plus = jnp.concatenate(
        [(both[1][:half] + from_minus.astype(f32)), both[1][half:]], axis=0
    ).astype(jnp.bfloat16)
    to_minus = jnp.concatenate(
        [both[2][:half], (both[2][half:] + from_plus.astype(f32))], axis=0
    ).astype(jnp.bfloat16)
    left = lax.ppermute(to_plus, "row", row_perm(1))
    right = lax.ppermute(to_minus, "row", row_perm(-1))
    summed = both[3] + left.astype(f32) + right.astype(f32)

    neighbor_mean = (summed / degree.astype(f32)[:, None]).astype(jnp.bfloat16)
    total = jnp.dot(owned, w_self, preferred_element_type=f32)
    total = total + jnp.dot(neighbor_mean, w_neigh, preferred_element_type=f32)
    total = total + bias.astype(f32)[None, :]
    return jnp.maximum(total, f32(0.0)).astype(jnp.bfloat16)


def solution(mesh):
    in_specs = (
        P(("row", "col"), None),
        P(("row", "col")),
        P(("row", "col")),
        P("row", "col", None),
        P("row", "col", None),
        P("row", "col"),
        P("row", "col", None, None, None),
        P(),
        P(),
        P(),
    )
    out_specs = P(("row", "col"), None)
    return jax.shard_map(
        per_device, mesh=mesh, in_specs=in_specs, out_specs=out_specs, check_vma=False
    )
```

```python
import functools

import jax
import jax.numpy as jnp
from jax import lax
from jax.experimental import pallas as pl
from jax.experimental.pallas import tpu as pltpu
from jax.sharding import PartitionSpec as P

SLOT_ROWS = 16
POS_ROW = 12
PAIRS = 8
BLOCK = 2 * PAIRS
BUFS = 8
SUMS = 3
LIST = 1280
MB = 1 << 20


def iota(shape, dim):
    return lax.broadcasted_iota(jnp.int32, shape, dim)


def onehot(mask):
    return jnp.where(mask, 1.0, 0.0).astype(jnp.bfloat16)


def pack_kernel(home_ref, table_ref, out_ref):
    rows = table_ref.shape[0]
    home = home_ref[...]
    dest = home >> 9
    pos = home & 511
    dest_f = dest.astype(jnp.float32)
    dest_col = jnp.broadcast_to(dest_f, (128, rows)).T[:, :1]
    before = (dest_col == dest_f) & (iota((rows, rows), 0) < iota((rows, rows), 1))
    rank = jnp.sum(jnp.where(before, 1.0, 0.0), axis=0, keepdims=True).astype(jnp.int32)
    place = dest * SLOT_ROWS + rank
    outs = out_ref.shape[0]
    spread = onehot(iota((outs, rows), 0) == place)
    data = jnp.dot(spread, table_ref[...], preferred_element_type=jnp.float32)
    lane = iota((256, rows), 0)
    high = jnp.broadcast_to(((pos >> 1) + 1).astype(jnp.float32), (256, rows))
    low = jnp.broadcast_to((pos & 1).astype(jnp.float32), (256, rows))
    marks = jnp.where(lane == rank, high, jnp.where(lane == rank + 128, low, 0.0)).astype(
        jnp.bfloat16
    )
    owner = onehot(iota((128, rows), 0) == dest)
    pos_rows = lax.dot_general(
        owner, marks, (((1,), (1,)), ((), ())), preferred_element_type=jnp.float32
    ).astype(jnp.bfloat16)
    lift = onehot(iota((outs, 128), 0) == iota((outs, 128), 1) * SLOT_ROWS + POS_ROW)
    data = data + jnp.dot(lift, pos_rows, preferred_element_type=jnp.float32)
    out_ref[...] = data.astype(jnp.bfloat16)


def unpack_kernel(in_ref, out_ref):
    ins = in_ref.shape[0]
    rows = out_ref.shape[0]
    data = in_ref[...]
    drop = onehot(iota((128, ins), 1) == iota((128, ins), 0) * SLOT_ROWS + POS_ROW)
    pos_rows = jnp.dot(drop, data, preferred_element_type=jnp.float32).astype(jnp.bfloat16)
    within = onehot(iota((128, ins), 0) == (iota((128, ins), 1) & (SLOT_ROWS - 1)))
    mine = (iota((128, ins), 1) >> 4) == iota((128, ins), 0)

    def lanes(part):
        spread = jnp.dot(part, within, preferred_element_type=jnp.float32)
        return jnp.sum(jnp.where(mine, spread, 0.0), axis=0, keepdims=True).astype(jnp.int32)

    high = lanes(pos_rows[:, :128])
    low = lanes(pos_rows[:, 128:])
    target = 4 * (high - 1) + 2 * low + (iota((1, ins), 1) & 1)
    pick = onehot(iota((rows, ins), 0) == target)
    out_ref[...] = jnp.dot(pick, data, preferred_element_type=jnp.float32).astype(jnp.bfloat16)


def ring_order(step):
    return jnp.where(step == 0, 0, jnp.where(step == 3, 1, jnp.where(step == 1, 2, 3)))


def plan_kernel(where_ref, count_ref, rows_ref, cols_ref, code_ref, start_ref):
    slots = rows_ref.shape[1]
    count = count_ref[0]
    x, core, z, y = where_ref[0], where_ref[1], where_ref[2], where_ref[3]
    row = rows_ref[...]
    col = cols_ref[...]
    source = col >> 3
    order_z = ring_order(((source >> 2) - z) & 3)
    order_y = ring_order(((source & 3) - y) & 3)
    half = (col >> 2) & 1
    outer = jnp.where(half == 0, order_z, order_y)
    inner = jnp.where(half == 0, order_y, order_z)
    stage = jnp.where(outer == 3, 2, jnp.where((inner < 2) | (outer == 0), 0, 1))
    near = half * 32 + inner * 4 + jnp.where(outer == 0, 0, 8 + outer * 8)
    middle = half * 16 + (outer - 1) * 8 + (inner - 2) * 4
    tile = jnp.where(stage == 0, near, jnp.where(stage == 1, middle, half * 16 + inner * 4))
    tile = tile + (col & 3)
    owner = row >> 3
    dx = ((owner >> 1) - x) & 3
    order_x = jnp.where(dx == 2, 0, jnp.where(dx == 1, 1, jnp.where(dx == 3, 2, 3)))
    chunk = jnp.where((owner & 1) == core, 4, 0) + order_x
    key = stage * 64 + chunk * 8 + (row & 7)
    slot = iota((1, slots), 1)
    key = jnp.where(slot < count, key, 255)
    code = ((row & 7) << 18) + (slot << 8) + tile + 1

    def column(v):
        return jnp.broadcast_to(v.astype(jnp.float32), (128, slots)).T

    key_row = key.astype(jnp.float32)
    key_col = column(key)[:, :1]
    code_col = column(code)[:, :1]
    same = (key_col == key_row) & (iota((slots, slots), 1) < iota((slots, slots), 0))
    rank = jnp.sum(jnp.where(same, 1.0, 0.0), axis=1, keepdims=True)
    bucket = iota((slots, 256), 1).astype(jnp.float32)
    member = (key_col == bucket) & (bucket < 192)
    cnt = jnp.sum(jnp.where(member, 1.0, 0.0), axis=0, keepdims=True).astype(jnp.int32)
    pairs = jnp.broadcast_to((cnt + 1) >> 1, (16, 256)).astype(jnp.float32).astype(jnp.bfloat16)
    a, b = iota((256, 256), 0), iota((256, 256), 1)
    same_chunk = (a >> 3) == (b >> 3)
    inside = jnp.dot(pairs, onehot(same_chunk & (a < b)), preferred_element_type=jnp.float32)
    total = jnp.dot(pairs, onehot(same_chunk), preferred_element_type=jnp.float32)
    blocks = ((total.astype(jnp.int32) + (PAIRS - 1)) >> 3).astype(jnp.float32)
    blocks = blocks.astype(jnp.bfloat16)
    ahead = jnp.dot(
        blocks, onehot(((a & 7) == 0) & ((a >> 3) < (b >> 3))), preferred_element_type=jnp.float32
    )
    begin = (ahead * BLOCK + inside * 2.0)[:1]
    base = jnp.sum(jnp.where(member, begin, 0.0), axis=1, keepdims=True)
    live = iota((slots, 1), 0) < count
    place = jnp.where(live, base + rank, -1.0)
    lists = code_ref.shape[1]
    hit = place == iota((slots, lists), 1).astype(jnp.float32)
    code_ref[...] = jnp.sum(jnp.where(hit, code_col, 0.0), axis=0, keepdims=True).astype(jnp.int32)
    start_ref[...] = ahead[:1].astype(jnp.int32)


def tiles_kernel(stage_index, n_pieces, chunks, *refs):
    resume, late = stage_index > 0, stage_index == 2
    code_ref, start_ref, weights = refs[:3]
    pieces = refs[3 : 3 + n_pieces]
    k = 3 + n_pieces
    if resume:
        sum_in = refs[k]
        k += 1
    out = refs[k]
    panel, wbuf, acc, rounded, wsem, psem, isem, osem = refs[k + 1 :]
    lo, n_chunks = chunks
    base = 64 * stage_index
    first = start_ref[base + 8 * lo]
    last = start_ref[base + 8 * (lo + n_chunks)]
    out_depth = 2 if late else SUMS

    offset = 1
    copies = []
    for i, piece in enumerate(pieces):
        n = piece.shape[0]
        copies.append(pltpu.make_async_copy(piece, panel.at[pl.ds(offset, n)], psem.at[i]))
        offset += n
    for c in copies:
        c.start()

    def fetch(block):
        slot = lax.rem(block, BUFS)
        for i in range(BLOCK):
            s = (code_ref[block * BLOCK + i] >> 8) & 1023
            pltpu.make_async_copy(weights.at[s], wbuf.at[slot, i], wsem.at[slot]).start()

    def sum_copy(q):
        par = lax.rem(q, SUMS)
        return pltpu.make_async_copy(sum_in.at[lo + q], acc.at[par], isem.at[par])

    def out_copy(q):
        par = lax.rem(q, out_depth)
        return pltpu.make_async_copy((rounded if late else acc).at[par], out.at[q], osem.at[par])

    if resume:
        sum_copy(0).start()
    for i in range(BUFS - 1):
        pl.when(first + i < last)(functools.partial(fetch, first + i))
    panel[0] = jnp.zeros(panel.shape[1:], panel.dtype)
    for c in copies:
        c.wait()

    def run_chunk(q, _):
        par = lax.rem(q, SUMS)
        if resume:
            if not late:
                @pl.when((q >= 2) & (q + 1 < n_chunks))
                def _():
                    out_copy(q - 2).wait()

            @pl.when(q + 1 < n_chunks)
            def _():
                sum_copy(q + 1).start()

            sum_copy(q).wait()
        else:
            @pl.when(q >= SUMS)
            def _():
                out_copy(q - SUMS).wait()

            acc[par] = jnp.zeros(acc.shape[1:], acc.dtype)

        def run_block(block, _):
            @pl.when(block + (BUFS - 1) < last)
            def _():
                fetch(block + (BUFS - 1))

            slot = lax.rem(block, BUFS)
            pltpu.make_async_copy(weights.at[pl.ds(0, BLOCK)], wbuf.at[slot], wsem.at[slot]).wait()
            for u in range(PAIRS):
                c0 = code_ref[block * BLOCK + 2 * u]
                c1 = code_ref[block * BLOCK + 2 * u + 1]
                w = jnp.concatenate([wbuf[slot, 2 * u], wbuf[slot, 2 * u + 1]], axis=1)
                f = jnp.concatenate([panel[c0 & 255], panel[c1 & 255]], axis=0)
                acc[par, c0 >> 18] += jnp.dot(w, f, preferred_element_type=jnp.float32)
            return 0

        lax.fori_loop(start_ref[base + 8 * (lo + q)], start_ref[base + 8 * (lo + q) + 8], run_block, 0)
        if late:
            @pl.when(q >= out_depth)
            def _():
                out_copy(q - out_depth).wait()

            rounded[lax.rem(q, out_depth)] = acc[par].astype(jnp.bfloat16)
        out_copy(q).start()
        return 0

    lax.fori_loop(0, n_chunks, run_chunk, 0)
    for q in range(n_chunks - out_depth, n_chunks):
        out_copy(q).wait()


def run_tiles(stage_index, chunks, code, start, weights, pieces, sums=None):
    any_spec = pl.BlockSpec(memory_space=pl.ANY)
    smem = pl.BlockSpec(memory_space=pltpu.SMEM)
    pieces = [p.reshape(-1, weights.shape[1], p.shape[-1]) for p in pieces]
    n = len(pieces)
    tiles = sum(p.shape[0] for p in pieces) + 1
    t, f = pieces[0].shape[1:]
    late = stage_index == 2
    args = [code, start, weights, *pieces] + ([sums] if stage_index else [])
    share = 352 * (tiles - 1) // 128 * chunks[1] // 8
    return pl.pallas_call(
        functools.partial(tiles_kernel, stage_index, n, chunks),
        out_shape=jax.ShapeDtypeStruct((chunks[1], 8, t, f), jnp.bfloat16 if late else jnp.float32),
        in_specs=[smem, smem] + [any_spec] * (len(args) - 2),
        out_specs=any_spec,
        scratch_shapes=[
            pltpu.VMEM((tiles, t, f), jnp.bfloat16),
            pltpu.VMEM((BUFS, BLOCK, t, t), jnp.bfloat16),
            pltpu.VMEM((SUMS, 8, t, f), jnp.float32),
            pltpu.VMEM((2, 8, t, f) if late else (2, 8, 128), jnp.bfloat16),
            pltpu.SemaphoreType.DMA((BUFS,)),
            pltpu.SemaphoreType.DMA((n,)),
            pltpu.SemaphoreType.DMA((SUMS,)),
            pltpu.SemaphoreType.DMA((SUMS,)),
        ],
        compiler_params=pltpu.CompilerParams(vmem_limit_bytes=31 * MB),
        cost_estimate=pl.CostEstimate(
            flops=share * 2 * t * t * f * 2, bytes_accessed=share * 2 * t * t * 2, transcendentals=0
        ),
        name=f"tiles_{stage_index}",
    )(*args)


def col_perm(dz, dy):
    return [(z * 4 + y, (z + dz) % 4 * 4 + (y + dy) % 4) for z in range(4) for y in range(4)]


def row_perm(dx, flip=0):
    return [(x * 2 + c, (x + dx) % 4 * 2 + (c ^ flip)) for x in range(4) for c in range(2)]


def per_device(
    table, home, degree, tile_rows, tile_cols, tile_count, tile_values, w_self, w_neigh, bias
):
    rows, width = table.shape
    devices = lax.axis_size("row") * lax.axis_size("col")
    slots, tile = tile_values.shape[2:4]
    row_index = lax.axis_index("row")
    col_index = lax.axis_index("col")
    where = jnp.stack([row_index // 2, row_index % 2, col_index // 4, col_index % 4]).astype(
        jnp.int32
    )
    vmem = pl.BlockSpec(memory_space=pltpu.VMEM)
    smem = pl.BlockSpec(memory_space=pltpu.SMEM)
    big = pltpu.CompilerParams(vmem_limit_bytes=48 * MB)

    outgoing = pl.pallas_call(
        pack_kernel,
        out_shape=jax.ShapeDtypeStruct((devices * SLOT_ROWS, width), jnp.bfloat16),
        in_specs=[vmem, vmem],
        out_specs=vmem,
        compiler_params=big,
        name="pack",
    )(jnp.repeat(home, 2).reshape(1, rows), table)
    incoming = lax.all_to_all(
        outgoing.reshape(devices, SLOT_ROWS, width),
        ("row", "col"),
        split_axis=0,
        concat_axis=0,
        tiled=True,
    )
    owned = pl.pallas_call(
        unpack_kernel,
        out_shape=jax.ShapeDtypeStruct((rows, width), jnp.bfloat16),
        in_specs=[vmem],
        out_specs=vmem,
        compiler_params=big,
        name="unpack",
    )(incoming.reshape(devices * SLOT_ROWS, width))

    code, start = pl.pallas_call(
        plan_kernel,
        out_shape=(
            jax.ShapeDtypeStruct((1, LIST), jnp.int32),
            jax.ShapeDtypeStruct((1, 256), jnp.int32),
        ),
        in_specs=[smem, smem, vmem, vmem],
        out_specs=(vmem, vmem),
        compiler_params=big,
        name="plan",
    )(where, tile_count.reshape(1), tile_rows.reshape(1, slots), tile_cols.reshape(1, slots))
    code = code.reshape(LIST)
    start = start.reshape(256)
    weights = tile_values.reshape(slots, tile, tile)

    def send(v, dz, dy):
        return lax.ppermute(v, "col", col_perm(dz, dy))

    half = rows // 2
    quarter = half // 2

    def cat(*parts):
        return jnp.concatenate(parts, axis=0)

    a0, b0 = owned[:half], owned[half:]
    ap, am = send(a0, 0, 1), send(a0, 0, -1)
    bp, bm = send(b0, 1, 0), send(b0, -1, 0)
    a_lo, b_lo = cat(a0, ap), cat(b0, bp)
    a_lo_p, a_lo_m = send(a_lo, 1, 0), send(a_lo, -1, 0)
    b_lo_p, b_lo_m = send(b_lo, 0, 1), send(b_lo, 0, -1)
    am, bm, code, start = lax.optimization_barrier((am, bm, code, start))
    a_hi = cat(am, send(ap[:quarter], 0, 1), send(am[quarter:], 0, -1))
    b_hi = cat(bm, send(bp[:quarter], 1, 0), send(bm[quarter:], -1, 0))
    a_hi_p, a_hi_m = send(a_hi, 1, 0), send(a_hi, -1, 0)
    b_hi_p, b_hi_m = send(b_hi, 0, 1), send(b_hi, 0, -1)
    a_far, b_far = [send(a_lo_p, 1, 0)], [send(b_lo_p, 0, 1)]
    near = [a_lo, a_hi, a_lo_p, a_lo_m, b_lo, b_hi, b_lo_p, b_lo_m]
    sums = run_tiles(0, (0, 8), code, start, weights, near)
    a_hi_m, b_hi_m, sums = lax.optimization_barrier((a_hi_m, b_hi_m, sums))
    a_far.append(send(a_hi_m, -1, 0))
    b_far.append(send(b_hi_m, 0, -1))
    sums = run_tiles(1, (0, 8), code, start, weights, [a_hi_p, a_hi_m, b_hi_p, b_hi_m], sums)
    other = run_tiles(2, (0, 4), code, start, weights, a_far + b_far, sums)
    mine = run_tiles(2, (4, 4), code, start, weights, a_far + b_far, sums)
    other = other.reshape(4, rows, width)
    mine = mine.reshape(4, rows, width)

    f32 = jnp.float32
    got = lax.ppermute(other, "row", row_perm(0, 1))
    both = [(mine[i].astype(f32) + got[i].astype(f32)) for i in range(4)]
    across = both[0].astype(jnp.bfloat16)
    from_minus = lax.ppermute(across[:half], "row", row_perm(1))
    from_plus = lax.ppermute(across[half:], "row", row_perm(-1))
    to_plus = jnp.concatenate(
        [(both[1][:half] + from_minus.astype(f32)), both[1][half:]], axis=0
    ).astype(jnp.bfloat16)
    to_minus = jnp.concatenate(
        [both[2][:half], (both[2][half:] + from_plus.astype(f32))], axis=0
    ).astype(jnp.bfloat16)
    left = lax.ppermute(to_plus, "row", row_perm(1))
    right = lax.ppermute(to_minus, "row", row_perm(-1))
    summed = both[3] + left.astype(f32) + right.astype(f32)

    neighbor_mean = (summed / degree.astype(f32)[:, None]).astype(jnp.bfloat16)
    total = jnp.dot(owned, w_self, preferred_element_type=f32)
    total = total + jnp.dot(neighbor_mean, w_neigh, preferred_element_type=f32)
    total = total + bias.astype(f32)[None, :]
    return jnp.maximum(total, f32(0.0)).astype(jnp.bfloat16)


def solution(mesh):
    in_specs = (
        P(("row", "col"), None),
        P(("row", "col")),
        P(("row", "col")),
        P("row", "col", None),
        P("row", "col", None),
        P("row", "col"),
        P("row", "col", None, None, None),
        P(),
        P(),
        P(),
    )
    out_specs = P(("row", "col"), None)
    return jax.shard_map(
        per_device, mesh=mesh, in_specs=in_specs, out_specs=out_specs, check_vma=False
    )
```

```python
import functools

import jax
import jax.numpy as jnp
from jax import lax
from jax.experimental import pallas as pl
from jax.experimental.pallas import tpu as pltpu
from jax.sharding import PartitionSpec as P

SLOT_ROWS = 16
POS_ROW = 12
PAIRS = 8
BLOCK = 2 * PAIRS
BUFS = 8
LIST = 1152
LANES = 384
MB = 1 << 20
VMEM_TILES = 30 * MB


def iota(shape, dim):
    return lax.broadcasted_iota(jnp.int32, shape, dim)


def onehot(mask):
    return jnp.where(mask, 1.0, 0.0).astype(jnp.bfloat16)


def pack_kernel(home_ref, table_ref, out_ref):
    rows = table_ref.shape[0]
    blocks = home_ref.shape[1]
    parts = jnp.where(iota((16, blocks), 0) == 0, home_ref[...] >> 8, home_ref[...] & 255)
    twice = onehot(iota((blocks, rows), 0) == (iota((blocks, rows), 1) >> 1))
    parts = jnp.dot(
        parts.astype(jnp.float32).astype(jnp.bfloat16), twice, preferred_element_type=jnp.float32
    ).astype(jnp.int32)
    home = (parts[:1] << 8) + parts[1:2]
    dest = home >> 9
    pos = home & 511
    dest_f = dest.astype(jnp.float32)
    dest_col = jnp.broadcast_to(dest_f, (128, rows)).T[:, :1]
    before = (dest_col == dest_f) & (iota((rows, rows), 0) < iota((rows, rows), 1))
    rank = jnp.sum(jnp.where(before, 1.0, 0.0), axis=0, keepdims=True).astype(jnp.int32)
    place = dest * SLOT_ROWS + rank
    outs = out_ref.shape[0]
    spread = onehot(iota((outs, rows), 0) == place)
    data = jnp.dot(spread, table_ref[...], preferred_element_type=jnp.float32)
    lane = iota((256, rows), 0)
    high = jnp.broadcast_to(((pos >> 1) + 1).astype(jnp.float32), (256, rows))
    low = jnp.broadcast_to((pos & 1).astype(jnp.float32), (256, rows))
    marks = jnp.where(lane == rank, high, jnp.where(lane == rank + 128, low, 0.0)).astype(
        jnp.bfloat16
    )
    owner = onehot(iota((128, rows), 0) == dest)
    pos_rows = lax.dot_general(
        owner, marks, (((1,), (1,)), ((), ())), preferred_element_type=jnp.float32
    ).astype(jnp.bfloat16)
    lift = onehot(iota((outs, 128), 0) == iota((outs, 128), 1) * SLOT_ROWS + POS_ROW)
    data = data + jnp.dot(lift, pos_rows, preferred_element_type=jnp.float32)
    out_ref[...] = data.astype(jnp.bfloat16)


def unpack_kernel(in_ref, a_ref, b_ref):
    ins = in_ref.shape[0]
    rows = a_ref.shape[0] + b_ref.shape[0]
    data = in_ref[...]
    drop = onehot(iota((128, ins), 1) == iota((128, ins), 0) * SLOT_ROWS + POS_ROW)
    pos_rows = jnp.dot(drop, data, preferred_element_type=jnp.float32).astype(jnp.bfloat16)
    within = onehot(iota((128, ins), 0) == (iota((128, ins), 1) & (SLOT_ROWS - 1)))
    mine = (iota((128, ins), 1) >> 4) == iota((128, ins), 0)

    def lanes(part):
        spread = jnp.dot(part, within, preferred_element_type=jnp.float32)
        return jnp.sum(jnp.where(mine, spread, 0.0), axis=0, keepdims=True).astype(jnp.int32)

    high = lanes(pos_rows[:, :128])
    low = lanes(pos_rows[:, 128:])
    target = 4 * (high - 1) + 2 * low + (iota((1, ins), 1) & 1)
    pick = onehot(iota((rows, ins), 0) == target)
    owned = jnp.dot(pick, data, preferred_element_type=jnp.float32).astype(jnp.bfloat16)
    a_ref[...] = owned[: rows // 2]
    b_ref[...] = owned[rows // 2 :]


def ring_order(step):
    return jnp.where(step == 0, 0, jnp.where(step == 3, 1, jnp.where(step == 1, 2, 3)))


def plan_kernel(where_ref, count_ref, rows_ref, cols_ref, code_ref, start_ref):
    slots = rows_ref.shape[1]
    count = count_ref[0]
    x, core, z, y = where_ref[0], where_ref[1], where_ref[2], where_ref[3]
    row = rows_ref[...]
    col = cols_ref[...]
    source = col >> 3
    order_z = ring_order(((source >> 2) - z) & 3)
    order_y = ring_order(((source & 3) - y) & 3)
    half = (col >> 2) & 1
    outer = jnp.where(half == 0, order_z, order_y)
    inner = jnp.where(half == 0, order_y, order_z)
    stage = jnp.where((outer == 1) == (inner < 2), 1, 2)
    stage = jnp.where(outer == 3, 3, jnp.where(outer == 0, 0, stage))
    tile = half * 16 + inner * 4 + (col & 3)
    owner = row >> 3
    dx = ((owner >> 1) - x) & 3
    order_x = jnp.where(dx == 2, 0, jnp.where(dx == 1, 1, jnp.where(dx == 3, 2, 3)))
    own = (owner & 1) == core
    chunk = jnp.where(order_x == 0, jnp.where(own, 1, 0), jnp.where(own, 4, 1) + order_x)
    key = stage * 64 + chunk * 8 + (row & 7)
    slot = iota((1, slots), 1)
    key = jnp.where(slot < count, key, 511)
    code = ((chunk * 8 + (row & 7)) << 18) + (slot << 8) + tile + 1

    def column(v):
        return jnp.broadcast_to(v.astype(jnp.float32), (128, slots)).T

    key_row = key.astype(jnp.float32)
    key_col = column(key)[:, :1]
    code_col = column(code)[:, :1]
    same = (key_col == key_row) & (iota((slots, slots), 1) < iota((slots, slots), 0))
    rank = jnp.sum(jnp.where(same, 1.0, 0.0), axis=1, keepdims=True)
    bucket = iota((slots, LANES), 1).astype(jnp.float32)
    member = key_col == bucket
    cnt = jnp.sum(jnp.where(member, 1.0, 0.0), axis=0, keepdims=True).astype(jnp.int32)
    pairs = jnp.broadcast_to((cnt + 1) >> 1, (16, LANES)).astype(jnp.float32).astype(jnp.bfloat16)
    a, b = iota((LANES, LANES), 0), iota((LANES, LANES), 1)

    def region(k):
        late = jnp.where(k < 232, 4, jnp.where(k < 256, 5, 6))
        return jnp.where(k < 192, k >> 6, jnp.where(k < 208, 3, late))

    same_region = region(a) == region(b)
    opens = (a == 0) | (a == 64) | (a == 128) | (a == 192) | (a == 208) | (a == 232)
    inside = jnp.dot(pairs, onehot(same_region & (a < b)), preferred_element_type=jnp.float32)
    total = jnp.dot(pairs, onehot(same_region), preferred_element_type=jnp.float32)
    blocks = ((total.astype(jnp.int32) + (PAIRS - 1)) >> 3).astype(jnp.float32)
    blocks = blocks.astype(jnp.bfloat16)
    ahead = jnp.dot(
        blocks, onehot(opens & (region(a) < region(b))), preferred_element_type=jnp.float32
    )
    begin = (ahead * BLOCK + inside * 2.0)[:1]
    base = jnp.sum(jnp.where(member, begin, 0.0), axis=1, keepdims=True)
    live = iota((slots, 1), 0) < count
    place = jnp.where(live, base + rank, -1.0)
    lists = code_ref.shape[1]
    hit = place == iota((slots, lists), 1).astype(jnp.float32)
    code_ref[...] = jnp.sum(jnp.where(hit, code_col, 0.0), axis=0, keepdims=True).astype(jnp.int32)
    start_ref[...] = ahead[:1].astype(jnp.int32)


def tiles_kernel(buckets, opening, n_pieces, make_panel, outs, *refs):
    code_ref, start_ref, weights = refs[:3]
    k = 3
    pieces = refs[k : k + n_pieces]
    k += n_pieces
    if not n_pieces:
        panel = refs[k]
        k += 1
    if not opening:
        k += 2
    acc, wbuf = refs[k : k + 2]
    k += 2
    if make_panel:
        panel = refs[k]
        k += 1
    out_refs = refs[k : k + len(outs)]
    k += len(outs)
    if n_pieces and not make_panel:
        panel = refs[k]
        k += 1
    wsem = refs[k]
    first = start_ref[buckets[0]]
    last = start_ref[buckets[1]]
    total = start_ref[256]
    ahead = BUFS - 1

    copies = []
    if n_pieces:
        psem = refs[k + 1]
        offset = 1
        for i, piece in enumerate(pieces):
            n = piece.shape[0]
            copies.append(pltpu.make_async_copy(piece, panel.at[pl.ds(offset, n)], psem.at[i]))
            offset += n
        for c in copies:
            c.start()
        panel[0] = jnp.zeros(panel.shape[1:], panel.dtype)

    def fetch(block):
        slot = lax.rem(block, BUFS)
        for i in range(BLOCK):
            s = (code_ref[block * BLOCK + i] >> 8) & 1023
            pltpu.make_async_copy(weights.at[s], wbuf.at[slot, i], wsem.at[slot]).start()

    def arrive(block):
        slot = lax.rem(block, BUFS)
        pltpu.make_async_copy(weights.at[pl.ds(0, BLOCK)], wbuf.at[slot], wsem.at[slot]).wait()

    if opening:
        for i in range(ahead):
            pl.when(first + i < total)(functools.partial(fetch, first + i))

        def clear(i, _):
            acc[i] = jnp.zeros(acc.shape[1:], acc.dtype)
            return 0

        lax.fori_loop(0, acc.shape[0], clear, 0)
    fetched = first if opening else first + ahead
    for c in copies:
        c.wait()

    def run_block(block, _):
        pl.when(block + ahead < total)(functools.partial(fetch, block + ahead))
        pl.when(block >= fetched)(functools.partial(arrive, block))
        slot = lax.rem(block, BUFS)
        for u in range(PAIRS):
            c0 = code_ref[block * BLOCK + 2 * u]
            c1 = code_ref[block * BLOCK + 2 * u + 1]
            w = jnp.concatenate([wbuf[slot, 2 * u], wbuf[slot, 2 * u + 1]], axis=1)
            f = jnp.concatenate([panel[c0 & 255], panel[c1 & 255]], axis=0)
            acc[c0 >> 18] += jnp.dot(w, f, preferred_element_type=jnp.float32)
        return 0

    lax.fori_loop(first, last, run_block, 0)
    for out, (lo, n) in zip(out_refs, outs):

        def give(i, _, out=out, lo=lo):
            out[i] = acc[lo + i].astype(out.dtype)
            return 0

        lax.fori_loop(0, n, give, 0)
    for i in range(ahead):
        pl.when((last + i < total) & (last + i >= fetched))(functools.partial(arrive, last + i))


def run_tiles(buckets, code, start, weights, pieces=(), panel=None, state=None, make_panel=False, outs=()):
    any_spec = pl.BlockSpec(memory_space=pl.ANY)
    vmem = pl.BlockSpec(memory_space=pltpu.VMEM)
    smem = pl.BlockSpec(memory_space=pltpu.SMEM)
    t = weights.shape[1]
    pieces = [p.reshape(-1, t, p.shape[-1]) for p in pieces]
    n = len(pieces)
    tiles = sum(p.shape[0] for p in pieces) + 1
    f = (pieces[0] if n else panel).shape[2]
    args = [code, start, weights, *pieces]
    in_specs = [smem, smem, any_spec] + [any_spec] * n
    if panel is not None:
        args.append(panel)
        in_specs.append(vmem)
    aliases = {}
    if state is not None:
        aliases = {len(args): 0, len(args) + 1: 1}
        args += list(state)
        in_specs += [vmem, vmem]
    out_shape = [
        pltpu.VMEM((64, t, f), jnp.float32),
        pltpu.VMEM((BUFS, BLOCK, t, t), jnp.bfloat16),
    ]
    if make_panel:
        out_shape.append(pltpu.VMEM((tiles, t, f), jnp.bfloat16))
    out_shape += [pltpu.VMEM((k, t, f), jnp.bfloat16) for _, k in outs]
    scratch = [pltpu.VMEM((tiles, t, f), jnp.bfloat16)] if n and not make_panel else []
    scratch.append(pltpu.SemaphoreType.DMA((BUFS,)))
    if n:
        scratch.append(pltpu.SemaphoreType.DMA((n,)))
    share = 352 * (buckets[1] - buckets[0]) // 256
    return pl.pallas_call(
        functools.partial(tiles_kernel, buckets, state is None, n, make_panel, outs),
        out_shape=out_shape,
        in_specs=in_specs,
        out_specs=[vmem] * len(out_shape),
        scratch_shapes=scratch,
        input_output_aliases=aliases,
        compiler_params=pltpu.CompilerParams(vmem_limit_bytes=VMEM_TILES),
        cost_estimate=pl.CostEstimate(
            flops=share * 4 * t * t * f, bytes_accessed=share * 4 * t * t, transcendentals=0
        ),
        name=f"tiles_{buckets[0]}",
    )(*args)


def col_perm(dz, dy):
    return [(z * 4 + y, (z + dz) % 4 * 4 + (y + dy) % 4) for z in range(4) for y in range(4)]


def row_perm(dx, flip=0):
    return [(x * 2 + c, (x + dx) % 4 * 2 + (c ^ flip)) for x in range(4) for c in range(2)]


def per_device(
    table, home, degree, tile_rows, tile_cols, tile_count, tile_values, w_self, w_neigh, bias
):
    rows, width = table.shape
    devices = lax.axis_size("row") * lax.axis_size("col")
    slots, tile = tile_values.shape[2:4]
    row_index = lax.axis_index("row")
    col_index = lax.axis_index("col")
    where = jnp.stack([row_index // 2, row_index % 2, col_index // 4, col_index % 4]).astype(
        jnp.int32
    )
    vmem = pl.BlockSpec(memory_space=pltpu.VMEM)
    smem = pl.BlockSpec(memory_space=pltpu.SMEM)
    big = pltpu.CompilerParams(vmem_limit_bytes=48 * MB)

    outgoing = pl.pallas_call(
        pack_kernel,
        out_shape=jax.ShapeDtypeStruct((devices * SLOT_ROWS, width), jnp.bfloat16),
        in_specs=[vmem, vmem],
        out_specs=vmem,
        compiler_params=big,
        name="pack",
    )(home.reshape(1, -1), table)
    incoming = lax.all_to_all(
        outgoing.reshape(devices, SLOT_ROWS, width),
        ("row", "col"),
        split_axis=0,
        concat_axis=0,
        tiled=True,
    )
    half = rows // 2
    quarter = half // 2
    a0, b0 = pl.pallas_call(
        unpack_kernel,
        out_shape=(jax.ShapeDtypeStruct((half, width), jnp.bfloat16),) * 2,
        in_specs=[vmem],
        out_specs=(vmem, vmem),
        compiler_params=big,
        name="unpack",
    )(incoming.reshape(devices * SLOT_ROWS, width))

    code, start = pl.pallas_call(
        plan_kernel,
        out_shape=(
            jax.ShapeDtypeStruct((1, LIST), jnp.int32),
            jax.ShapeDtypeStruct((1, LANES), jnp.int32),
        ),
        in_specs=[smem, smem, vmem, vmem],
        out_specs=(vmem, vmem),
        compiler_params=big,
        name="plan",
    )(where, tile_count.reshape(1), tile_rows.reshape(1, slots), tile_cols.reshape(1, slots))
    code = code.reshape(LIST)
    start = start.reshape(LANES)
    weights = tile_values.reshape(slots, tile, tile)

    def send(v, dz, dy):
        return lax.ppermute(v, "col", col_perm(dz, dy))

    def cat(*parts):
        return jnp.concatenate(parts, axis=0)

    ap, am = send(a0, 0, 1), send(a0, 0, -1)
    bp, bm = send(b0, 1, 0), send(b0, -1, 0)
    a_hi = cat(am, send(ap[:quarter], 0, 1), send(am[quarter:], 0, -1))
    b_hi = cat(bm, send(bp[:quarter], 1, 0), send(bm[quarter:], -1, 0))
    a_hi, b_hi, ap, bp, code, start = lax.optimization_barrier((a_hi, b_hi, ap, bp, code, start))
    a_lo, b_lo = cat(a0, ap), cat(b0, bp)
    lists = (code, start, weights)
    a_lo_p, a_hi_m = send(a_lo, 1, 0), send(a_hi, -1, 0)
    b_lo_p, b_hi_m = send(b_lo, 0, 1), send(b_hi, 0, -1)
    state = run_tiles((0, 64), *lists, [a_lo, a_hi, b_lo, b_hi])
    a_lo, a_hi, b_lo, b_hi, *state = lax.optimization_barrier((a_lo, a_hi, b_lo, b_hi, *state))
    a_hi_p, a_lo_m = send(a_hi, 1, 0), send(a_lo, -1, 0)
    b_hi_p, b_lo_m = send(b_hi, 0, 1), send(b_lo, 0, -1)
    state = run_tiles((64, 128), *lists, [a_lo_p, a_hi_m, b_lo_p, b_hi_m], state=state)
    a_lo_p, a_hi_m, b_lo_p, b_hi_m, *state = lax.optimization_barrier(
        (a_lo_p, a_hi_m, b_lo_p, b_hi_m, *state)
    )
    far = [send(a_lo_p, 1, 0), send(a_hi_m, -1, 0), send(b_lo_p, 0, 1), send(b_hi_m, 0, -1)]
    state = run_tiles((128, 192), *lists, [a_lo_m, a_hi_p, b_lo_m, b_hi_p], state=state)
    f32 = jnp.float32

    def over(v, dx, flip=0):
        return lax.ppermute(v, "row", row_perm(dx, flip))

    *state, panel, other_far, mine_far = run_tiles(
        (192, 208), *lists, far, state=state, make_panel=True, outs=((0, 8), (8, 8))
    )
    got_far = over(other_far.reshape(rows, width), 0, 1)
    *state, other_rest = run_tiles((208, 232), *lists, panel=panel, state=state, outs=((16, 24),))
    across = (mine_far.reshape(rows, width).astype(f32) + got_far.astype(f32)).astype(jnp.bfloat16)
    across, *state = lax.optimization_barrier((across, *state))
    from_minus, from_plus = over(across[:half], 1), over(across[half:], -1)
    got_rest = over(other_rest.reshape(3, rows, width), 0, 1)
    *state, mine_rest = run_tiles((232, 256), *lists, panel=panel, state=state, outs=((40, 24),))
    mine_rest = mine_rest.reshape(3, rows, width)
    both = [mine_rest[i].astype(f32) + got_rest[i].astype(f32) for i in range(3)]
    to_plus = cat(both[0][:half] + from_minus.astype(f32), both[0][half:]).astype(jnp.bfloat16)
    to_minus = cat(both[1][:half], both[1][half:] + from_plus.astype(f32)).astype(jnp.bfloat16)
    summed = both[2] + over(to_plus, 1).astype(f32) + over(to_minus, -1).astype(f32)

    neighbor_mean = (summed / degree.astype(f32)[:, None]).astype(jnp.bfloat16)
    total = jnp.dot(cat(a0, b0), w_self, preferred_element_type=f32)
    total = total + jnp.dot(neighbor_mean, w_neigh, preferred_element_type=f32)
    total = total + bias.astype(f32)[None, :]
    return jnp.maximum(total, f32(0.0)).astype(jnp.bfloat16)


def solution(mesh):
    in_specs = (
        P(("row", "col"), None),
        P(("row", "col")),
        P(("row", "col")),
        P("row", "col", None),
        P("row", "col", None),
        P("row", "col"),
        P("row", "col", None, None, None),
        P(),
        P(),
        P(),
    )
    out_specs = P(("row", "col"), None)
    return jax.shard_map(
        per_device, mesh=mesh, in_specs=in_specs, out_specs=out_specs, check_vma=False
    )
```

```python
import functools

import jax
import jax.numpy as jnp
from jax import lax
from jax.experimental import pallas as pl
from jax.experimental.pallas import tpu as pltpu
from jax.sharding import PartitionSpec as P

SLOT_ROWS = 16
POS_ROW = 12
PAIRS = 8
BLOCK = 2 * PAIRS
BUFS = 8
LIST = 1024
LANES = 384
MB = 1 << 20
VMEM_TILES = 30 * MB


def iota(shape, dim):
    return lax.broadcasted_iota(jnp.int32, shape, dim)


def onehot(mask):
    return jnp.where(mask, 1.0, 0.0).astype(jnp.bfloat16)


def pack_kernel(home_ref, table_ref, out_ref):
    rows = table_ref.shape[0]
    blocks = home_ref.shape[1]
    parts = jnp.where(iota((16, blocks), 0) == 0, home_ref[...] >> 8, home_ref[...] & 255)
    twice = onehot(iota((blocks, rows), 0) == (iota((blocks, rows), 1) >> 1))
    parts = jnp.dot(
        parts.astype(jnp.float32).astype(jnp.bfloat16), twice, preferred_element_type=jnp.float32
    ).astype(jnp.int32)
    home = (parts[:1] << 8) + parts[1:2]
    dest = home >> 9
    pos = home & 511
    dest_f = dest.astype(jnp.float32)
    dest_col = jnp.broadcast_to(dest_f, (128, rows)).T[:, :1]
    before = (dest_col == dest_f) & (iota((rows, rows), 0) < iota((rows, rows), 1))
    rank = jnp.sum(jnp.where(before, 1.0, 0.0), axis=0, keepdims=True).astype(jnp.int32)
    place = dest * SLOT_ROWS + rank
    outs = out_ref.shape[0]
    spread = onehot(iota((outs, rows), 0) == place)
    data = jnp.dot(spread, table_ref[...], preferred_element_type=jnp.float32)
    lane = iota((256, rows), 0)
    high = jnp.broadcast_to(((pos >> 1) + 1).astype(jnp.float32), (256, rows))
    low = jnp.broadcast_to((pos & 1).astype(jnp.float32), (256, rows))
    marks = jnp.where(lane == rank, high, jnp.where(lane == rank + 128, low, 0.0)).astype(
        jnp.bfloat16
    )
    owner = onehot(iota((128, rows), 0) == dest)
    pos_rows = lax.dot_general(
        owner, marks, (((1,), (1,)), ((), ())), preferred_element_type=jnp.float32
    ).astype(jnp.bfloat16)
    lift = onehot(iota((outs, 128), 0) == iota((outs, 128), 1) * SLOT_ROWS + POS_ROW)
    data = data + jnp.dot(lift, pos_rows, preferred_element_type=jnp.float32)
    out_ref[...] = data.astype(jnp.bfloat16)


def unpack_kernel(in_ref, out_ref):
    ins = in_ref.shape[0]
    rows = out_ref.shape[0]
    data = in_ref[...]
    drop = onehot(iota((128, ins), 1) == iota((128, ins), 0) * SLOT_ROWS + POS_ROW)
    pos_rows = jnp.dot(drop, data, preferred_element_type=jnp.float32).astype(jnp.bfloat16)
    within = onehot(iota((128, ins), 0) == (iota((128, ins), 1) & (SLOT_ROWS - 1)))
    mine = (iota((128, ins), 1) >> 4) == iota((128, ins), 0)

    def lanes(part):
        spread = jnp.dot(part, within, preferred_element_type=jnp.float32)
        return jnp.sum(jnp.where(mine, spread, 0.0), axis=0, keepdims=True).astype(jnp.int32)

    high = lanes(pos_rows[:, :128])
    low = lanes(pos_rows[:, 128:])
    target = 4 * (high - 1) + 2 * low + (iota((1, ins), 1) & 1)
    pick = onehot(iota((rows, ins), 0) == target)
    out_ref[...] = jnp.dot(pick, data, preferred_element_type=jnp.float32).astype(jnp.bfloat16)


def plan_kernel(where_ref, count_ref, rows_ref, cols_ref, code_ref, start_ref):
    slots = rows_ref.shape[1]
    count = count_ref[0]
    x, core, z, y = where_ref[0], where_ref[1], where_ref[2], where_ref[3]
    row = rows_ref[...]
    col = cols_ref[...]
    source = col >> 3
    dz = ((source >> 2) - z) & 3
    dy = ((source & 3) - y) & 3
    steps = jnp.where(dz == 3, 1, dz) + jnp.where(dy == 3, 1, dy)
    stage = jnp.maximum(steps - 1, 0)
    part, rest = (col & 7) >> 2, col & 3
    side_z, side_y = jnp.where(dz == 3, 0, 4), jnp.where(dy == 3, 0, 4)
    tile_0 = jnp.where(dz == 0, jnp.where(dy == 0, 0, side_y * 2 + 8), side_z * 2 + 24) + (col & 7)
    corner = jnp.where(part == 0, side_y * 3 + side_z, side_z * 3 + side_y + 24)
    tile_1 = jnp.where(dz == 0, part * 12 + 8, jnp.where(dy == 0, part * 12 + 32, corner)) + rest
    on_y = jnp.where(part == 0, 4 - side_z, side_z + 8)
    on_z = jnp.where(part == 1, 20 - side_y, side_y + 24)
    tile_2 = jnp.where(dy == 2, on_y, on_z) + rest
    tile = jnp.where(stage == 0, tile_0, jnp.where(stage == 1, tile_1, jnp.where(stage == 2, tile_2, col & 7)))
    owner = row >> 3
    dx = ((owner >> 1) - x) & 3
    order_x = jnp.where(dx == 2, 0, jnp.where(dx == 1, 1, jnp.where(dx == 3, 2, 3)))
    own = (owner & 1) == core
    chunk = jnp.where(order_x == 0, jnp.where(own, 1, 0), jnp.where(own, 4, 1) + order_x)
    key = stage * 64 + chunk * 8 + (row & 7)
    slot = iota((1, slots), 1)
    key = jnp.where(slot < count, key, 511)
    code = ((chunk * 8 + (row & 7)) << 18) + (slot << 8) + tile + 1

    def column(v):
        return jnp.broadcast_to(v.astype(jnp.float32), (128, slots)).T

    key_row = key.astype(jnp.float32)
    key_col = column(key)[:, :1]
    code_col = column(code)[:, :1]
    same = (key_col == key_row) & (iota((slots, slots), 1) < iota((slots, slots), 0))
    rank = jnp.sum(jnp.where(same, 1.0, 0.0), axis=1, keepdims=True)
    bucket = iota((slots, LANES), 1).astype(jnp.float32)
    member = key_col == bucket
    cnt = jnp.sum(jnp.where(member, 1.0, 0.0), axis=0, keepdims=True).astype(jnp.int32)
    pairs = jnp.broadcast_to((cnt + 1) >> 1, (16, LANES)).astype(jnp.float32).astype(jnp.bfloat16)
    a, b = iota((LANES, LANES), 0), iota((LANES, LANES), 1)

    same_stage = (a >> 6) == (b >> 6)
    opens = ((a & 63) == 0) & ((a >> 6) < (b >> 6))
    inside = jnp.dot(pairs, onehot(same_stage & (a < b)), preferred_element_type=jnp.float32)
    total = jnp.dot(pairs, onehot(same_stage), preferred_element_type=jnp.float32)
    blocks = ((total.astype(jnp.int32) + (PAIRS - 1)) >> 3).astype(jnp.float32)
    blocks = blocks.astype(jnp.bfloat16)
    ahead = jnp.dot(
        blocks, onehot(opens), preferred_element_type=jnp.float32
    )
    begin = (ahead * BLOCK + inside * 2.0)[:1]
    base = jnp.sum(jnp.where(member, begin, 0.0), axis=1, keepdims=True)
    live = iota((slots, 1), 0) < count
    place = jnp.where(live, base + rank, -1.0)
    lists = code_ref.shape[1]
    hit = place == iota((slots, lists), 1).astype(jnp.float32)
    code_ref[...] = jnp.sum(jnp.where(hit, code_col, 0.0), axis=0, keepdims=True).astype(jnp.int32)
    start_ref[...] = ahead[:1].astype(jnp.int32)


def tiles_kernel(stage, n_pieces, outs, *refs):
    opening = stage == 0
    code_ref, start_ref, weights = refs[:3]
    pieces = refs[3 : 3 + n_pieces]
    k = 3 + n_pieces
    if not opening:
        k += 2
    acc, wbuf = refs[k : k + 2]
    out_refs = refs[k + 2 : k + 2 + len(outs)]
    panel, wsem, psem = refs[k + 2 + len(outs) :]
    first = start_ref[64 * stage]
    last = start_ref[64 * stage + 64]
    total = start_ref[256]
    ahead = BUFS - 1

    copies = []
    offset = 1
    for i, piece in enumerate(pieces):
        n = piece.shape[0]
        copies.append(pltpu.make_async_copy(piece, panel.at[pl.ds(offset, n)], psem.at[i]))
        offset += n
    for c in copies:
        c.start()
    panel[0] = jnp.zeros(panel.shape[1:], panel.dtype)

    def fetch(block):
        slot = lax.rem(block, BUFS)
        for i in range(BLOCK):
            s = (code_ref[block * BLOCK + i] >> 8) & 1023
            pltpu.make_async_copy(weights.at[s], wbuf.at[slot, i], wsem.at[slot]).start()

    def arrive(block):
        slot = lax.rem(block, BUFS)
        pltpu.make_async_copy(weights.at[pl.ds(0, BLOCK)], wbuf.at[slot], wsem.at[slot]).wait()

    if opening:
        for i in range(ahead):
            pl.when(first + i < total)(functools.partial(fetch, first + i))

        def clear(i, _):
            acc[i] = jnp.zeros(acc.shape[1:], acc.dtype)
            return 0

        lax.fori_loop(0, acc.shape[0], clear, 0)
    fetched = first if opening else first + ahead
    for c in copies:
        c.wait()

    def run_block(block, _):
        pl.when(block + ahead < total)(functools.partial(fetch, block + ahead))
        pl.when(block >= fetched)(functools.partial(arrive, block))
        slot = lax.rem(block, BUFS)
        for u in range(PAIRS):
            c0 = code_ref[block * BLOCK + 2 * u]
            c1 = code_ref[block * BLOCK + 2 * u + 1]
            w = jnp.concatenate([wbuf[slot, 2 * u], wbuf[slot, 2 * u + 1]], axis=1)
            f = jnp.concatenate([panel[c0 & 255], panel[c1 & 255]], axis=0)
            acc[c0 >> 18] += jnp.dot(w, f, preferred_element_type=jnp.float32)
        return 0

    lax.fori_loop(first, last, run_block, 0)
    for out, (lo, n) in zip(out_refs, outs):

        def give(i, _, out=out, lo=lo):
            out[i] = acc[lo + i].astype(out.dtype)
            return 0

        lax.fori_loop(0, n, give, 0)
    for i in range(ahead):
        pl.when((last + i < total) & (last + i >= fetched))(functools.partial(arrive, last + i))


def run_tiles(stage, code, start, weights, pieces, state=(), outs=()):
    any_spec = pl.BlockSpec(memory_space=pl.ANY)
    vmem = pl.BlockSpec(memory_space=pltpu.VMEM)
    smem = pl.BlockSpec(memory_space=pltpu.SMEM)
    t = weights.shape[1]
    pieces = [p.reshape(-1, t, p.shape[-1]) for p in pieces]
    n = len(pieces)
    tiles = sum(p.shape[0] for p in pieces) + 1
    f = pieces[0].shape[2]
    args = [code, start, weights, *pieces]
    in_specs = [smem, smem] + [any_spec] * (n + 1)
    aliases = {len(args) + i: i for i in range(len(state))}
    out_shape = [
        pltpu.VMEM((64, t, f), jnp.float32),
        pltpu.VMEM((BUFS, BLOCK, t, t), jnp.bfloat16),
    ] + [pltpu.VMEM((k, t, f), jnp.bfloat16) for _, k in outs]
    share = 352 * (tiles - 1) // 128
    return pl.pallas_call(
        functools.partial(tiles_kernel, stage, n, outs),
        out_shape=out_shape,
        in_specs=in_specs + [vmem] * len(state),
        out_specs=[vmem] * len(out_shape),
        scratch_shapes=[
            pltpu.VMEM((tiles, t, f), jnp.bfloat16),
            pltpu.SemaphoreType.DMA((BUFS,)),
            pltpu.SemaphoreType.DMA((n,)),
        ],
        input_output_aliases=aliases,
        compiler_params=pltpu.CompilerParams(vmem_limit_bytes=VMEM_TILES),
        cost_estimate=pl.CostEstimate(
            flops=share * 4 * t * t * f, bytes_accessed=share * 4 * t * t, transcendentals=0
        ),
        name=f"tiles_{stage}",
    )(*args, *state)


def col_perm(dz, dy):
    return [(z * 4 + y, (z + dz) % 4 * 4 + (y + dy) % 4) for z in range(4) for y in range(4)]


def row_perm(dx, flip=0):
    return [(x * 2 + c, (x + dx) % 4 * 2 + (c ^ flip)) for x in range(4) for c in range(2)]


def per_device(
    table, home, degree, tile_rows, tile_cols, tile_count, tile_values, w_self, w_neigh, bias
):
    rows, width = table.shape
    devices = lax.axis_size("row") * lax.axis_size("col")
    slots, tile = tile_values.shape[2:4]
    row_index = lax.axis_index("row")
    col_index = lax.axis_index("col")
    where = jnp.stack([row_index // 2, row_index % 2, col_index // 4, col_index % 4]).astype(
        jnp.int32
    )
    vmem = pl.BlockSpec(memory_space=pltpu.VMEM)
    smem = pl.BlockSpec(memory_space=pltpu.SMEM)
    big = pltpu.CompilerParams(vmem_limit_bytes=48 * MB)

    outgoing = pl.pallas_call(
        pack_kernel,
        out_shape=jax.ShapeDtypeStruct((devices * SLOT_ROWS, width), jnp.bfloat16),
        in_specs=[vmem, vmem],
        out_specs=vmem,
        compiler_params=big,
        name="pack",
    )(home.reshape(1, -1), table)
    incoming = lax.all_to_all(
        outgoing.reshape(devices, SLOT_ROWS, width),
        ("row", "col"),
        split_axis=0,
        concat_axis=0,
        tiled=True,
    )
    half = rows // 2
    quarter = half // 2
    owned = pl.pallas_call(
        unpack_kernel,
        out_shape=jax.ShapeDtypeStruct((rows, width), jnp.bfloat16),
        in_specs=[vmem],
        out_specs=vmem,
        compiler_params=big,
        name="unpack",
    )(incoming.reshape(devices * SLOT_ROWS, width))

    code, start = pl.pallas_call(
        plan_kernel,
        out_shape=(
            jax.ShapeDtypeStruct((1, LIST), jnp.int32),
            jax.ShapeDtypeStruct((1, LANES), jnp.int32),
        ),
        in_specs=[smem, smem, vmem, vmem],
        out_specs=(vmem, vmem),
        compiler_params=big,
        name="plan",
    )(where, tile_count.reshape(1), tile_rows.reshape(1, slots), tile_cols.reshape(1, slots))
    code = code.reshape(LIST)
    start = start.reshape(LANES)
    weights = tile_values.reshape(slots, tile, tile)

    def send(v, dz, dy):
        return lax.ppermute(v, "col", col_perm(dz, dy))

    def spread(to_yp, to_ym, to_zp, to_zm):
        return [send(to_yp, 0, 1), send(to_ym, 0, -1), send(to_zp, 1, 0), send(to_zm, -1, 0)]

    def cat(*parts):
        return jnp.concatenate(parts, axis=0)

    def one(v):
        return v[:half]

    def two(v):
        return v[half:]

    near = spread(owned, owned, owned, owned)
    *near, code, start = lax.optimization_barrier((*near, code, start))
    ym, yp, zm, zp = near
    lists = (code, start, weights)
    diagonal = spread(
        cat(one(zm), one(zp), one(ym)),
        cat(one(zm), one(zp), two(yp)),
        cat(two(ym), two(yp), one(zm)),
        cat(two(ym), two(yp), two(zp)),
    )
    state = run_tiles(0, *lists, [owned, *near])
    (ym, yp, zm, zp), state = lax.optimization_barrier((diagonal, state))
    third = spread(
        cat(ym[half:rows], one(ym)),
        cat(zm[half:rows], zp[half:rows]),
        cat(zm[half:rows], one(zm)),
        cat(ym[half:rows], yp[half:rows]),
    )
    state = run_tiles(1, *lists, [ym, yp, zm, zp], state)
    (ym, yp, zm, zp), state = lax.optimization_barrier((third, state))
    last = spread(zp[:quarter], zp[-quarter:], yp[:quarter], yp[-quarter:])
    state = run_tiles(2, *lists, [ym, yp, zm, zp], state)
    *_, other_far, mine_far, other_rest, mine_rest = run_tiles(
        3, *lists, last, state, ((0, 8), (8, 8), (16, 24), (40, 24))
    )

    f32 = jnp.float32

    def over(v, dx, flip=0):
        return lax.ppermute(v, "row", row_perm(dx, flip))

    got_far = over(other_far.reshape(rows, width), 0, 1)
    across = (mine_far.reshape(rows, width).astype(f32) + got_far.astype(f32)).astype(jnp.bfloat16)
    across, other_rest = lax.optimization_barrier((across, other_rest))
    from_minus, from_plus = over(across[:half], 1), over(across[half:], -1)
    got_rest = over(other_rest.reshape(3, rows, width), 0, 1)
    mine_rest = mine_rest.reshape(3, rows, width)
    both = [mine_rest[i].astype(f32) + got_rest[i].astype(f32) for i in range(3)]
    to_plus = cat(both[0][:half] + from_minus.astype(f32), both[0][half:]).astype(jnp.bfloat16)
    to_minus = cat(both[1][:half], both[1][half:] + from_plus.astype(f32)).astype(jnp.bfloat16)
    summed = both[2] + over(to_plus, 1).astype(f32) + over(to_minus, -1).astype(f32)

    neighbor_mean = (summed / degree.astype(f32)[:, None]).astype(jnp.bfloat16)
    total = jnp.dot(owned, w_self, preferred_element_type=f32)
    total = total + jnp.dot(neighbor_mean, w_neigh, preferred_element_type=f32)
    total = total + bias.astype(f32)[None, :]
    return jnp.maximum(total, f32(0.0)).astype(jnp.bfloat16)


def solution(mesh):
    in_specs = (
        P(("row", "col"), None),
        P(("row", "col")),
        P(("row", "col")),
        P("row", "col", None),
        P("row", "col", None),
        P("row", "col"),
        P("row", "col", None, None, None),
        P(),
        P(),
        P(),
    )
    out_specs = P(("row", "col"), None)
    return jax.shard_map(
        per_device, mesh=mesh, in_specs=in_specs, out_specs=out_specs, check_vma=False
    )
```

```python
import functools

import jax
import jax.numpy as jnp
from jax import lax
from jax.experimental import pallas as pl
from jax.experimental.pallas import tpu as pltpu
from jax.sharding import PartitionSpec as P

SLOT_ROWS = 16
POS_ROW = 12
PAIRS = 8
BLOCK = 2 * PAIRS
BUFS = 8
LIST = 1024
LANES = 384
MB = 1 << 20
VMEM_TILES = 30 * MB


def iota(shape, dim):
    return lax.broadcasted_iota(jnp.int32, shape, dim)


def onehot(mask):
    return jnp.where(mask, 1.0, 0.0).astype(jnp.bfloat16)


def pack_kernel(home_ref, table_ref, out_ref):
    rows = table_ref.shape[0]
    blocks = home_ref.shape[1]
    parts = jnp.where(iota((16, blocks), 0) == 0, home_ref[...] >> 8, home_ref[...] & 255)
    twice = onehot(iota((blocks, rows), 0) == (iota((blocks, rows), 1) >> 1))
    parts = jnp.dot(
        parts.astype(jnp.float32).astype(jnp.bfloat16), twice, preferred_element_type=jnp.float32
    ).astype(jnp.int32)
    home = (parts[:1] << 8) + parts[1:2]
    dest = home >> 9
    pos = home & 511
    dest_f = dest.astype(jnp.float32)
    dest_col = jnp.broadcast_to(dest_f, (128, rows)).T[:, :1]
    before = (dest_col == dest_f) & (iota((rows, rows), 0) < iota((rows, rows), 1))
    rank = jnp.sum(jnp.where(before, 1.0, 0.0), axis=0, keepdims=True).astype(jnp.int32)
    place = dest * SLOT_ROWS + rank
    outs = out_ref.shape[0]
    spread = onehot(iota((outs, rows), 0) == place)
    data = jnp.dot(spread, table_ref[...], preferred_element_type=jnp.float32)
    lane = iota((256, rows), 0)
    high = jnp.broadcast_to(((pos >> 1) + 1).astype(jnp.float32), (256, rows))
    low = jnp.broadcast_to((pos & 1).astype(jnp.float32), (256, rows))
    marks = jnp.where(lane == rank, high, jnp.where(lane == rank + 128, low, 0.0)).astype(
        jnp.bfloat16
    )
    owner = onehot(iota((128, rows), 0) == dest)
    pos_rows = lax.dot_general(
        owner, marks, (((1,), (1,)), ((), ())), preferred_element_type=jnp.float32
    ).astype(jnp.bfloat16)
    lift = onehot(iota((outs, 128), 0) == iota((outs, 128), 1) * SLOT_ROWS + POS_ROW)
    data = data + jnp.dot(lift, pos_rows, preferred_element_type=jnp.float32)
    out_ref[...] = data.astype(jnp.bfloat16)


def unpack_kernel(in_ref, a_ref, b_ref):
    ins = in_ref.shape[0]
    rows = a_ref.shape[0] + b_ref.shape[0]
    data = in_ref[...]
    drop = onehot(iota((128, ins), 1) == iota((128, ins), 0) * SLOT_ROWS + POS_ROW)
    pos_rows = jnp.dot(drop, data, preferred_element_type=jnp.float32).astype(jnp.bfloat16)
    within = onehot(iota((128, ins), 0) == (iota((128, ins), 1) & (SLOT_ROWS - 1)))
    mine = (iota((128, ins), 1) >> 4) == iota((128, ins), 0)

    def lanes(part):
        spread = jnp.dot(part, within, preferred_element_type=jnp.float32)
        return jnp.sum(jnp.where(mine, spread, 0.0), axis=0, keepdims=True).astype(jnp.int32)

    high = lanes(pos_rows[:, :128])
    low = lanes(pos_rows[:, 128:])
    target = 4 * (high - 1) + 2 * low + (iota((1, ins), 1) & 1)
    pick = onehot(iota((rows, ins), 0) == target)
    owned = jnp.dot(pick, data, preferred_element_type=jnp.float32).astype(jnp.bfloat16)
    a_ref[...] = owned[: rows // 2]
    b_ref[...] = owned[rows // 2 :]


def ring_order(step):
    return jnp.where(step == 0, 0, jnp.where(step == 3, 1, jnp.where(step == 1, 2, 3)))


def plan_kernel(where_ref, count_ref, rows_ref, cols_ref, code_ref, start_ref):
    slots = rows_ref.shape[1]
    count = count_ref[0]
    x, core, z, y = where_ref[0], where_ref[1], where_ref[2], where_ref[3]
    row = rows_ref[...]
    col = cols_ref[...]
    source = col >> 3
    order_z = ring_order(((source >> 2) - z) & 3)
    order_y = ring_order(((source & 3) - y) & 3)
    half = (col >> 2) & 1
    outer = jnp.where(half == 0, order_z, order_y)
    inner = jnp.where(half == 0, order_y, order_z)
    stage = jnp.where((outer == 1) == (inner < 2), 1, 2)
    stage = jnp.where(outer == 3, 3, jnp.where(outer == 0, 0, stage))
    tile = half * 16 + inner * 4 + (col & 3)
    owner = row >> 3
    dx = ((owner >> 1) - x) & 3
    order_x = jnp.where(dx == 2, 0, jnp.where(dx == 1, 1, jnp.where(dx == 3, 2, 3)))
    own = (owner & 1) == core
    chunk = jnp.where(order_x == 0, jnp.where(own, 1, 0), jnp.where(own, 4, 1) + order_x)
    key = stage * 64 + chunk * 8 + (row & 7)
    slot = iota((1, slots), 1)
    key = jnp.where(slot < count, key, 511)
    code = ((chunk * 8 + (row & 7)) << 18) + (slot << 8) + tile + 1

    def column(v):
        return jnp.broadcast_to(v.astype(jnp.float32), (128, slots)).T

    key_row = key.astype(jnp.float32)
    key_col = column(key)[:, :1]
    code_col = column(code)[:, :1]
    same = (key_col == key_row) & (iota((slots, slots), 1) < iota((slots, slots), 0))
    rank = jnp.sum(jnp.where(same, 1.0, 0.0), axis=1, keepdims=True)
    bucket = iota((slots, LANES), 1).astype(jnp.float32)
    member = key_col == bucket
    cnt = jnp.sum(jnp.where(member, 1.0, 0.0), axis=0, keepdims=True).astype(jnp.int32)
    pairs = jnp.broadcast_to((cnt + 1) >> 1, (16, LANES)).astype(jnp.float32).astype(jnp.bfloat16)
    a, b = iota((LANES, LANES), 0), iota((LANES, LANES), 1)

    same_stage = (a >> 6) == (b >> 6)
    opens = ((a & 63) == 0) & ((a >> 6) < (b >> 6))
    inside = jnp.dot(pairs, onehot(same_stage & (a < b)), preferred_element_type=jnp.float32)
    total = jnp.dot(pairs, onehot(same_stage), preferred_element_type=jnp.float32)
    blocks = ((total.astype(jnp.int32) + (PAIRS - 1)) >> 3).astype(jnp.float32)
    blocks = blocks.astype(jnp.bfloat16)
    ahead = jnp.dot(
        blocks, onehot(opens), preferred_element_type=jnp.float32
    )
    begin = (ahead * BLOCK + inside * 2.0)[:1]
    base = jnp.sum(jnp.where(member, begin, 0.0), axis=1, keepdims=True)
    live = iota((slots, 1), 0) < count
    place = jnp.where(live, base + rank, -1.0)
    lists = code_ref.shape[1]
    hit = place == iota((slots, lists), 1).astype(jnp.float32)
    code_ref[...] = jnp.sum(jnp.where(hit, code_col, 0.0), axis=0, keepdims=True).astype(jnp.int32)
    start_ref[...] = ahead[:1].astype(jnp.int32)


def tiles_kernel(stage, n_pieces, outs, *refs):
    opening = stage == 0
    code_ref, start_ref, weights = refs[:3]
    pieces = refs[3 : 3 + n_pieces]
    k = 3 + n_pieces
    if not opening:
        k += 2
    acc, wbuf = refs[k : k + 2]
    out_refs = refs[k + 2 : k + 2 + len(outs)]
    panel, wsem, psem = refs[k + 2 + len(outs) :]
    first = start_ref[64 * stage]
    last = start_ref[64 * stage + 64]
    total = start_ref[256]
    ahead = BUFS - 1

    copies = []
    offset = 1
    for i, piece in enumerate(pieces):
        n = piece.shape[0]
        copies.append(pltpu.make_async_copy(piece, panel.at[pl.ds(offset, n)], psem.at[i]))
        offset += n
    for c in copies:
        c.start()
    panel[0] = jnp.zeros(panel.shape[1:], panel.dtype)

    def fetch(block):
        slot = lax.rem(block, BUFS)
        for i in range(BLOCK):
            s = (code_ref[block * BLOCK + i] >> 8) & 1023
            pltpu.make_async_copy(weights.at[s], wbuf.at[slot, i], wsem.at[slot]).start()

    def arrive(block):
        slot = lax.rem(block, BUFS)
        pltpu.make_async_copy(weights.at[pl.ds(0, BLOCK)], wbuf.at[slot], wsem.at[slot]).wait()

    if opening:
        for i in range(ahead):
            pl.when(first + i < total)(functools.partial(fetch, first + i))

        def clear(i, _):
            acc[i] = jnp.zeros(acc.shape[1:], acc.dtype)
            return 0

        lax.fori_loop(0, acc.shape[0], clear, 0)
    fetched = first if opening else first + ahead
    for c in copies:
        c.wait()

    def run_block(block, _):
        pl.when(block + ahead < total)(functools.partial(fetch, block + ahead))
        pl.when(block >= fetched)(functools.partial(arrive, block))
        slot = lax.rem(block, BUFS)
        for u in range(PAIRS):
            c0 = code_ref[block * BLOCK + 2 * u]
            c1 = code_ref[block * BLOCK + 2 * u + 1]
            w = jnp.concatenate([wbuf[slot, 2 * u], wbuf[slot, 2 * u + 1]], axis=1)
            f = jnp.concatenate([panel[c0 & 255], panel[c1 & 255]], axis=0)
            acc[c0 >> 18] += jnp.dot(w, f, preferred_element_type=jnp.float32)
        return 0

    lax.fori_loop(first, last, run_block, 0)
    for out, (lo, n) in zip(out_refs, outs):

        def give(i, _, out=out, lo=lo):
            out[i] = acc[lo + i].astype(out.dtype)
            return 0

        lax.fori_loop(0, n, give, 0)
    for i in range(ahead):
        pl.when((last + i < total) & (last + i >= fetched))(functools.partial(arrive, last + i))


def run_tiles(stage, code, start, weights, pieces, state=(), outs=()):
    any_spec = pl.BlockSpec(memory_space=pl.ANY)
    vmem = pl.BlockSpec(memory_space=pltpu.VMEM)
    smem = pl.BlockSpec(memory_space=pltpu.SMEM)
    t = weights.shape[1]
    pieces = [p.reshape(-1, t, p.shape[-1]) for p in pieces]
    n = len(pieces)
    tiles = sum(p.shape[0] for p in pieces) + 1
    f = pieces[0].shape[2]
    args = [code, start, weights, *pieces]
    in_specs = [smem, smem] + [any_spec] * (n + 1)
    aliases = {len(args) + i: i for i in range(len(state))}
    out_shape = [
        pltpu.VMEM((64, t, f), jnp.float32),
        pltpu.VMEM((BUFS, BLOCK, t, t), jnp.bfloat16),
    ] + [pltpu.VMEM((k, t, f), jnp.bfloat16) for _, k in outs]
    share = 352 * (tiles - 1) // 128
    return pl.pallas_call(
        functools.partial(tiles_kernel, stage, n, outs),
        out_shape=out_shape,
        in_specs=in_specs + [vmem] * len(state),
        out_specs=[vmem] * len(out_shape),
        scratch_shapes=[
            pltpu.VMEM((tiles, t, f), jnp.bfloat16),
            pltpu.SemaphoreType.DMA((BUFS,)),
            pltpu.SemaphoreType.DMA((n,)),
        ],
        input_output_aliases=aliases,
        compiler_params=pltpu.CompilerParams(vmem_limit_bytes=VMEM_TILES),
        cost_estimate=pl.CostEstimate(
            flops=share * 4 * t * t * f, bytes_accessed=share * 4 * t * t, transcendentals=0
        ),
        name=f"tiles_{stage}",
    )(*args, *state)


def col_perm(dz, dy):
    return [(z * 4 + y, (z + dz) % 4 * 4 + (y + dy) % 4) for z in range(4) for y in range(4)]


def row_perm(dx, flip=0):
    return [(x * 2 + c, (x + dx) % 4 * 2 + (c ^ flip)) for x in range(4) for c in range(2)]


def per_device(
    table, home, degree, tile_rows, tile_cols, tile_count, tile_values, w_self, w_neigh, bias
):
    rows, width = table.shape
    devices = lax.axis_size("row") * lax.axis_size("col")
    slots, tile = tile_values.shape[2:4]
    row_index = lax.axis_index("row")
    col_index = lax.axis_index("col")
    where = jnp.stack([row_index // 2, row_index % 2, col_index // 4, col_index % 4]).astype(
        jnp.int32
    )
    vmem = pl.BlockSpec(memory_space=pltpu.VMEM)
    smem = pl.BlockSpec(memory_space=pltpu.SMEM)
    big = pltpu.CompilerParams(vmem_limit_bytes=48 * MB)

    outgoing = pl.pallas_call(
        pack_kernel,
        out_shape=jax.ShapeDtypeStruct((devices * SLOT_ROWS, width), jnp.bfloat16),
        in_specs=[vmem, vmem],
        out_specs=vmem,
        compiler_params=big,
        name="pack",
    )(home.reshape(1, -1), table)
    incoming = lax.all_to_all(
        outgoing.reshape(devices, SLOT_ROWS, width),
        ("row", "col"),
        split_axis=0,
        concat_axis=0,
        tiled=True,
    )
    half = rows // 2
    quarter = half // 2
    a0, b0 = pl.pallas_call(
        unpack_kernel,
        out_shape=(jax.ShapeDtypeStruct((half, width), jnp.bfloat16),) * 2,
        in_specs=[vmem],
        out_specs=(vmem, vmem),
        compiler_params=big,
        name="unpack",
    )(incoming.reshape(devices * SLOT_ROWS, width))

    code, start = pl.pallas_call(
        plan_kernel,
        out_shape=(
            jax.ShapeDtypeStruct((1, LIST), jnp.int32),
            jax.ShapeDtypeStruct((1, LANES), jnp.int32),
        ),
        in_specs=[smem, smem, vmem, vmem],
        out_specs=(vmem, vmem),
        compiler_params=big,
        name="plan",
    )(where, tile_count.reshape(1), tile_rows.reshape(1, slots), tile_cols.reshape(1, slots))
    code = code.reshape(LIST)
    start = start.reshape(LANES)
    weights = tile_values.reshape(slots, tile, tile)

    def send(v, dz, dy):
        return lax.ppermute(v, "col", col_perm(dz, dy))

    def cat(*parts):
        return jnp.concatenate(parts, axis=0)

    ap, am = send(a0, 0, 1), send(a0, 0, -1)
    bp, bm = send(b0, 1, 0), send(b0, -1, 0)
    bp, bm, code, start = lax.optimization_barrier((bp, bm, code, start))
    a_far = (send(ap[:quarter], 0, 1), send(am[quarter:], 0, -1))
    b_far = (send(bp[:quarter], 1, 0), send(bm[quarter:], -1, 0))
    ap, b_far = lax.optimization_barrier((ap, b_far))
    bp, a_far = lax.optimization_barrier((bp, a_far))
    a_lo, b_lo = cat(a0, ap), cat(b0, bp)
    a_hi, b_hi = cat(am, *a_far), cat(bm, *b_far)
    lists = (code, start, weights)
    a_lo_p, a_hi_m = send(a_lo, 1, 0), send(a_hi, -1, 0)
    b_lo_p, b_hi_m = send(b_lo, 0, 1), send(b_hi, 0, -1)
    state = run_tiles(0, *lists, [a_lo, a_hi, b_lo, b_hi])
    a_lo, a_hi, b_lo, b_hi, *state = lax.optimization_barrier((a_lo, a_hi, b_lo, b_hi, *state))
    a_hi_p, a_lo_m = send(a_hi, 1, 0), send(a_lo, -1, 0)
    b_hi_p, b_lo_m = send(b_hi, 0, 1), send(b_lo, 0, -1)
    state = run_tiles(1, *lists, [a_lo_p, a_hi_m, b_lo_p, b_hi_m], state)
    a_lo_p, a_hi_m, b_lo_p, b_hi_m, *state = lax.optimization_barrier(
        (a_lo_p, a_hi_m, b_lo_p, b_hi_m, *state)
    )
    far = [send(a_lo_p, 1, 0), send(a_hi_m, -1, 0), send(b_lo_p, 0, 1), send(b_hi_m, 0, -1)]
    state = run_tiles(2, *lists, [a_lo_m, a_hi_p, b_lo_m, b_hi_p], state)
    *_, other_far, mine_far, other_rest, mine_rest = run_tiles(
        3, *lists, far, state, ((0, 8), (8, 8), (16, 24), (40, 24))
    )

    f32 = jnp.float32

    def over(v, dx, flip=0):
        return lax.ppermute(v, "row", row_perm(dx, flip))

    got_far = over(other_far.reshape(rows, width), 0, 1)
    across = (mine_far.reshape(rows, width).astype(f32) + got_far.astype(f32)).astype(jnp.bfloat16)
    across, other_rest = lax.optimization_barrier((across, other_rest))
    from_minus, from_plus = over(across[:half], 1), over(across[half:], -1)
    got_rest = over(other_rest.reshape(3, rows, width), 0, 1)
    mine_rest = mine_rest.reshape(3, rows, width)
    both = [mine_rest[i].astype(f32) + got_rest[i].astype(f32) for i in range(3)]
    to_plus = cat(both[0][:half] + from_minus.astype(f32), both[0][half:]).astype(jnp.bfloat16)
    to_minus = cat(both[1][:half], both[1][half:] + from_plus.astype(f32)).astype(jnp.bfloat16)
    summed = both[2] + over(to_plus, 1).astype(f32) + over(to_minus, -1).astype(f32)

    neighbor_mean = (summed / degree.astype(f32)[:, None]).astype(jnp.bfloat16)
    total = jnp.dot(cat(a0, b0), w_self, preferred_element_type=f32)
    total = total + jnp.dot(neighbor_mean, w_neigh, preferred_element_type=f32)
    total = total + bias.astype(f32)[None, :]
    return jnp.maximum(total, f32(0.0)).astype(jnp.bfloat16)


def solution(mesh):
    in_specs = (
        P(("row", "col"), None),
        P(("row", "col")),
        P(("row", "col")),
        P("row", "col", None),
        P("row", "col", None),
        P("row", "col"),
        P("row", "col", None, None, None),
        P(),
        P(),
        P(),
    )
    out_specs = P(("row", "col"), None)
    return jax.shard_map(
        per_device, mesh=mesh, in_specs=in_specs, out_specs=out_specs, check_vma=False
    )
```

```python
import functools

import jax
import jax.numpy as jnp
from jax import lax
from jax.experimental import pallas as pl
from jax.experimental.pallas import tpu as pltpu
from jax.sharding import PartitionSpec as P

SLOT_ROWS = 16
POS_ROW = 12
PAIRS = 8
BLOCK = 2 * PAIRS
BUFS = 8
LIST = 1024
LANES = 384
MB = 1 << 20
VMEM_TILES = 30 * MB


def iota(shape, dim):
    return lax.broadcasted_iota(jnp.int32, shape, dim)


def onehot(mask):
    return jnp.where(mask, 1.0, 0.0).astype(jnp.bfloat16)


def pack_kernel(home_ref, table_ref, out_ref):
    rows = table_ref.shape[0]
    blocks = home_ref.shape[1]
    parts = jnp.where(iota((16, blocks), 0) == 0, home_ref[...] >> 8, home_ref[...] & 255)
    twice = onehot(iota((blocks, rows), 0) == (iota((blocks, rows), 1) >> 1))
    parts = jnp.dot(
        parts.astype(jnp.float32).astype(jnp.bfloat16), twice, preferred_element_type=jnp.float32
    ).astype(jnp.int32)
    home = (parts[:1] << 8) + parts[1:2]
    dest = home >> 9
    pos = home & 511
    dest_f = dest.astype(jnp.float32)
    dest_col = jnp.broadcast_to(dest_f, (128, rows)).T[:, :1]
    before = (dest_col == dest_f) & (iota((rows, rows), 0) < iota((rows, rows), 1))
    rank = jnp.sum(jnp.where(before, 1.0, 0.0), axis=0, keepdims=True).astype(jnp.int32)
    place = dest * SLOT_ROWS + rank
    outs = out_ref.shape[0]
    spread = onehot(iota((outs, rows), 0) == place)
    data = jnp.dot(spread, table_ref[...], preferred_element_type=jnp.float32)
    lane = iota((256, rows), 0)
    high = jnp.broadcast_to(((pos >> 1) + 1).astype(jnp.float32), (256, rows))
    low = jnp.broadcast_to((pos & 1).astype(jnp.float32), (256, rows))
    marks = jnp.where(lane == rank, high, jnp.where(lane == rank + 128, low, 0.0)).astype(
        jnp.bfloat16
    )
    owner = onehot(iota((128, rows), 0) == dest)
    pos_rows = lax.dot_general(
        owner, marks, (((1,), (1,)), ((), ())), preferred_element_type=jnp.float32
    ).astype(jnp.bfloat16)
    lift = onehot(iota((outs, 128), 0) == iota((outs, 128), 1) * SLOT_ROWS + POS_ROW)
    data = data + jnp.dot(lift, pos_rows, preferred_element_type=jnp.float32)
    out_ref[...] = data.astype(jnp.bfloat16)


def unpack_kernel(in_ref, out_ref):
    ins = in_ref.shape[0]
    rows = out_ref.shape[0]
    data = in_ref[...]
    drop = onehot(iota((128, ins), 1) == iota((128, ins), 0) * SLOT_ROWS + POS_ROW)
    pos_rows = jnp.dot(drop, data, preferred_element_type=jnp.float32).astype(jnp.bfloat16)
    within = onehot(iota((128, ins), 0) == (iota((128, ins), 1) & (SLOT_ROWS - 1)))
    mine = (iota((128, ins), 1) >> 4) == iota((128, ins), 0)

    def lanes(part):
        spread = jnp.dot(part, within, preferred_element_type=jnp.float32)
        return jnp.sum(jnp.where(mine, spread, 0.0), axis=0, keepdims=True).astype(jnp.int32)

    high = lanes(pos_rows[:, :128])
    low = lanes(pos_rows[:, 128:])
    target = 4 * (high - 1) + 2 * low + (iota((1, ins), 1) & 1)
    pick = onehot(iota((rows, ins), 0) == target)
    out_ref[...] = jnp.dot(pick, data, preferred_element_type=jnp.float32).astype(jnp.bfloat16)


def ring_order(step):
    return jnp.where(step == 0, 0, jnp.where(step == 3, 1, jnp.where(step == 1, 2, 3)))


def plan_kernel(where_ref, count_ref, rows_ref, cols_ref, code_ref, start_ref):
    slots = rows_ref.shape[1]
    count = count_ref[0]
    x, core, z, y = where_ref[0], where_ref[1], where_ref[2], where_ref[3]
    row = rows_ref[...]
    col = cols_ref[...]
    source = col >> 3
    order_z = ring_order(((source >> 2) - z) & 3)
    order_y = ring_order(((source & 3) - y) & 3)
    outer = jnp.where(core == 0, order_z, order_y)
    inner = jnp.where(core == 0, order_y, order_z)
    stage = jnp.where((outer == 1) == (inner < 2), 1, 2)
    stage = jnp.where(outer == 3, 3, jnp.where(outer == 0, 0, stage))
    tile = inner * 8 + (col & 7)
    owner = row >> 3
    dx = ((owner >> 1) - x) & 3
    order_x = jnp.where(dx == 2, 0, jnp.where(dx == 1, 1, jnp.where(dx == 3, 2, 3)))
    own = (owner & 1) == core
    chunk = jnp.where(order_x == 0, jnp.where(own, 1, 0), jnp.where(own, 4, 1) + order_x)
    key = stage * 64 + chunk * 8 + (row & 7)
    slot = iota((1, slots), 1)
    key = jnp.where(slot < count, key, 511)
    code = ((chunk * 8 + (row & 7)) << 18) + (slot << 8) + tile + 1

    def column(v):
        return jnp.broadcast_to(v.astype(jnp.float32), (128, slots)).T

    key_row = key.astype(jnp.float32)
    key_col = column(key)[:, :1]
    code_col = column(code)[:, :1]
    same = (key_col == key_row) & (iota((slots, slots), 1) < iota((slots, slots), 0))
    rank = jnp.sum(jnp.where(same, 1.0, 0.0), axis=1, keepdims=True)
    bucket = iota((slots, LANES), 1).astype(jnp.float32)
    member = key_col == bucket
    cnt = jnp.sum(jnp.where(member, 1.0, 0.0), axis=0, keepdims=True).astype(jnp.int32)
    pairs = jnp.broadcast_to((cnt + 1) >> 1, (16, LANES)).astype(jnp.float32).astype(jnp.bfloat16)
    a, b = iota((LANES, LANES), 0), iota((LANES, LANES), 1)

    same_stage = (a >> 6) == (b >> 6)
    opens = ((a & 63) == 0) & ((a >> 6) < (b >> 6))
    inside = jnp.dot(pairs, onehot(same_stage & (a < b)), preferred_element_type=jnp.float32)
    total = jnp.dot(pairs, onehot(same_stage), preferred_element_type=jnp.float32)
    blocks = ((total.astype(jnp.int32) + (PAIRS - 1)) >> 3).astype(jnp.float32)
    blocks = blocks.astype(jnp.bfloat16)
    ahead = jnp.dot(
        blocks, onehot(opens), preferred_element_type=jnp.float32
    )
    begin = (ahead * BLOCK + inside * 2.0)[:1]
    base = jnp.sum(jnp.where(member, begin, 0.0), axis=1, keepdims=True)
    live = iota((slots, 1), 0) < count
    place = jnp.where(live, base + rank, -1.0)
    lists = code_ref.shape[1]
    hit = place == iota((slots, lists), 1).astype(jnp.float32)
    code_ref[...] = jnp.sum(jnp.where(hit, code_col, 0.0), axis=0, keepdims=True).astype(jnp.int32)
    start_ref[...] = ahead[:1].astype(jnp.int32)


def tiles_kernel(stage, n_pieces, outs, *refs):
    opening = stage == 0
    code_ref, start_ref, weights = refs[:3]
    pieces = refs[3 : 3 + n_pieces]
    k = 3 + n_pieces
    if not opening:
        k += 2
    acc, wbuf = refs[k : k + 2]
    out_refs = refs[k + 2 : k + 2 + len(outs)]
    panel, wsem, psem = refs[k + 2 + len(outs) :]
    first = start_ref[64 * stage]
    last = start_ref[64 * stage + 64]
    total = start_ref[256]
    ahead = BUFS - 1

    copies = []
    offset = 1
    for i, piece in enumerate(pieces):
        n = piece.shape[0]
        copies.append(pltpu.make_async_copy(piece, panel.at[pl.ds(offset, n)], psem.at[i]))
        offset += n
    for c in copies:
        c.start()
    panel[0] = jnp.zeros(panel.shape[1:], panel.dtype)

    def fetch(block):
        slot = lax.rem(block, BUFS)
        for i in range(BLOCK):
            s = (code_ref[block * BLOCK + i] >> 8) & 1023
            pltpu.make_async_copy(weights.at[s], wbuf.at[slot, i], wsem.at[slot]).start()

    def arrive(block):
        slot = lax.rem(block, BUFS)
        pltpu.make_async_copy(weights.at[pl.ds(0, BLOCK)], wbuf.at[slot], wsem.at[slot]).wait()

    if opening:
        for i in range(ahead):
            pl.when(first + i < total)(functools.partial(fetch, first + i))

        def clear(i, _):
            acc[i] = jnp.zeros(acc.shape[1:], acc.dtype)
            return 0

        lax.fori_loop(0, acc.shape[0], clear, 0)
    fetched = first if opening else first + ahead
    for c in copies:
        c.wait()

    def run_block(block, _):
        pl.when(block + ahead < total)(functools.partial(fetch, block + ahead))
        pl.when(block >= fetched)(functools.partial(arrive, block))
        slot = lax.rem(block, BUFS)
        for u in range(PAIRS):
            c0 = code_ref[block * BLOCK + 2 * u]
            c1 = code_ref[block * BLOCK + 2 * u + 1]
            w = jnp.concatenate([wbuf[slot, 2 * u], wbuf[slot, 2 * u + 1]], axis=1)
            f = jnp.concatenate([panel[c0 & 255], panel[c1 & 255]], axis=0)
            acc[c0 >> 18] += jnp.dot(w, f, preferred_element_type=jnp.float32)
        return 0

    lax.fori_loop(first, last, run_block, 0)
    for out, (lo, n) in zip(out_refs, outs):

        def give(i, _, out=out, lo=lo):
            out[i] = acc[lo + i].astype(out.dtype)
            return 0

        lax.fori_loop(0, n, give, 0)
    for i in range(ahead):
        pl.when((last + i < total) & (last + i >= fetched))(functools.partial(arrive, last + i))


def run_tiles(stage, code, start, weights, pieces, state=(), outs=()):
    any_spec = pl.BlockSpec(memory_space=pl.ANY)
    vmem = pl.BlockSpec(memory_space=pltpu.VMEM)
    smem = pl.BlockSpec(memory_space=pltpu.SMEM)
    t = weights.shape[1]
    pieces = [p.reshape(-1, t, p.shape[-1]) for p in pieces]
    n = len(pieces)
    tiles = sum(p.shape[0] for p in pieces) + 1
    f = pieces[0].shape[2]
    args = [code, start, weights, *pieces]
    in_specs = [smem, smem] + [any_spec] * (n + 1)
    aliases = {len(args) + i: i for i in range(len(state))}
    out_shape = [
        pltpu.VMEM((64, t, f), jnp.float32),
        pltpu.VMEM((BUFS, BLOCK, t, t), jnp.bfloat16),
    ] + [pltpu.VMEM((k, t, f), jnp.bfloat16) for _, k in outs]
    share = 352 * (tiles - 1) // 128
    return pl.pallas_call(
        functools.partial(tiles_kernel, stage, n, outs),
        out_shape=out_shape,
        in_specs=in_specs + [vmem] * len(state),
        out_specs=[vmem] * len(out_shape),
        scratch_shapes=[
            pltpu.VMEM((tiles, t, f), jnp.bfloat16),
            pltpu.SemaphoreType.DMA((BUFS,)),
            pltpu.SemaphoreType.DMA((n,)),
        ],
        input_output_aliases=aliases,
        compiler_params=pltpu.CompilerParams(vmem_limit_bytes=VMEM_TILES),
        cost_estimate=pl.CostEstimate(
            flops=share * 4 * t * t * f, bytes_accessed=share * 4 * t * t, transcendentals=0
        ),
        name=f"tiles_{stage}",
    )(*args, *state)


def panel_perm(turn, step):
    pairs = []
    for row in range(8):
        along_y = row % 2 == turn
        for z in range(4):
            for y in range(4):
                to = z * 4 + (y + step) % 4 if along_y else (z + step) % 4 * 4 + y
                pairs.append((row * 16 + z * 4 + y, row * 16 + to))
    return pairs


def row_perm(dx, flip=0):
    return [(x * 2 + c, (x + dx) % 4 * 2 + (c ^ flip)) for x in range(4) for c in range(2)]


def per_device(
    table, home, degree, tile_rows, tile_cols, tile_count, tile_values, w_self, w_neigh, bias
):
    rows, width = table.shape
    devices = lax.axis_size("row") * lax.axis_size("col")
    slots, tile = tile_values.shape[2:4]
    row_index = lax.axis_index("row")
    col_index = lax.axis_index("col")
    where = jnp.stack([row_index // 2, row_index % 2, col_index // 4, col_index % 4]).astype(
        jnp.int32
    )
    vmem = pl.BlockSpec(memory_space=pltpu.VMEM)
    smem = pl.BlockSpec(memory_space=pltpu.SMEM)
    big = pltpu.CompilerParams(vmem_limit_bytes=48 * MB)

    outgoing = pl.pallas_call(
        pack_kernel,
        out_shape=jax.ShapeDtypeStruct((devices * SLOT_ROWS, width), jnp.bfloat16),
        in_specs=[vmem, vmem],
        out_specs=vmem,
        compiler_params=big,
        name="pack",
    )(home.reshape(1, -1), table)
    incoming = lax.all_to_all(
        outgoing.reshape(devices, SLOT_ROWS, width),
        ("row", "col"),
        split_axis=0,
        concat_axis=0,
        tiled=True,
    )
    half = rows // 2
    owned = pl.pallas_call(
        unpack_kernel,
        out_shape=jax.ShapeDtypeStruct((rows, width), jnp.bfloat16),
        in_specs=[vmem],
        out_specs=vmem,
        compiler_params=big,
        name="unpack",
    )(incoming.reshape(devices * SLOT_ROWS, width))

    code, start = pl.pallas_call(
        plan_kernel,
        out_shape=(
            jax.ShapeDtypeStruct((1, LIST), jnp.int32),
            jax.ShapeDtypeStruct((1, LANES), jnp.int32),
        ),
        in_specs=[smem, smem, vmem, vmem],
        out_specs=(vmem, vmem),
        compiler_params=big,
        name="plan",
    )(where, tile_count.reshape(1), tile_rows.reshape(1, slots), tile_cols.reshape(1, slots))
    code = code.reshape(LIST)
    start = start.reshape(LANES)
    weights = tile_values.reshape(slots, tile, tile)

    def send(v, turn, step):
        return lax.ppermute(v, ("row", "col"), panel_perm(turn, step))

    def cat(*parts):
        return jnp.concatenate(parts, axis=0)

    plus, minus = send(owned, 0, 1), send(owned, 0, -1)
    plus, minus, code, start = lax.optimization_barrier((plus, minus, code, start))
    hi = cat(minus, send(plus[:half], 0, 1), send(minus[half:], 0, -1))
    hi, plus = lax.optimization_barrier((hi, plus))
    lo = cat(owned, plus)
    lists = (code, start, weights)
    lo_p, hi_m = send(lo, 1, 1), send(hi, 1, -1)
    hi_p, lo_m = send(hi, 1, 1), send(lo, 1, -1)
    state = run_tiles(0, *lists, [lo, hi])
    lo_p, hi_m, *state = lax.optimization_barrier((lo_p, hi_m, *state))
    far = [send(lo_p, 1, 1), send(hi_m, 1, -1)]
    state = run_tiles(1, *lists, [lo_p, hi_m], state)
    state = run_tiles(2, *lists, [lo_m, hi_p], state)
    *_, other_far, mine_far, other_rest, mine_rest = run_tiles(
        3, *lists, far, state, ((0, 8), (8, 8), (16, 24), (40, 24))
    )

    f32 = jnp.float32

    def over(v, dx, flip=0):
        return lax.ppermute(v, "row", row_perm(dx, flip))

    got_far = over(other_far.reshape(rows, width), 0, 1)
    across = (mine_far.reshape(rows, width).astype(f32) + got_far.astype(f32)).astype(jnp.bfloat16)
    across, other_rest = lax.optimization_barrier((across, other_rest))
    from_minus, from_plus = over(across[:half], 1), over(across[half:], -1)
    got_rest = over(other_rest.reshape(3, rows, width), 0, 1)
    mine_rest = mine_rest.reshape(3, rows, width)
    both = [mine_rest[i].astype(f32) + got_rest[i].astype(f32) for i in range(3)]
    to_plus = cat(both[0][:half] + from_minus.astype(f32), both[0][half:]).astype(jnp.bfloat16)
    to_minus = cat(both[1][:half], both[1][half:] + from_plus.astype(f32)).astype(jnp.bfloat16)
    summed = both[2] + over(to_plus, 1).astype(f32) + over(to_minus, -1).astype(f32)

    neighbor_mean = (summed / degree.astype(f32)[:, None]).astype(jnp.bfloat16)
    total = jnp.dot(owned, w_self, preferred_element_type=f32)
    total = total + jnp.dot(neighbor_mean, w_neigh, preferred_element_type=f32)
    total = total + bias.astype(f32)[None, :]
    return jnp.maximum(total, f32(0.0)).astype(jnp.bfloat16)


def solution(mesh):
    in_specs = (
        P(("row", "col"), None),
        P(("row", "col")),
        P(("row", "col")),
        P("row", "col", None),
        P("row", "col", None),
        P("row", "col"),
        P("row", "col", None, None, None),
        P(),
        P(),
        P(),
    )
    out_specs = P(("row", "col"), None)
    return jax.shard_map(
        per_device, mesh=mesh, in_specs=in_specs, out_specs=out_specs, check_vma=False
    )
```

```python
import functools

import jax
import jax.numpy as jnp
from jax import lax
from jax.experimental import pallas as pl
from jax.experimental.pallas import tpu as pltpu
from jax.sharding import PartitionSpec as P

SLOT_ROWS = 16
POS_ROW = 12
PAIRS = 8
BLOCK = 2 * PAIRS
BUFS = 8
LIST = 1152
STAGES = 5
LANES = 384
MB = 1 << 20
VMEM_TILES = 30 * MB


def iota(shape, dim):
    return lax.broadcasted_iota(jnp.int32, shape, dim)


def onehot(mask):
    return jnp.where(mask, 1.0, 0.0).astype(jnp.bfloat16)


def pack_kernel(home_ref, table_ref, out_ref):
    rows = table_ref.shape[0]
    blocks = home_ref.shape[1]
    home = home_ref[...]
    dest = home >> 9
    dest_f = dest.astype(jnp.float32)
    dest_col = jnp.broadcast_to(dest_f, (128, blocks)).T[:, :1]
    before = (dest_col == dest_f) & (iota((blocks, blocks), 0) < iota((blocks, blocks), 1))
    rank = jnp.sum(jnp.where(before, 1.0, 0.0), axis=0, keepdims=True).astype(jnp.int32)
    line = iota((16, blocks), 0)
    parts = jnp.where(line == 2, (home & 511) >> 1, home & 1)
    parts = jnp.where(line == 0, dest, jnp.where(line == 1, rank, parts))
    twice = onehot(iota((blocks, rows), 0) == (iota((blocks, rows), 1) >> 1))
    parts = jnp.dot(
        parts.astype(jnp.float32).astype(jnp.bfloat16), twice, preferred_element_type=jnp.float32
    ).astype(jnp.int32)
    dest = parts[:1]
    rank = parts[1:2] * 2 + (iota((1, rows), 1) & 1)
    place = dest * SLOT_ROWS + rank
    outs = out_ref.shape[0]
    spread = onehot(iota((outs, rows), 0) == place)
    data = jnp.dot(spread, table_ref[...], preferred_element_type=jnp.float32)
    lane = iota((256, rows), 0)
    high = jnp.broadcast_to((parts[2:3] + 1).astype(jnp.float32), (256, rows))
    low = jnp.broadcast_to(parts[3:4].astype(jnp.float32), (256, rows))
    marks = jnp.where(lane == rank, high, jnp.where(lane == rank + 128, low, 0.0)).astype(
        jnp.bfloat16
    )
    owner = onehot(iota((128, rows), 0) == dest)
    pos_rows = lax.dot_general(
        owner, marks, (((1,), (1,)), ((), ())), preferred_element_type=jnp.float32
    ).astype(jnp.bfloat16)
    lift = onehot(iota((outs, 128), 0) == iota((outs, 128), 1) * SLOT_ROWS + POS_ROW)
    data = data + jnp.dot(lift, pos_rows, preferred_element_type=jnp.float32)
    out_ref[...] = data.astype(jnp.bfloat16)


def unpack_kernel(in_ref, out_ref):
    ins = in_ref.shape[0]
    rows = out_ref.shape[0]
    data = in_ref[...]
    drop = onehot(iota((128, ins), 1) == iota((128, ins), 0) * SLOT_ROWS + POS_ROW)
    pos_rows = jnp.dot(drop, data, preferred_element_type=jnp.float32).astype(jnp.bfloat16)
    within = onehot(iota((128, ins), 0) == (iota((128, ins), 1) & (SLOT_ROWS - 1)))
    mine = (iota((128, ins), 1) >> 4) == iota((128, ins), 0)

    def lanes(part):
        spread = jnp.dot(part, within, preferred_element_type=jnp.float32)
        return jnp.sum(jnp.where(mine, spread, 0.0), axis=0, keepdims=True).astype(jnp.int32)

    high = lanes(pos_rows[:, :128])
    low = lanes(pos_rows[:, 128:])
    target = 4 * (high - 1) + 2 * low + (iota((1, ins), 1) & 1)
    pick = onehot(iota((rows, ins), 0) == target)
    out_ref[...] = jnp.dot(pick, data, preferred_element_type=jnp.float32).astype(jnp.bfloat16)


def ring_order(step):
    return jnp.where(step == 0, 0, jnp.where(step == 3, 1, jnp.where(step == 1, 2, 3)))


def plan_kernel(where_ref, count_ref, rows_ref, cols_ref, code_ref, start_ref):
    slots = rows_ref.shape[1]
    count = count_ref[0]
    x, core, z, y = where_ref[0], where_ref[1], where_ref[2], where_ref[3]
    row = rows_ref[...]
    col = cols_ref[...]
    source = col >> 3
    order_z = ring_order(((source >> 2) - z) & 3)
    order_y = ring_order(((source & 3) - y) & 3)
    outer = jnp.where(core == 0, order_z, order_y)
    inner = jnp.where(core == 0, order_y, order_z)
    stage = jnp.where(outer == 0, 0, jnp.where(inner < 2, 1, 2) + jnp.where(outer == 3, 2, 0))
    side = (inner & 1) * 8 + jnp.where(outer == 2, 16, 0)
    tile = jnp.where(outer == 0, inner * 8, side) + (col & 7)
    owner = row >> 3
    dx = ((owner >> 1) - x) & 3
    order_x = jnp.where(dx == 2, 0, jnp.where(dx == 1, 1, jnp.where(dx == 3, 2, 3)))
    own = (owner & 1) == core
    chunk = jnp.where(order_x == 0, jnp.where(own, 1, 0), jnp.where(own, 4, 1) + order_x)
    key = stage * 64 + chunk * 8 + (row & 7)
    slot = iota((1, slots), 1)
    key = jnp.where(slot < count, key, 511)
    code = ((chunk * 8 + (row & 7)) << 18) + (slot << 8) + tile + 1

    def column(v):
        return jnp.broadcast_to(v.astype(jnp.float32), (128, slots)).T

    key_row = key.astype(jnp.float32)
    key_col = column(key)[:, :1]
    code_col = column(code)[:, :1]
    same = (key_col == key_row) & (iota((slots, slots), 1) < iota((slots, slots), 0))
    rank = jnp.sum(jnp.where(same, 1.0, 0.0), axis=1, keepdims=True)
    bucket = iota((slots, LANES), 1).astype(jnp.float32)
    member = key_col == bucket
    cnt = jnp.sum(jnp.where(member, 1.0, 0.0), axis=0, keepdims=True).astype(jnp.int32)
    pairs = jnp.broadcast_to((cnt + 1) >> 1, (16, LANES)).astype(jnp.float32).astype(jnp.bfloat16)
    a, b = iota((LANES, LANES), 0), iota((LANES, LANES), 1)

    same_stage = (a >> 6) == (b >> 6)
    opens = ((a & 63) == 0) & ((a >> 6) < (b >> 6))
    inside = jnp.dot(pairs, onehot(same_stage & (a < b)), preferred_element_type=jnp.float32)
    total = jnp.dot(pairs, onehot(same_stage), preferred_element_type=jnp.float32)
    blocks = ((total.astype(jnp.int32) + (PAIRS - 1)) >> 3).astype(jnp.float32)
    blocks = blocks.astype(jnp.bfloat16)
    ahead = jnp.dot(
        blocks, onehot(opens), preferred_element_type=jnp.float32
    )
    begin = (ahead * BLOCK + inside * 2.0)[:1]
    base = jnp.sum(jnp.where(member, begin, 0.0), axis=1, keepdims=True)
    live = iota((slots, 1), 0) < count
    place = jnp.where(live, base + rank, -1.0)
    lists = code_ref.shape[1]
    hit = place == iota((slots, lists), 1).astype(jnp.float32)
    code_ref[...] = jnp.sum(jnp.where(hit, code_col, 0.0), axis=0, keepdims=True).astype(jnp.int32)
    start_ref[...] = ahead[:1].astype(jnp.int32)


def tiles_kernel(stage, n_pieces, outs, *refs):
    opening = stage == 0
    code_ref, start_ref, weights = refs[:3]
    pieces = refs[3 : 3 + n_pieces]
    k = 3 + n_pieces
    if not opening:
        k += 2
    acc, wbuf = refs[k : k + 2]
    out_refs = refs[k + 2 : k + 2 + len(outs)]
    panel, wsem, psem = refs[k + 2 + len(outs) :]
    first = start_ref[64 * stage]
    last = start_ref[64 * stage + 64]
    total = start_ref[64 * STAGES]
    ahead = BUFS - 1

    copies = []
    offset = 1
    for i, piece in enumerate(pieces):
        n = piece.shape[0]
        copies.append(pltpu.make_async_copy(piece, panel.at[pl.ds(offset, n)], psem.at[i]))
        offset += n
    for c in copies:
        c.start()
    panel[0] = jnp.zeros(panel.shape[1:], panel.dtype)

    def fetch(block):
        slot = lax.rem(block, BUFS)
        for i in range(BLOCK):
            s = (code_ref[block * BLOCK + i] >> 8) & 1023
            pltpu.make_async_copy(weights.at[s], wbuf.at[slot, i], wsem.at[slot]).start()

    def arrive(block):
        slot = lax.rem(block, BUFS)
        pltpu.make_async_copy(weights.at[pl.ds(0, BLOCK)], wbuf.at[slot], wsem.at[slot]).wait()

    if opening:
        for i in range(ahead):
            pl.when(first + i < total)(functools.partial(fetch, first + i))

        def clear(i, _):
            acc[i] = jnp.zeros(acc.shape[1:], acc.dtype)
            return 0

        lax.fori_loop(0, acc.shape[0], clear, 0)
    fetched = first if opening else first + ahead
    for c in copies:
        c.wait()

    def run_block(block, _):
        pl.when(block + ahead < total)(functools.partial(fetch, block + ahead))
        pl.when(block >= fetched)(functools.partial(arrive, block))
        slot = lax.rem(block, BUFS)
        for u in range(PAIRS):
            c0 = code_ref[block * BLOCK + 2 * u]
            c1 = code_ref[block * BLOCK + 2 * u + 1]
            w = jnp.concatenate([wbuf[slot, 2 * u], wbuf[slot, 2 * u + 1]], axis=1)
            f = jnp.concatenate([panel[c0 & 255], panel[c1 & 255]], axis=0)
            acc[c0 >> 18] += jnp.dot(w, f, preferred_element_type=jnp.float32)
        return 0

    lax.fori_loop(first, last, run_block, 0)
    for out, (lo, n) in zip(out_refs, outs):

        def give(i, _, out=out, lo=lo):
            out[i] = acc[lo + i].astype(out.dtype)
            return 0

        lax.fori_loop(0, n, give, 0)
    for i in range(ahead):
        pl.when((last + i < total) & (last + i >= fetched))(functools.partial(arrive, last + i))


def run_tiles(stage, code, start, weights, pieces, state=(), outs=()):
    any_spec = pl.BlockSpec(memory_space=pl.ANY)
    vmem = pl.BlockSpec(memory_space=pltpu.VMEM)
    smem = pl.BlockSpec(memory_space=pltpu.SMEM)
    t = weights.shape[1]
    pieces = [p.reshape(-1, t, p.shape[-1]) for p in pieces]
    n = len(pieces)
    tiles = sum(p.shape[0] for p in pieces) + 1
    f = pieces[0].shape[2]
    args = [code, start, weights, *pieces]
    in_specs = [smem, smem] + [any_spec] * (n + 1)
    aliases = {len(args) + i: i for i in range(len(state))}
    out_shape = [
        pltpu.VMEM((64, t, f), jnp.float32),
        pltpu.VMEM((BUFS, BLOCK, t, t), jnp.bfloat16),
    ] + [pltpu.VMEM((k, t, f), jnp.bfloat16) for _, k in outs]
    share = 352 * (tiles - 1) // 128
    return pl.pallas_call(
        functools.partial(tiles_kernel, stage, n, outs),
        out_shape=out_shape,
        in_specs=in_specs + [vmem] * len(state),
        out_specs=[vmem] * len(out_shape),
        scratch_shapes=[
            pltpu.VMEM((tiles, t, f), jnp.bfloat16),
            pltpu.SemaphoreType.DMA((BUFS,)),
            pltpu.SemaphoreType.DMA((n,)),
        ],
        input_output_aliases=aliases,
        compiler_params=pltpu.CompilerParams(vmem_limit_bytes=VMEM_TILES),
        cost_estimate=pl.CostEstimate(
            flops=share * 4 * t * t * f, bytes_accessed=share * 4 * t * t, transcendentals=0
        ),
        name=f"tiles_{stage}",
    )(*args, *state)


def panel_perm(turn, step):
    pairs = []
    for row in range(8):
        along_y = row % 2 == turn
        for z in range(4):
            for y in range(4):
                to = z * 4 + (y + step) % 4 if along_y else (z + step) % 4 * 4 + y
                pairs.append((row * 16 + z * 4 + y, row * 16 + to))
    return pairs


def row_perm(dx, flip=0):
    return [(x * 2 + c, (x + dx) % 4 * 2 + (c ^ flip)) for x in range(4) for c in range(2)]


def per_device(
    table, home, degree, tile_rows, tile_cols, tile_count, tile_values, w_self, w_neigh, bias
):
    rows, width = table.shape
    devices = lax.axis_size("row") * lax.axis_size("col")
    slots, tile = tile_values.shape[2:4]
    row_index = lax.axis_index("row")
    col_index = lax.axis_index("col")
    where = jnp.stack([row_index // 2, row_index % 2, col_index // 4, col_index % 4]).astype(
        jnp.int32
    )
    vmem = pl.BlockSpec(memory_space=pltpu.VMEM)
    smem = pl.BlockSpec(memory_space=pltpu.SMEM)
    big = pltpu.CompilerParams(vmem_limit_bytes=48 * MB)

    outgoing = pl.pallas_call(
        pack_kernel,
        out_shape=jax.ShapeDtypeStruct((devices * SLOT_ROWS, width), jnp.bfloat16),
        in_specs=[vmem, vmem],
        out_specs=vmem,
        compiler_params=big,
        name="pack",
    )(home.reshape(1, -1), table)
    incoming = lax.all_to_all(
        outgoing.reshape(devices, SLOT_ROWS, width),
        ("row", "col"),
        split_axis=0,
        concat_axis=0,
        tiled=True,
    )
    half = rows // 2
    owned = pl.pallas_call(
        unpack_kernel,
        out_shape=jax.ShapeDtypeStruct((rows, width), jnp.bfloat16),
        in_specs=[vmem],
        out_specs=vmem,
        compiler_params=big,
        name="unpack",
    )(incoming.reshape(devices * SLOT_ROWS, width))

    code, start = pl.pallas_call(
        plan_kernel,
        out_shape=(
            jax.ShapeDtypeStruct((1, LIST), jnp.int32),
            jax.ShapeDtypeStruct((1, LANES), jnp.int32),
        ),
        in_specs=[smem, smem, vmem, vmem],
        out_specs=(vmem, vmem),
        compiler_params=big,
        name="plan",
    )(where, tile_count.reshape(1), tile_rows.reshape(1, slots), tile_cols.reshape(1, slots))
    code = code.reshape(LIST)
    start = start.reshape(LANES)
    weights = tile_values.reshape(slots, tile, tile)

    def send(v, turn, step):
        return lax.ppermute(v, ("row", "col"), panel_perm(turn, step))

    def cat(*parts):
        return jnp.concatenate(parts, axis=0)

    plus, minus = send(owned, 0, 1), send(owned, 0, -1)
    plus, minus, code, start = lax.optimization_barrier((plus, minus, code, start))
    hi = cat(minus, send(plus[:half], 0, 1), send(minus[half:], 0, -1))
    lo = cat(owned, plus)
    lists = (code, start, weights)
    lo_p, lo_m = send(lo, 1, 1), send(lo, 1, -1)
    hi_p, hi_m = send(hi, 1, 1), send(hi, 1, -1)
    state = run_tiles(0, *lists, [lo, hi])
    lo_p, lo_m, *state = lax.optimization_barrier((lo_p, lo_m, *state))
    far_lo = [send(lo_p[:rows], 1, 1), send(lo_m[rows:], 1, -1)]
    state = run_tiles(1, *lists, [lo_p, lo_m], state)
    hi_p, hi_m, *state = lax.optimization_barrier((hi_p, hi_m, *state))
    far_hi = [send(hi_p[:rows], 1, 1), send(hi_m[rows:], 1, -1)]
    state = run_tiles(2, *lists, [hi_p, hi_m], state)
    state = run_tiles(3, *lists, far_lo, state)
    *_, other_far, mine_far, other_rest, mine_rest = run_tiles(
        4, *lists, far_hi, state, ((0, 8), (8, 8), (16, 24), (40, 24))
    )

    f32 = jnp.float32

    def over(v, dx, flip=0):
        return lax.ppermute(v, "row", row_perm(dx, flip))

    got_far = over(other_far.reshape(rows, width), 0, 1)
    across = (mine_far.reshape(rows, width).astype(f32) + got_far.astype(f32)).astype(jnp.bfloat16)
    across, other_rest = lax.optimization_barrier((across, other_rest))
    from_minus, from_plus = over(across[:half], 1), over(across[half:], -1)
    got_rest = over(other_rest.reshape(3, rows, width), 0, 1)
    mine_rest = mine_rest.reshape(3, rows, width)
    both = [mine_rest[i].astype(f32) + got_rest[i].astype(f32) for i in range(3)]
    to_plus = cat(both[0][:half] + from_minus.astype(f32), both[0][half:]).astype(jnp.bfloat16)
    to_minus = cat(both[1][:half], both[1][half:] + from_plus.astype(f32)).astype(jnp.bfloat16)
    summed = both[2] + over(to_plus, 1).astype(f32) + over(to_minus, -1).astype(f32)

    neighbor_mean = (summed / degree.astype(f32)[:, None]).astype(jnp.bfloat16)
    total = jnp.dot(owned, w_self, preferred_element_type=f32)
    total = total + jnp.dot(neighbor_mean, w_neigh, preferred_element_type=f32)
    total = total + bias.astype(f32)[None, :]
    return jnp.maximum(total, f32(0.0)).astype(jnp.bfloat16)


def solution(mesh):
    in_specs = (
        P(("row", "col"), None),
        P(("row", "col")),
        P(("row", "col")),
        P("row", "col", None),
        P("row", "col", None),
        P("row", "col"),
        P("row", "col", None, None, None),
        P(),
        P(),
        P(),
    )
    out_specs = P(("row", "col"), None)
    return jax.shard_map(
        per_device, mesh=mesh, in_specs=in_specs, out_specs=out_specs, check_vma=False
    )
```

```python
import functools

import jax
import jax.numpy as jnp
from jax import lax
from jax.experimental import pallas as pl
from jax.experimental.pallas import tpu as pltpu
from jax.sharding import PartitionSpec as P

SLOT_ROWS = 16
POS_ROW = 12
PAIRS = 8
BLOCK = 2 * PAIRS
BUFS = 8
LIST = 1024
STAGES = 4
LANES = 384
MB = 1 << 20
VMEM_TILES = 30 * MB


def iota(shape, dim):
    return lax.broadcasted_iota(jnp.int32, shape, dim)


def onehot(mask):
    return jnp.where(mask, 1.0, 0.0).astype(jnp.bfloat16)


def pack_kernel(home_ref, table_ref, out_ref):
    rows = table_ref.shape[0]
    blocks = home_ref.shape[1]
    home = home_ref[...]
    dest = home >> 9
    dest_f = dest.astype(jnp.float32)
    dest_col = jnp.broadcast_to(dest_f, (128, blocks)).T[:, :1]
    before = (dest_col == dest_f) & (iota((blocks, blocks), 0) < iota((blocks, blocks), 1))
    rank = jnp.sum(jnp.where(before, 1.0, 0.0), axis=0, keepdims=True).astype(jnp.int32)
    line = iota((16, blocks), 0)
    parts = jnp.where(line == 2, (home & 511) >> 1, home & 1)
    parts = jnp.where(line == 0, dest, jnp.where(line == 1, rank, parts))
    twice = onehot(iota((blocks, rows), 0) == (iota((blocks, rows), 1) >> 1))
    parts = jnp.dot(
        parts.astype(jnp.float32).astype(jnp.bfloat16), twice, preferred_element_type=jnp.float32
    ).astype(jnp.int32)
    dest = parts[:1]
    rank = parts[1:2] * 2 + (iota((1, rows), 1) & 1)
    place = dest * SLOT_ROWS + rank
    outs = out_ref.shape[0]
    spread = onehot(iota((outs, rows), 0) == place)
    data = jnp.dot(spread, table_ref[...], preferred_element_type=jnp.float32)
    lane = iota((256, rows), 0)
    high = jnp.broadcast_to((parts[2:3] + 1).astype(jnp.float32), (256, rows))
    low = jnp.broadcast_to(parts[3:4].astype(jnp.float32), (256, rows))
    marks = jnp.where(lane == rank, high, jnp.where(lane == rank + 128, low, 0.0)).astype(
        jnp.bfloat16
    )
    owner = onehot(iota((128, rows), 0) == dest)
    pos_rows = lax.dot_general(
        owner, marks, (((1,), (1,)), ((), ())), preferred_element_type=jnp.float32
    ).astype(jnp.bfloat16)
    lift = onehot(iota((outs, 128), 0) == iota((outs, 128), 1) * SLOT_ROWS + POS_ROW)
    data = data + jnp.dot(lift, pos_rows, preferred_element_type=jnp.float32)
    out_ref[...] = data.astype(jnp.bfloat16)


def unpack_kernel(in_ref, out_ref):
    ins = in_ref.shape[0]
    rows = out_ref.shape[0]
    data = in_ref[...]
    drop = onehot(iota((128, ins), 1) == iota((128, ins), 0) * SLOT_ROWS + POS_ROW)
    pos_rows = jnp.dot(drop, data, preferred_element_type=jnp.float32).astype(jnp.bfloat16)
    within = onehot(iota((128, ins), 0) == (iota((128, ins), 1) & (SLOT_ROWS - 1)))
    mine = (iota((128, ins), 1) >> 4) == iota((128, ins), 0)

    def lanes(part):
        spread = jnp.dot(part, within, preferred_element_type=jnp.float32)
        return jnp.sum(jnp.where(mine, spread, 0.0), axis=0, keepdims=True).astype(jnp.int32)

    high = lanes(pos_rows[:, :128])
    low = lanes(pos_rows[:, 128:])
    target = 4 * (high - 1) + 2 * low + (iota((1, ins), 1) & 1)
    pick = onehot(iota((rows, ins), 0) == target)
    out_ref[...] = jnp.dot(pick, data, preferred_element_type=jnp.float32).astype(jnp.bfloat16)


def ring_order(step):
    return jnp.where(step == 0, 0, jnp.where(step == 3, 1, jnp.where(step == 1, 2, 3)))


def plan_kernel(where_ref, count_ref, rows_ref, cols_ref, code_ref, start_ref):
    slots = rows_ref.shape[1]
    count = count_ref[0]
    x, core, z, y = where_ref[0], where_ref[1], where_ref[2], where_ref[3]
    row = rows_ref[...]
    col = cols_ref[...]
    source = col >> 3
    order_z = ring_order(((source >> 2) - z) & 3)
    order_y = ring_order(((source & 3) - y) & 3)
    outer = jnp.where(core == 0, order_z, order_y)
    inner = jnp.where(core == 0, order_y, order_z)
    stage = jnp.where(outer == 0, 0, jnp.where(inner < 2, 1, 2) + jnp.where(outer == 3, 1, 0))
    side = (inner & 1) * 8 + jnp.where(outer == 2, 16, jnp.where((outer == 3) & (inner < 2), 32, 0))
    tile = jnp.where(outer == 0, inner * 8, side) + (col & 7)
    owner = row >> 3
    dx = ((owner >> 1) - x) & 3
    order_x = jnp.where(dx == 2, 0, jnp.where(dx == 1, 1, jnp.where(dx == 3, 2, 3)))
    own = (owner & 1) == core
    chunk = jnp.where(order_x == 0, jnp.where(own, 1, 0), jnp.where(own, 4, 1) + order_x)
    key = stage * 64 + chunk * 8 + (row & 7)
    slot = iota((1, slots), 1)
    key = jnp.where(slot < count, key, 511)
    code = ((chunk * 8 + (row & 7)) << 18) + (slot << 8) + tile + 1

    def column(v):
        return jnp.broadcast_to(v.astype(jnp.float32), (128, slots)).T

    key_row = key.astype(jnp.float32)
    key_col = column(key)[:, :1]
    code_col = column(code)[:, :1]
    same = (key_col == key_row) & (iota((slots, slots), 1) < iota((slots, slots), 0))
    rank = jnp.sum(jnp.where(same, 1.0, 0.0), axis=1, keepdims=True)
    bucket = iota((slots, LANES), 1).astype(jnp.float32)
    member = key_col == bucket
    cnt = jnp.sum(jnp.where(member, 1.0, 0.0), axis=0, keepdims=True).astype(jnp.int32)
    pairs = jnp.broadcast_to((cnt + 1) >> 1, (16, LANES)).astype(jnp.float32).astype(jnp.bfloat16)
    a, b = iota((LANES, LANES), 0), iota((LANES, LANES), 1)

    same_stage = (a >> 6) == (b >> 6)
    opens = ((a & 63) == 0) & ((a >> 6) < (b >> 6))
    inside = jnp.dot(pairs, onehot(same_stage & (a < b)), preferred_element_type=jnp.float32)
    total = jnp.dot(pairs, onehot(same_stage), preferred_element_type=jnp.float32)
    blocks = ((total.astype(jnp.int32) + (PAIRS - 1)) >> 3).astype(jnp.float32)
    blocks = blocks.astype(jnp.bfloat16)
    ahead = jnp.dot(
        blocks, onehot(opens), preferred_element_type=jnp.float32
    )
    begin = (ahead * BLOCK + inside * 2.0)[:1]
    base = jnp.sum(jnp.where(member, begin, 0.0), axis=1, keepdims=True)
    live = iota((slots, 1), 0) < count
    place = jnp.where(live, base + rank, -1.0)
    lists = code_ref.shape[1]
    hit = place == iota((slots, lists), 1).astype(jnp.float32)
    code_ref[...] = jnp.sum(jnp.where(hit, code_col, 0.0), axis=0, keepdims=True).astype(jnp.int32)
    start_ref[...] = ahead[:1].astype(jnp.int32)


def fetch(block, code_ref, weights, wbuf, wsem):
    slot = lax.rem(block, BUFS)
    for i in range(BLOCK):
        s = (code_ref[block * BLOCK + i] >> 8) & 1023
        pltpu.make_async_copy(weights.at[s], wbuf.at[slot, i], wsem.at[slot]).start()


def arrive(block, weights, wbuf, wsem):
    slot = lax.rem(block, BUFS)
    pltpu.make_async_copy(weights.at[pl.ds(0, BLOCK)], wbuf.at[slot], wsem.at[slot]).wait()


def open_kernel(code_ref, start_ref, weights, acc, wbuf, wsem):
    total = start_ref[64 * STAGES]
    for i in range(BUFS - 1):
        pl.when(i < total)(functools.partial(fetch, i, code_ref, weights, wbuf, wsem))

    def clear(i, _):
        acc[i] = jnp.zeros(acc.shape[1:], acc.dtype)
        return 0

    lax.fori_loop(0, acc.shape[0], clear, 0)
    for i in range(BUFS - 1):
        pl.when(i < total)(functools.partial(arrive, i, weights, wbuf, wsem))


def tiles_kernel(stage, n_pieces, outs, *refs):
    code_ref, start_ref, weights = refs[:3]
    pieces = refs[3 : 3 + n_pieces]
    k = 5 + n_pieces
    acc, wbuf = refs[k : k + 2]
    out_refs = refs[k + 2 : k + 2 + len(outs)]
    panel, wsem, psem = refs[k + 2 + len(outs) :]
    first = start_ref[64 * stage]
    last = start_ref[64 * stage + 64]
    total = start_ref[64 * STAGES]
    ahead = BUFS - 1

    copies = []
    offset = 1
    for i, piece in enumerate(pieces):
        n = piece.shape[0]
        copies.append(pltpu.make_async_copy(piece, panel.at[pl.ds(offset, n)], psem.at[i]))
        offset += n
    for c in copies:
        c.start()
    panel[0] = jnp.zeros(panel.shape[1:], panel.dtype)
    fetched = first + ahead
    for c in copies:
        c.wait()

    def run_block(block, _):
        pl.when(block + ahead < total)(functools.partial(fetch, block + ahead, code_ref, weights, wbuf, wsem))
        pl.when(block >= fetched)(functools.partial(arrive, block, weights, wbuf, wsem))
        slot = lax.rem(block, BUFS)
        for u in range(PAIRS):
            c0 = code_ref[block * BLOCK + 2 * u]
            c1 = code_ref[block * BLOCK + 2 * u + 1]
            w = jnp.concatenate([wbuf[slot, 2 * u], wbuf[slot, 2 * u + 1]], axis=1)
            f = jnp.concatenate([panel[c0 & 255], panel[c1 & 255]], axis=0)
            acc[c0 >> 18] += jnp.dot(w, f, preferred_element_type=jnp.float32)
        return 0

    lax.fori_loop(first, last, run_block, 0)
    for out, (lo, n) in zip(out_refs, outs):

        def give(i, _, out=out, lo=lo):
            out[i] = acc[lo + i].astype(out.dtype)
            return 0

        lax.fori_loop(0, n, give, 0)
    for i in range(ahead):
        pl.when((last + i < total) & (last + i >= fetched))(
            functools.partial(arrive, last + i, weights, wbuf, wsem)
        )


def open_tiles(code, start, weights, width):
    vmem = pl.BlockSpec(memory_space=pltpu.VMEM)
    smem = pl.BlockSpec(memory_space=pltpu.SMEM)
    t = weights.shape[1]
    return pl.pallas_call(
        open_kernel,
        out_shape=[
            pltpu.VMEM((64, t, width), jnp.float32),
            pltpu.VMEM((BUFS, BLOCK, t, t), jnp.bfloat16),
        ],
        in_specs=[smem, smem, pl.BlockSpec(memory_space=pl.ANY)],
        out_specs=[vmem, vmem],
        scratch_shapes=[pltpu.SemaphoreType.DMA((BUFS,))],
        compiler_params=pltpu.CompilerParams(vmem_limit_bytes=VMEM_TILES),
        name="tiles_open",
    )(code, start, weights)


def run_tiles(stage, code, start, weights, pieces, state, outs=()):
    any_spec = pl.BlockSpec(memory_space=pl.ANY)
    vmem = pl.BlockSpec(memory_space=pltpu.VMEM)
    smem = pl.BlockSpec(memory_space=pltpu.SMEM)
    t = weights.shape[1]
    pieces = [p.reshape(-1, t, p.shape[-1]) for p in pieces]
    n = len(pieces)
    tiles = sum(p.shape[0] for p in pieces) + 1
    f = pieces[0].shape[2]
    args = [code, start, weights, *pieces]
    in_specs = [smem, smem] + [any_spec] * (n + 1)
    aliases = {len(args) + i: i for i in range(len(state))}
    out_shape = [
        pltpu.VMEM((64, t, f), jnp.float32),
        pltpu.VMEM((BUFS, BLOCK, t, t), jnp.bfloat16),
    ] + [pltpu.VMEM((k, t, f), jnp.bfloat16) for _, k in outs]
    share = 352 * (tiles - 1) // 128
    return pl.pallas_call(
        functools.partial(tiles_kernel, stage, n, outs),
        out_shape=out_shape,
        in_specs=in_specs + [vmem] * len(state),
        out_specs=[vmem] * len(out_shape),
        scratch_shapes=[
            pltpu.VMEM((tiles, t, f), jnp.bfloat16),
            pltpu.SemaphoreType.DMA((BUFS,)),
            pltpu.SemaphoreType.DMA((n,)),
        ],
        input_output_aliases=aliases,
        compiler_params=pltpu.CompilerParams(vmem_limit_bytes=VMEM_TILES),
        cost_estimate=pl.CostEstimate(
            flops=share * 4 * t * t * f, bytes_accessed=share * 4 * t * t, transcendentals=0
        ),
        name=f"tiles_{stage}",
    )(*args, *state)


def panel_perm(turn, step):
    pairs = []
    for row in range(8):
        along_y = row % 2 == turn
        for z in range(4):
            for y in range(4):
                to = z * 4 + (y + step) % 4 if along_y else (z + step) % 4 * 4 + y
                pairs.append((row * 16 + z * 4 + y, row * 16 + to))
    return pairs


def row_perm(dx, flip=0):
    return [(x * 2 + c, (x + dx) % 4 * 2 + (c ^ flip)) for x in range(4) for c in range(2)]


def per_device(
    table, home, degree, tile_rows, tile_cols, tile_count, tile_values, w_self, w_neigh, bias
):
    rows, width = table.shape
    devices = lax.axis_size("row") * lax.axis_size("col")
    slots, tile = tile_values.shape[2:4]
    row_index = lax.axis_index("row")
    col_index = lax.axis_index("col")
    where = jnp.stack([row_index // 2, row_index % 2, col_index // 4, col_index % 4]).astype(
        jnp.int32
    )
    vmem = pl.BlockSpec(memory_space=pltpu.VMEM)
    smem = pl.BlockSpec(memory_space=pltpu.SMEM)
    big = pltpu.CompilerParams(vmem_limit_bytes=48 * MB)

    outgoing = pl.pallas_call(
        pack_kernel,
        out_shape=jax.ShapeDtypeStruct((devices * SLOT_ROWS, width), jnp.bfloat16),
        in_specs=[vmem, vmem],
        out_specs=vmem,
        compiler_params=big,
        name="pack",
    )(home.reshape(1, -1), table)
    incoming = lax.all_to_all(
        outgoing.reshape(devices, SLOT_ROWS, width),
        ("row", "col"),
        split_axis=0,
        concat_axis=0,
        tiled=True,
    )
    half = rows // 2
    owned = pl.pallas_call(
        unpack_kernel,
        out_shape=jax.ShapeDtypeStruct((rows, width), jnp.bfloat16),
        in_specs=[vmem],
        out_specs=vmem,
        compiler_params=big,
        name="unpack",
    )(incoming.reshape(devices * SLOT_ROWS, width))

    code, start = pl.pallas_call(
        plan_kernel,
        out_shape=(
            jax.ShapeDtypeStruct((1, LIST), jnp.int32),
            jax.ShapeDtypeStruct((1, LANES), jnp.int32),
        ),
        in_specs=[smem, smem, vmem, vmem],
        out_specs=(vmem, vmem),
        compiler_params=big,
        name="plan",
    )(where, tile_count.reshape(1), tile_rows.reshape(1, slots), tile_cols.reshape(1, slots))
    code = code.reshape(LIST)
    start = start.reshape(LANES)
    weights = tile_values.reshape(slots, tile, tile)

    def send(v, turn, step):
        return lax.ppermute(v, ("row", "col"), panel_perm(turn, step))

    def cat(*parts):
        return jnp.concatenate(parts, axis=0)

    plus, minus = send(owned, 0, 1), send(owned, 0, -1)
    state = open_tiles(code, start, weights, width)
    plus, minus, code, start, *state = lax.optimization_barrier((plus, minus, code, start, *state))
    hi = cat(minus, send(plus[:half], 0, 1), send(minus[half:], 0, -1))
    lo = cat(owned, plus)
    lists = (code, start, weights)
    lo_p, lo_m = send(lo, 1, 1), send(lo, 1, -1)
    hi_p, hi_m = send(hi, 1, 1), send(hi, 1, -1)
    state = run_tiles(0, *lists, [lo, hi], state)
    lo_p, lo_m, *state = lax.optimization_barrier((lo_p, lo_m, *state))
    far_lo = [send(lo_p[:rows], 1, 1), send(lo_m[rows:], 1, -1)]
    state = run_tiles(1, *lists, [lo_p, lo_m], state)
    hi_p, hi_m, *state = lax.optimization_barrier((hi_p, hi_m, *state))
    far_hi = [send(hi_p[:rows], 1, 1), send(hi_m[rows:], 1, -1)]
    state = run_tiles(2, *lists, [hi_p, hi_m, *far_lo], state)
    *_, other_far, mine_far, other_rest, mine_rest = run_tiles(
        3, *lists, far_hi, state, ((0, 8), (8, 8), (16, 24), (40, 24))
    )

    f32 = jnp.float32

    def over(v, dx, flip=0):
        return lax.ppermute(v, "row", row_perm(dx, flip))

    got_far = over(other_far.reshape(rows, width), 0, 1)
    across = (mine_far.reshape(rows, width).astype(f32) + got_far.astype(f32)).astype(jnp.bfloat16)
    across, other_rest = lax.optimization_barrier((across, other_rest))
    from_minus, from_plus = over(across[:half], 1), over(across[half:], -1)
    got_rest = over(other_rest.reshape(3, rows, width), 0, 1)
    mine_rest = mine_rest.reshape(3, rows, width)
    both = [mine_rest[i].astype(f32) + got_rest[i].astype(f32) for i in range(3)]
    to_plus = cat(both[0][:half] + from_minus.astype(f32), both[0][half:]).astype(jnp.bfloat16)
    to_minus = cat(both[1][:half], both[1][half:] + from_plus.astype(f32)).astype(jnp.bfloat16)
    summed = both[2] + over(to_plus, 1).astype(f32) + over(to_minus, -1).astype(f32)

    neighbor_mean = (summed / degree.astype(f32)[:, None]).astype(jnp.bfloat16)
    total = jnp.dot(owned, w_self, preferred_element_type=f32)
    total = total + jnp.dot(neighbor_mean, w_neigh, preferred_element_type=f32)
    total = total + bias.astype(f32)[None, :]
    return jnp.maximum(total, f32(0.0)).astype(jnp.bfloat16)


def solution(mesh):
    in_specs = (
        P(("row", "col"), None),
        P(("row", "col")),
        P(("row", "col")),
        P("row", "col", None),
        P("row", "col", None),
        P("row", "col"),
        P("row", "col", None, None, None),
        P(),
        P(),
        P(),
    )
    out_specs = P(("row", "col"), None)
    return jax.shard_map(
        per_device, mesh=mesh, in_specs=in_specs, out_specs=out_specs, check_vma=False
    )
```

```python
import functools

import jax
import jax.numpy as jnp
from jax import lax
from jax.experimental import pallas as pl
from jax.experimental.pallas import tpu as pltpu
from jax.sharding import PartitionSpec as P

SLOT_ROWS = 16
POS_ROW = 12
PAIRS = 8
BLOCK = 2 * PAIRS
BUFS = 8
LIST = 1024
STAGES = 4
LANES = 384
MB = 1 << 20
VMEM_TILES = 30 * MB


def iota(shape, dim):
    return lax.broadcasted_iota(jnp.int32, shape, dim)


def onehot(mask):
    return jnp.where(mask, 1.0, 0.0).astype(jnp.bfloat16)


def pack_kernel(home_ref, table_ref, out_ref):
    rows = table_ref.shape[0]
    blocks = home_ref.shape[1]
    home = home_ref[...]
    dest = home >> 9
    dest_f = dest.astype(jnp.float32)
    dest_col = jnp.broadcast_to(dest_f, (128, blocks)).T[:, :1]
    before = (dest_col == dest_f) & (iota((blocks, blocks), 0) < iota((blocks, blocks), 1))
    rank = jnp.sum(jnp.where(before, 1.0, 0.0), axis=0, keepdims=True).astype(jnp.int32)
    line = iota((16, blocks), 0)
    parts = jnp.where(line == 2, (home & 511) >> 1, home & 1)
    parts = jnp.where(line == 0, dest, jnp.where(line == 1, rank, parts))
    twice = onehot(iota((blocks, rows), 0) == (iota((blocks, rows), 1) >> 1))
    parts = jnp.dot(
        parts.astype(jnp.float32).astype(jnp.bfloat16), twice, preferred_element_type=jnp.float32
    ).astype(jnp.int32)
    dest = parts[:1]
    rank = parts[1:2] * 2 + (iota((1, rows), 1) & 1)
    place = dest * SLOT_ROWS + rank
    outs = out_ref.shape[0]
    spread = onehot(iota((outs, rows), 0) == place)
    data = jnp.dot(spread, table_ref[...], preferred_element_type=jnp.float32)
    lane = iota((256, rows), 0)
    high = jnp.broadcast_to((parts[2:3] + 1).astype(jnp.float32), (256, rows))
    low = jnp.broadcast_to(parts[3:4].astype(jnp.float32), (256, rows))
    marks = jnp.where(lane == rank, high, jnp.where(lane == rank + 128, low, 0.0)).astype(
        jnp.bfloat16
    )
    owner = onehot(iota((128, rows), 0) == dest)
    pos_rows = lax.dot_general(
        owner, marks, (((1,), (1,)), ((), ())), preferred_element_type=jnp.float32
    ).astype(jnp.bfloat16)
    lift = onehot(iota((outs, 128), 0) == iota((outs, 128), 1) * SLOT_ROWS + POS_ROW)
    data = data + jnp.dot(lift, pos_rows, preferred_element_type=jnp.float32)
    out_ref[...] = data.astype(jnp.bfloat16)


def unpack_kernel(in_ref, out_ref):
    ins = in_ref.shape[0]
    rows = out_ref.shape[0]
    data = in_ref[...]
    drop = onehot(iota((128, ins), 1) == iota((128, ins), 0) * SLOT_ROWS + POS_ROW)
    pos_rows = jnp.dot(drop, data, preferred_element_type=jnp.float32).astype(jnp.bfloat16)
    within = onehot(iota((128, ins), 0) == (iota((128, ins), 1) & (SLOT_ROWS - 1)))
    mine = (iota((128, ins), 1) >> 4) == iota((128, ins), 0)

    def lanes(part):
        spread = jnp.dot(part, within, preferred_element_type=jnp.float32)
        return jnp.sum(jnp.where(mine, spread, 0.0), axis=0, keepdims=True).astype(jnp.int32)

    high = lanes(pos_rows[:, :128])
    low = lanes(pos_rows[:, 128:])
    target = 4 * (high - 1) + 2 * low + (iota((1, ins), 1) & 1)
    pick = onehot(iota((rows, ins), 0) == target)
    out_ref[...] = jnp.dot(pick, data, preferred_element_type=jnp.float32).astype(jnp.bfloat16)


def ring_order(step):
    return jnp.where(step == 0, 0, jnp.where(step == 3, 1, jnp.where(step == 1, 2, 3)))


def plan_kernel(where_ref, count_ref, rows_ref, cols_ref, code_ref, start_ref):
    slots = rows_ref.shape[1]
    count = count_ref[0]
    x, core, z, y = where_ref[0], where_ref[1], where_ref[2], where_ref[3]
    row = rows_ref[...]
    col = cols_ref[...]
    source = col >> 3
    order_z = ring_order(((source >> 2) - z) & 3)
    order_y = ring_order(((source & 3) - y) & 3)
    outer = jnp.where(core == 0, order_z, order_y)
    inner = jnp.where(core == 0, order_y, order_z)
    stage = jnp.where(outer == 0, 0, jnp.where(outer == 3, 3, jnp.where(inner < 2, 1, 2)))
    side = (inner & 1) * 8 + jnp.where(outer == 2, 16, 0)
    tile = jnp.where((outer == 0) | (outer == 3), inner * 8, side) + (col & 7)
    owner = row >> 3
    dx = ((owner >> 1) - x) & 3
    order_x = jnp.where(dx == 2, 0, jnp.where(dx == 1, 1, jnp.where(dx == 3, 2, 3)))
    own = (owner & 1) == core
    chunk = jnp.where(order_x == 0, jnp.where(own, 1, 0), jnp.where(own, 4, 1) + order_x)
    key = stage * 64 + chunk * 8 + (row & 7)
    slot = iota((1, slots), 1)
    key = jnp.where(slot < count, key, 511)
    code = ((chunk * 8 + (row & 7)) << 18) + (slot << 8) + tile + 1

    def column(v):
        return jnp.broadcast_to(v.astype(jnp.float32), (128, slots)).T

    key_row = key.astype(jnp.float32)
    key_col = column(key)[:, :1]
    code_col = column(code)[:, :1]
    same = (key_col == key_row) & (iota((slots, slots), 1) < iota((slots, slots), 0))
    rank = jnp.sum(jnp.where(same, 1.0, 0.0), axis=1, keepdims=True)
    bucket = iota((slots, LANES), 1).astype(jnp.float32)
    member = key_col == bucket
    cnt = jnp.sum(jnp.where(member, 1.0, 0.0), axis=0, keepdims=True).astype(jnp.int32)
    pairs = jnp.broadcast_to((cnt + 1) >> 1, (16, LANES)).astype(jnp.float32).astype(jnp.bfloat16)
    a, b = iota((LANES, LANES), 0), iota((LANES, LANES), 1)

    same_stage = (a >> 6) == (b >> 6)
    opens = ((a & 63) == 0) & ((a >> 6) < (b >> 6))
    inside = jnp.dot(pairs, onehot(same_stage & (a < b)), preferred_element_type=jnp.float32)
    total = jnp.dot(pairs, onehot(same_stage), preferred_element_type=jnp.float32)
    blocks = ((total.astype(jnp.int32) + (PAIRS - 1)) >> 3).astype(jnp.float32)
    blocks = blocks.astype(jnp.bfloat16)
    ahead = jnp.dot(
        blocks, onehot(opens), preferred_element_type=jnp.float32
    )
    begin = (ahead * BLOCK + inside * 2.0)[:1]
    base = jnp.sum(jnp.where(member, begin, 0.0), axis=1, keepdims=True)
    live = iota((slots, 1), 0) < count
    place = jnp.where(live, base + rank, -1.0)
    lists = code_ref.shape[1]
    hit = place == iota((slots, lists), 1).astype(jnp.float32)
    code_ref[...] = jnp.sum(jnp.where(hit, code_col, 0.0), axis=0, keepdims=True).astype(jnp.int32)
    start_ref[...] = ahead[:1].astype(jnp.int32)


def fetch(block, code_ref, weights, wbuf, wsem):
    slot = lax.rem(block, BUFS)
    for i in range(BLOCK):
        s = (code_ref[block * BLOCK + i] >> 8) & 1023
        pltpu.make_async_copy(weights.at[s], wbuf.at[slot, i], wsem.at[slot]).start()


def arrive(block, weights, wbuf, wsem):
    slot = lax.rem(block, BUFS)
    pltpu.make_async_copy(weights.at[pl.ds(0, BLOCK)], wbuf.at[slot], wsem.at[slot]).wait()


def open_kernel(code_ref, start_ref, weights, acc, wbuf, wsem):
    total = start_ref[64 * STAGES]
    for i in range(BUFS - 1):
        pl.when(i < total)(functools.partial(fetch, i, code_ref, weights, wbuf, wsem))

    def clear(i, _):
        acc[i] = jnp.zeros(acc.shape[1:], acc.dtype)
        return 0

    lax.fori_loop(0, acc.shape[0], clear, 0)
    for i in range(BUFS - 1):
        pl.when(i < total)(functools.partial(arrive, i, weights, wbuf, wsem))


def tiles_kernel(stage, n_pieces, outs, *refs):
    code_ref, start_ref, weights = refs[:3]
    pieces = refs[3 : 3 + n_pieces]
    k = 5 + n_pieces
    acc, wbuf = refs[k : k + 2]
    out_refs = refs[k + 2 : k + 2 + len(outs)]
    panel, wsem, psem = refs[k + 2 + len(outs) :]
    first = start_ref[64 * stage]
    last = start_ref[64 * stage + 64]
    total = start_ref[64 * STAGES]
    ahead = BUFS - 1

    copies = []
    offset = 1
    for i, piece in enumerate(pieces):
        n = piece.shape[0]
        copies.append(pltpu.make_async_copy(piece, panel.at[pl.ds(offset, n)], psem.at[i]))
        offset += n
    for c in copies:
        c.start()
    panel[0] = jnp.zeros(panel.shape[1:], panel.dtype)
    fetched = first + ahead
    for c in copies:
        c.wait()

    def run_block(block, _):
        pl.when(block + ahead < total)(functools.partial(fetch, block + ahead, code_ref, weights, wbuf, wsem))
        pl.when(block >= fetched)(functools.partial(arrive, block, weights, wbuf, wsem))
        slot = lax.rem(block, BUFS)
        for u in range(PAIRS):
            c0 = code_ref[block * BLOCK + 2 * u]
            c1 = code_ref[block * BLOCK + 2 * u + 1]
            w = jnp.concatenate([wbuf[slot, 2 * u], wbuf[slot, 2 * u + 1]], axis=1)
            f = jnp.concatenate([panel[c0 & 255], panel[c1 & 255]], axis=0)
            acc[c0 >> 18] += jnp.dot(w, f, preferred_element_type=jnp.float32)
        return 0

    lax.fori_loop(first, last, run_block, 0)
    for out, (lo, n) in zip(out_refs, outs):

        def give(i, _, out=out, lo=lo):
            out[i] = acc[lo + i].astype(out.dtype)
            return 0

        lax.fori_loop(0, n, give, 0)
    for i in range(ahead):
        pl.when((last + i < total) & (last + i >= fetched))(
            functools.partial(arrive, last + i, weights, wbuf, wsem)
        )


def open_tiles(code, start, weights, width):
    vmem = pl.BlockSpec(memory_space=pltpu.VMEM)
    smem = pl.BlockSpec(memory_space=pltpu.SMEM)
    t = weights.shape[1]
    return pl.pallas_call(
        open_kernel,
        out_shape=[
            pltpu.VMEM((64, t, width), jnp.float32),
            pltpu.VMEM((BUFS, BLOCK, t, t), jnp.bfloat16),
        ],
        in_specs=[smem, smem, pl.BlockSpec(memory_space=pl.ANY)],
        out_specs=[vmem, vmem],
        scratch_shapes=[pltpu.SemaphoreType.DMA((BUFS,))],
        compiler_params=pltpu.CompilerParams(vmem_limit_bytes=VMEM_TILES),
        name="tiles_open",
    )(code, start, weights)


def run_tiles(stage, code, start, weights, pieces, state, outs=()):
    any_spec = pl.BlockSpec(memory_space=pl.ANY)
    vmem = pl.BlockSpec(memory_space=pltpu.VMEM)
    smem = pl.BlockSpec(memory_space=pltpu.SMEM)
    t = weights.shape[1]
    pieces = [p.reshape(-1, t, p.shape[-1]) for p in pieces]
    n = len(pieces)
    tiles = sum(p.shape[0] for p in pieces) + 1
    f = pieces[0].shape[2]
    args = [code, start, weights, *pieces]
    in_specs = [smem, smem] + [any_spec] * (n + 1)
    aliases = {len(args) + i: i for i in range(len(state))}
    out_shape = [
        pltpu.VMEM((64, t, f), jnp.float32),
        pltpu.VMEM((BUFS, BLOCK, t, t), jnp.bfloat16),
    ] + [pltpu.VMEM((k, t, f), jnp.bfloat16) for _, k in outs]
    share = 352 * (tiles - 1) // 128
    return pl.pallas_call(
        functools.partial(tiles_kernel, stage, n, outs),
        out_shape=out_shape,
        in_specs=in_specs + [vmem] * len(state),
        out_specs=[vmem] * len(out_shape),
        scratch_shapes=[
            pltpu.VMEM((tiles, t, f), jnp.bfloat16),
            pltpu.SemaphoreType.DMA((BUFS,)),
            pltpu.SemaphoreType.DMA((n,)),
        ],
        input_output_aliases=aliases,
        compiler_params=pltpu.CompilerParams(vmem_limit_bytes=VMEM_TILES),
        cost_estimate=pl.CostEstimate(
            flops=share * 4 * t * t * f, bytes_accessed=share * 4 * t * t, transcendentals=0
        ),
        name=f"tiles_{stage}",
    )(*args, *state)


def panel_perm(turn, step):
    pairs = []
    for row in range(8):
        along_y = row % 2 == turn
        for z in range(4):
            for y in range(4):
                to = z * 4 + (y + step) % 4 if along_y else (z + step) % 4 * 4 + y
                pairs.append((row * 16 + z * 4 + y, row * 16 + to))
    return pairs


def row_perm(dx, flip=0):
    return [(x * 2 + c, (x + dx) % 4 * 2 + (c ^ flip)) for x in range(4) for c in range(2)]


def per_device(
    table, home, degree, tile_rows, tile_cols, tile_count, tile_values, w_self, w_neigh, bias
):
    rows, width = table.shape
    devices = lax.axis_size("row") * lax.axis_size("col")
    slots, tile = tile_values.shape[2:4]
    row_index = lax.axis_index("row")
    col_index = lax.axis_index("col")
    where = jnp.stack([row_index // 2, row_index % 2, col_index // 4, col_index % 4]).astype(
        jnp.int32
    )
    vmem = pl.BlockSpec(memory_space=pltpu.VMEM)
    smem = pl.BlockSpec(memory_space=pltpu.SMEM)
    big = pltpu.CompilerParams(vmem_limit_bytes=48 * MB)

    outgoing = pl.pallas_call(
        pack_kernel,
        out_shape=jax.ShapeDtypeStruct((devices * SLOT_ROWS, width), jnp.bfloat16),
        in_specs=[vmem, vmem],
        out_specs=vmem,
        compiler_params=big,
        name="pack",
    )(home.reshape(1, -1), table)
    incoming = lax.all_to_all(
        outgoing.reshape(devices, SLOT_ROWS, width),
        ("row", "col"),
        split_axis=0,
        concat_axis=0,
        tiled=True,
    )
    half = rows // 2
    owned = pl.pallas_call(
        unpack_kernel,
        out_shape=jax.ShapeDtypeStruct((rows, width), jnp.bfloat16),
        in_specs=[vmem],
        out_specs=vmem,
        compiler_params=big,
        name="unpack",
    )(incoming.reshape(devices * SLOT_ROWS, width))

    code, start = pl.pallas_call(
        plan_kernel,
        out_shape=(
            jax.ShapeDtypeStruct((1, LIST), jnp.int32),
            jax.ShapeDtypeStruct((1, LANES), jnp.int32),
        ),
        in_specs=[smem, smem, vmem, vmem],
        out_specs=(vmem, vmem),
        compiler_params=big,
        name="plan",
    )(where, tile_count.reshape(1), tile_rows.reshape(1, slots), tile_cols.reshape(1, slots))
    code = code.reshape(LIST)
    start = start.reshape(LANES)
    weights = tile_values.reshape(slots, tile, tile)

    def send(v, turn, step):
        return lax.ppermute(v, ("row", "col"), panel_perm(turn, step))

    def cat(*parts):
        return jnp.concatenate(parts, axis=0)

    plus, minus = send(owned, 0, 1), send(owned, 0, -1)
    state = open_tiles(code, start, weights, width)
    plus, minus, code, start, *state = lax.optimization_barrier((plus, minus, code, start, *state))
    hi = cat(minus, send(plus[:half], 0, 1), send(minus[half:], 0, -1))
    lo = cat(owned, plus)
    lists = (code, start, weights)
    lo_p, lo_m = send(lo, 1, 1), send(lo, 1, -1)
    hi_p, hi_m = send(hi, 1, 1), send(hi, 1, -1)
    state = run_tiles(0, *lists, [lo, hi], state)
    lo_p, lo_m, *state = lax.optimization_barrier((lo_p, lo_m, *state))
    far_lo = [send(lo_p[:rows], 1, 1), send(lo_m[rows:], 1, -1)]
    state = run_tiles(1, *lists, [lo_p, lo_m], state)
    hi_p, hi_m, *state = lax.optimization_barrier((hi_p, hi_m, *state))
    far_hi = [send(hi_p[:rows], 1, 1), send(hi_m[rows:], 1, -1)]
    state = run_tiles(2, *lists, [hi_p, hi_m], state)
    *_, other_far, mine_far, other_rest, mine_rest = run_tiles(
        3, *lists, far_lo + far_hi, state, ((0, 8), (8, 8), (16, 24), (40, 24))
    )

    f32 = jnp.float32

    def over(v, dx, flip=0):
        return lax.ppermute(v, "row", row_perm(dx, flip))

    got_far = over(other_far.reshape(rows, width), 0, 1)
    across = (mine_far.reshape(rows, width).astype(f32) + got_far.astype(f32)).astype(jnp.bfloat16)
    across, other_rest = lax.optimization_barrier((across, other_rest))
    from_minus, from_plus = over(across[:half], 1), over(across[half:], -1)
    got_rest = over(other_rest.reshape(3, rows, width), 0, 1)
    mine_rest = mine_rest.reshape(3, rows, width)
    both = [mine_rest[i].astype(f32) + got_rest[i].astype(f32) for i in range(3)]
    low = over(both[0][half:].astype(jnp.bfloat16), 1)
    high = over(both[1][:half].astype(jnp.bfloat16), -1)
    to_plus = (both[0][:half] + from_minus.astype(f32)).astype(jnp.bfloat16)
    to_minus = (both[1][half:] + from_plus.astype(f32)).astype(jnp.bfloat16)
    top = both[2][:half] + high.astype(f32)
    bottom = both[2][half:] + low.astype(f32)
    top, bottom = lax.optimization_barrier((top, bottom))
    last_top, last_bottom = over(to_plus, 1), over(to_minus, -1)
    summed = cat(top + last_top.astype(f32), bottom + last_bottom.astype(f32))

    neighbor_mean = (summed / degree.astype(f32)[:, None]).astype(jnp.bfloat16)
    total = jnp.dot(owned, w_self, preferred_element_type=f32)
    total = total + jnp.dot(neighbor_mean, w_neigh, preferred_element_type=f32)
    total = total + bias.astype(f32)[None, :]
    return jnp.maximum(total, f32(0.0)).astype(jnp.bfloat16)


def solution(mesh):
    in_specs = (
        P(("row", "col"), None),
        P(("row", "col")),
        P(("row", "col")),
        P("row", "col", None),
        P("row", "col", None),
        P("row", "col"),
        P("row", "col", None, None, None),
        P(),
        P(),
        P(),
    )
    out_specs = P(("row", "col"), None)
    return jax.shard_map(
        per_device, mesh=mesh, in_specs=in_specs, out_specs=out_specs, check_vma=False
    )
```

```python
import functools

import jax
import jax.numpy as jnp
from jax import lax
from jax.experimental import pallas as pl
from jax.experimental.pallas import tpu as pltpu
from jax.sharding import PartitionSpec as P

SLOT_ROWS = 16
POS_ROW = 12
PAIRS = 8
BLOCK = 2 * PAIRS
BUFS = 8
LIST = 1024
STAGES = 4
LANES = 384
MB = 1 << 20
VMEM_TILES = 30 * MB


def iota(shape, dim):
    return lax.broadcasted_iota(jnp.int32, shape, dim)


def onehot(mask):
    return jnp.where(mask, 1.0, 0.0).astype(jnp.bfloat16)


def pack_kernel(home_hbm, table_hbm, out_ref, home_ref, table_ref, sem):
    home_copy = pltpu.make_async_copy(home_hbm, home_ref, sem.at[0])
    table_copy = pltpu.make_async_copy(table_hbm, table_ref, sem.at[1])
    home_copy.start()
    table_copy.start()
    home_copy.wait()
    rows = table_ref.shape[0]
    blocks = home_ref.shape[1]
    home = home_ref[...]
    dest = home >> 9
    dest_f = dest.astype(jnp.float32)
    dest_col = jnp.broadcast_to(dest_f, (128, blocks)).T[:, :1]
    before = (dest_col == dest_f) & (iota((blocks, blocks), 0) < iota((blocks, blocks), 1))
    rank = jnp.sum(jnp.where(before, 1.0, 0.0), axis=0, keepdims=True).astype(jnp.int32)
    line = iota((16, blocks), 0)
    parts = jnp.where(line == 2, (home & 511) >> 1, home & 1)
    parts = jnp.where(line == 0, dest, jnp.where(line == 1, rank, parts))
    twice = onehot(iota((blocks, rows), 0) == (iota((blocks, rows), 1) >> 1))
    parts = jnp.dot(
        parts.astype(jnp.float32).astype(jnp.bfloat16), twice, preferred_element_type=jnp.float32
    ).astype(jnp.int32)
    dest = parts[:1]
    rank = parts[1:2] * 2 + (iota((1, rows), 1) & 1)
    place = dest * SLOT_ROWS + rank
    outs = out_ref.shape[0]
    spread = onehot(iota((outs, rows), 0) == place)
    table_copy.wait()
    data = jnp.dot(spread, table_ref[...], preferred_element_type=jnp.float32)
    lane = iota((256, rows), 0)
    high = jnp.broadcast_to((parts[2:3] + 1).astype(jnp.float32), (256, rows))
    low = jnp.broadcast_to(parts[3:4].astype(jnp.float32), (256, rows))
    marks = jnp.where(lane == rank, high, jnp.where(lane == rank + 128, low, 0.0)).astype(
        jnp.bfloat16
    )
    owner = onehot(iota((128, rows), 0) == dest)
    pos_rows = lax.dot_general(
        owner, marks, (((1,), (1,)), ((), ())), preferred_element_type=jnp.float32
    ).astype(jnp.bfloat16)
    lift = onehot(iota((outs, 128), 0) == iota((outs, 128), 1) * SLOT_ROWS + POS_ROW)
    data = data + jnp.dot(lift, pos_rows, preferred_element_type=jnp.float32)
    out_ref[...] = data.astype(jnp.bfloat16)


def unpack_kernel(in_ref, out_ref):
    ins = in_ref.shape[0]
    rows = out_ref.shape[0]
    data = in_ref[...]
    drop = onehot(iota((128, ins), 1) == iota((128, ins), 0) * SLOT_ROWS + POS_ROW)
    pos_rows = jnp.dot(drop, data, preferred_element_type=jnp.float32).astype(jnp.bfloat16)
    within = onehot(iota((128, ins), 0) == (iota((128, ins), 1) & (SLOT_ROWS - 1)))
    mine = (iota((128, ins), 1) >> 4) == iota((128, ins), 0)

    def lanes(part):
        spread = jnp.dot(part, within, preferred_element_type=jnp.float32)
        return jnp.sum(jnp.where(mine, spread, 0.0), axis=0, keepdims=True).astype(jnp.int32)

    high = lanes(pos_rows[:, :128])
    low = lanes(pos_rows[:, 128:])
    target = 4 * (high - 1) + 2 * low + (iota((1, ins), 1) & 1)
    pick = onehot(iota((rows, ins), 0) == target)
    out_ref[...] = jnp.dot(pick, data, preferred_element_type=jnp.float32).astype(jnp.bfloat16)


def ring_order(step):
    return jnp.where(step == 0, 0, jnp.where(step == 3, 1, jnp.where(step == 1, 2, 3)))


def plan_kernel(where_ref, count_ref, rows_ref, cols_ref, code_ref, start_ref):
    slots = rows_ref.shape[1]
    count = count_ref[0]
    x, core, z, y = where_ref[0], where_ref[1], where_ref[2], where_ref[3]
    row = rows_ref[...]
    col = cols_ref[...]
    source = col >> 3
    order_z = ring_order(((source >> 2) - z) & 3)
    order_y = ring_order(((source & 3) - y) & 3)
    outer = jnp.where(core == 0, order_z, order_y)
    inner = jnp.where(core == 0, order_y, order_z)
    stage = jnp.where(outer == 0, 0, jnp.where(outer == 3, 3, jnp.where(inner < 2, 1, 2)))
    side = (inner & 1) * 8 + jnp.where(outer == 2, 16, 0)
    tile = jnp.where((outer == 0) | (outer == 3), inner * 8, side) + (col & 7)
    owner = row >> 3
    dx = ((owner >> 1) - x) & 3
    order_x = jnp.where(dx == 2, 0, jnp.where(dx == 1, 1, jnp.where(dx == 3, 2, 3)))
    own = (owner & 1) == core
    chunk = jnp.where(order_x == 0, jnp.where(own, 1, 0), jnp.where(own, 4, 1) + order_x)
    key = stage * 64 + chunk * 8 + (row & 7)
    slot = iota((1, slots), 1)
    key = jnp.where(slot < count, key, 511)
    code = ((chunk * 8 + (row & 7)) << 18) + (slot << 8) + tile + 1

    def column(v):
        return jnp.broadcast_to(v.astype(jnp.float32), (128, slots)).T

    key_row = key.astype(jnp.float32)
    key_col = column(key)[:, :1]
    code_col = column(code)[:, :1]
    same = (key_col == key_row) & (iota((slots, slots), 1) < iota((slots, slots), 0))
    rank = jnp.sum(jnp.where(same, 1.0, 0.0), axis=1, keepdims=True)
    bucket = iota((slots, LANES), 1).astype(jnp.float32)
    member = key_col == bucket
    cnt = jnp.sum(jnp.where(member, 1.0, 0.0), axis=0, keepdims=True).astype(jnp.int32)
    pairs = jnp.broadcast_to((cnt + 1) >> 1, (16, LANES)).astype(jnp.float32).astype(jnp.bfloat16)
    a, b = iota((LANES, LANES), 0), iota((LANES, LANES), 1)

    same_stage = (a >> 6) == (b >> 6)
    opens = ((a & 63) == 0) & ((a >> 6) < (b >> 6))
    inside = jnp.dot(pairs, onehot(same_stage & (a < b)), preferred_element_type=jnp.float32)
    total = jnp.dot(pairs, onehot(same_stage), preferred_element_type=jnp.float32)
    blocks = ((total.astype(jnp.int32) + (PAIRS - 1)) >> 3).astype(jnp.float32)
    blocks = blocks.astype(jnp.bfloat16)
    ahead = jnp.dot(
        blocks, onehot(opens), preferred_element_type=jnp.float32
    )
    begin = (ahead * BLOCK + inside * 2.0)[:1]
    base = jnp.sum(jnp.where(member, begin, 0.0), axis=1, keepdims=True)
    live = iota((slots, 1), 0) < count
    place = jnp.where(live, base + rank, -1.0)
    lists = code_ref.shape[1]
    hit = place == iota((slots, lists), 1).astype(jnp.float32)
    code_ref[...] = jnp.sum(jnp.where(hit, code_col, 0.0), axis=0, keepdims=True).astype(jnp.int32)
    start_ref[...] = ahead[:1].astype(jnp.int32)


def fetch(block, code_ref, weights, wbuf, wsem):
    slot = lax.rem(block, BUFS)
    for i in range(BLOCK):
        s = (code_ref[block * BLOCK + i] >> 8) & 1023
        pltpu.make_async_copy(weights.at[s], wbuf.at[slot, i], wsem.at[slot]).start()


def arrive(block, weights, wbuf, wsem):
    slot = lax.rem(block, BUFS)
    pltpu.make_async_copy(weights.at[pl.ds(0, BLOCK)], wbuf.at[slot], wsem.at[slot]).wait()


def open_kernel(code_ref, start_ref, weights, acc, wbuf, wsem):
    total = start_ref[64 * STAGES]
    for i in range(BUFS - 1):
        pl.when(i < total)(functools.partial(fetch, i, code_ref, weights, wbuf, wsem))

    def clear(i, _):
        acc[i] = jnp.zeros(acc.shape[1:], acc.dtype)
        return 0

    lax.fori_loop(0, acc.shape[0], clear, 0)
    for i in range(BUFS - 1):
        pl.when(i < total)(functools.partial(arrive, i, weights, wbuf, wsem))


def tiles_kernel(stage, n_pieces, outs, *refs):
    code_ref, start_ref, weights = refs[:3]
    pieces = refs[3 : 3 + n_pieces]
    k = 5 + n_pieces
    acc, wbuf = refs[k : k + 2]
    out_refs = refs[k + 2 : k + 2 + len(outs)]
    panel, wsem, psem = refs[k + 2 + len(outs) :]
    first = start_ref[64 * stage]
    last = start_ref[64 * stage + 64]
    total = start_ref[64 * STAGES]
    ahead = BUFS - 1

    copies = []
    offset = 1
    for i, piece in enumerate(pieces):
        n = piece.shape[0]
        copies.append(pltpu.make_async_copy(piece, panel.at[pl.ds(offset, n)], psem.at[i]))
        offset += n
    for c in copies:
        c.start()
    panel[0] = jnp.zeros(panel.shape[1:], panel.dtype)
    fetched = first + ahead
    for c in copies:
        c.wait()

    def run_block(block, _):
        pl.when(block + ahead < total)(functools.partial(fetch, block + ahead, code_ref, weights, wbuf, wsem))
        pl.when(block >= fetched)(functools.partial(arrive, block, weights, wbuf, wsem))
        slot = lax.rem(block, BUFS)
        for u in range(PAIRS):
            c0 = code_ref[block * BLOCK + 2 * u]
            c1 = code_ref[block * BLOCK + 2 * u + 1]
            w = jnp.concatenate([wbuf[slot, 2 * u], wbuf[slot, 2 * u + 1]], axis=1)
            f = jnp.concatenate([panel[c0 & 255], panel[c1 & 255]], axis=0)
            acc[c0 >> 18] += jnp.dot(w, f, preferred_element_type=jnp.float32)
        return 0

    lax.fori_loop(first, last, run_block, 0)
    for out, (lo, n) in zip(out_refs, outs):

        def give(i, _, out=out, lo=lo):
            out[i] = acc[lo + i].astype(out.dtype)
            return 0

        lax.fori_loop(0, n, give, 0)
    for i in range(ahead):
        pl.when((last + i < total) & (last + i >= fetched))(
            functools.partial(arrive, last + i, weights, wbuf, wsem)
        )


def round_kernel(outs, acc, *out_refs):
    for out, (lo, n) in zip(out_refs, outs):

        def give(i, _, out=out, lo=lo):
            out[i] = acc[lo + i].astype(out.dtype)
            return 0

        lax.fori_loop(0, n, give, 0)


def round_rows(acc, outs):
    vmem = pl.BlockSpec(memory_space=pltpu.VMEM)
    return pl.pallas_call(
        functools.partial(round_kernel, outs),
        out_shape=[pltpu.VMEM((n, *acc.shape[1:]), jnp.bfloat16) for _, n in outs],
        in_specs=[vmem],
        out_specs=[vmem] * len(outs),
        compiler_params=pltpu.CompilerParams(vmem_limit_bytes=VMEM_TILES),
        cost_estimate=pl.CostEstimate(flops=1 << 22, bytes_accessed=12 * MB, transcendentals=0),
        name="round_rows",
    )(acc)


def open_tiles(code, start, weights, width):
    vmem = pl.BlockSpec(memory_space=pltpu.VMEM)
    smem = pl.BlockSpec(memory_space=pltpu.SMEM)
    t = weights.shape[1]
    return pl.pallas_call(
        open_kernel,
        out_shape=[
            pltpu.VMEM((64, t, width), jnp.float32),
            pltpu.VMEM((BUFS, BLOCK, t, t), jnp.bfloat16),
        ],
        in_specs=[smem, smem, pl.BlockSpec(memory_space=pl.ANY)],
        out_specs=[vmem, vmem],
        scratch_shapes=[pltpu.SemaphoreType.DMA((BUFS,))],
        compiler_params=pltpu.CompilerParams(vmem_limit_bytes=VMEM_TILES),
        name="tiles_open",
    )(code, start, weights)


def run_tiles(stage, code, start, weights, pieces, state, outs=()):
    any_spec = pl.BlockSpec(memory_space=pl.ANY)
    vmem = pl.BlockSpec(memory_space=pltpu.VMEM)
    smem = pl.BlockSpec(memory_space=pltpu.SMEM)
    t = weights.shape[1]
    pieces = [p.reshape(-1, t, p.shape[-1]) for p in pieces]
    n = len(pieces)
    tiles = sum(p.shape[0] for p in pieces) + 1
    f = pieces[0].shape[2]
    args = [code, start, weights, *pieces]
    in_specs = [smem, smem] + [any_spec] * (n + 1)
    aliases = {len(args) + i: i for i in range(len(state))}
    out_shape = [
        pltpu.VMEM((64, t, f), jnp.float32),
        pltpu.VMEM((BUFS, BLOCK, t, t), jnp.bfloat16),
    ] + [pltpu.VMEM((k, t, f), jnp.bfloat16) for _, k in outs]
    share = 352 * (tiles - 1) // 128
    return pl.pallas_call(
        functools.partial(tiles_kernel, stage, n, outs),
        out_shape=out_shape,
        in_specs=in_specs + [vmem] * len(state),
        out_specs=[vmem] * len(out_shape),
        scratch_shapes=[
            pltpu.VMEM((tiles, t, f), jnp.bfloat16),
            pltpu.SemaphoreType.DMA((BUFS,)),
            pltpu.SemaphoreType.DMA((n,)),
        ],
        input_output_aliases=aliases,
        compiler_params=pltpu.CompilerParams(vmem_limit_bytes=VMEM_TILES),
        cost_estimate=pl.CostEstimate(
            flops=share * 4 * t * t * f, bytes_accessed=share * 4 * t * t, transcendentals=0
        ),
        name=f"tiles_{stage}",
    )(*args, *state)


def panel_perm(turn, step):
    pairs = []
    for row in range(8):
        along_y = row % 2 == turn
        for z in range(4):
            for y in range(4):
                to = z * 4 + (y + step) % 4 if along_y else (z + step) % 4 * 4 + y
                pairs.append((row * 16 + z * 4 + y, row * 16 + to))
    return pairs


def row_perm(dx, flip=0):
    return [(x * 2 + c, (x + dx) % 4 * 2 + (c ^ flip)) for x in range(4) for c in range(2)]


def per_device(
    table, home, degree, tile_rows, tile_cols, tile_count, tile_values, w_self, w_neigh, bias
):
    rows, width = table.shape
    devices = lax.axis_size("row") * lax.axis_size("col")
    slots, tile = tile_values.shape[2:4]
    row_index = lax.axis_index("row")
    col_index = lax.axis_index("col")
    where = jnp.stack([row_index // 2, row_index % 2, col_index // 4, col_index % 4]).astype(
        jnp.int32
    )
    vmem = pl.BlockSpec(memory_space=pltpu.VMEM)
    smem = pl.BlockSpec(memory_space=pltpu.SMEM)
    big = pltpu.CompilerParams(vmem_limit_bytes=48 * MB)

    outgoing = pl.pallas_call(
        pack_kernel,
        out_shape=jax.ShapeDtypeStruct((devices * SLOT_ROWS, width), jnp.bfloat16),
        in_specs=[pl.BlockSpec(memory_space=pl.ANY)] * 2,
        out_specs=vmem,
        scratch_shapes=[
            pltpu.VMEM((1, home.shape[0]), jnp.int32),
            pltpu.VMEM(table.shape, jnp.bfloat16),
            pltpu.SemaphoreType.DMA((2,)),
        ],
        compiler_params=pltpu.CompilerParams(vmem_limit_bytes=60 * MB),
        name="pack",
    )(home.reshape(1, -1), table)
    incoming = lax.all_to_all(
        outgoing.reshape(devices, SLOT_ROWS, width),
        ("row", "col"),
        split_axis=0,
        concat_axis=0,
        tiled=True,
    )
    half = rows // 2
    owned = pl.pallas_call(
        unpack_kernel,
        out_shape=jax.ShapeDtypeStruct((rows, width), jnp.bfloat16),
        in_specs=[vmem],
        out_specs=vmem,
        compiler_params=big,
        name="unpack",
    )(incoming.reshape(devices * SLOT_ROWS, width))

    code, start = pl.pallas_call(
        plan_kernel,
        out_shape=(
            jax.ShapeDtypeStruct((1, LIST), jnp.int32),
            jax.ShapeDtypeStruct((1, LANES), jnp.int32),
        ),
        in_specs=[smem, smem, vmem, vmem],
        out_specs=(vmem, vmem),
        compiler_params=big,
        name="plan",
    )(where, tile_count.reshape(1), tile_rows.reshape(1, slots), tile_cols.reshape(1, slots))
    code = code.reshape(LIST)
    start = start.reshape(LANES)
    weights = tile_values.reshape(slots, tile, tile)

    def send(v, turn, step):
        return lax.ppermute(v, ("row", "col"), panel_perm(turn, step))

    def cat(*parts):
        return jnp.concatenate(parts, axis=0)

    plus, minus = send(owned, 0, 1), send(owned, 0, -1)
    state = open_tiles(code, start, weights, width)
    plus, minus, code, start, *state = lax.optimization_barrier((plus, minus, code, start, *state))
    hi = cat(minus, send(plus[:half], 0, 1), send(minus[half:], 0, -1))
    lo = cat(owned, plus)
    lists = (code, start, weights)
    lo_p, lo_m = send(lo, 1, 1), send(lo, 1, -1)
    hi_p, hi_m = send(hi, 1, 1), send(hi, 1, -1)
    state = run_tiles(0, *lists, [lo, hi], state)
    lo_p, lo_m, *state = lax.optimization_barrier((lo_p, lo_m, *state))
    far_lo = [send(lo_p[:rows], 1, 1), send(lo_m[rows:], 1, -1)]
    state = run_tiles(1, *lists, [lo_p, lo_m], state)
    hi_p, hi_m, *state = lax.optimization_barrier((hi_p, hi_m, *state))
    far_hi = [send(hi_p[:rows], 1, 1), send(hi_m[rows:], 1, -1)]
    state = run_tiles(2, *lists, [hi_p, hi_m], state)
    sums, _, other_far, mine_far = run_tiles(
        3, *lists, far_lo + far_hi, state, ((0, 8), (8, 8))
    )
    other_rest, mine_rest = round_rows(sums, ((16, 24), (40, 24)))

    f32 = jnp.float32

    def over(v, dx, flip=0):
        return lax.ppermute(v, "row", row_perm(dx, flip))

    got_far = over(other_far.reshape(rows, width), 0, 1)
    across = (mine_far.reshape(rows, width).astype(f32) + got_far.astype(f32)).astype(jnp.bfloat16)
    across, other_rest = lax.optimization_barrier((across, other_rest))
    from_minus, from_plus = over(across[:half], 1), over(across[half:], -1)
    got_rest = over(other_rest.reshape(3, rows, width), 0, 1)
    mine_rest = mine_rest.reshape(3, rows, width)
    both = [mine_rest[i].astype(f32) + got_rest[i].astype(f32) for i in range(3)]
    low = over(both[0][half:].astype(jnp.bfloat16), 1)
    high = over(both[1][:half].astype(jnp.bfloat16), -1)
    to_plus = (both[0][:half] + from_minus.astype(f32)).astype(jnp.bfloat16)
    to_minus = (both[1][half:] + from_plus.astype(f32)).astype(jnp.bfloat16)
    top = both[2][:half] + high.astype(f32)
    bottom = both[2][half:] + low.astype(f32)
    top, bottom = lax.optimization_barrier((top, bottom))
    last_top, last_bottom = over(to_plus, 1), over(to_minus, -1)
    summed = cat(top + last_top.astype(f32), bottom + last_bottom.astype(f32))

    neighbor_mean = (summed / degree.astype(f32)[:, None]).astype(jnp.bfloat16)
    total = jnp.dot(owned, w_self, preferred_element_type=f32)
    total = total + jnp.dot(neighbor_mean, w_neigh, preferred_element_type=f32)
    total = total + bias.astype(f32)[None, :]
    return jnp.maximum(total, f32(0.0)).astype(jnp.bfloat16)


def solution(mesh):
    in_specs = (
        P(("row", "col"), None),
        P(("row", "col")),
        P(("row", "col")),
        P("row", "col", None),
        P("row", "col", None),
        P("row", "col"),
        P("row", "col", None, None, None),
        P(),
        P(),
        P(),
    )
    out_specs = P(("row", "col"), None)
    return jax.shard_map(
        per_device, mesh=mesh, in_specs=in_specs, out_specs=out_specs, check_vma=False
    )
```

```python
import functools

import jax
import jax.numpy as jnp
from jax import lax
from jax.experimental import pallas as pl
from jax.experimental.pallas import tpu as pltpu
from jax.sharding import PartitionSpec as P

SLOT_ROWS = 16
POS_ROW = 12
PAIRS = 8
BLOCK = 2 * PAIRS
BUFS = 8
LIST = 1024
STAGES = 4
LANES = 384
MB = 1 << 20
VMEM_TILES = 30 * MB


def iota(shape, dim):
    return lax.broadcasted_iota(jnp.int32, shape, dim)


def onehot(mask):
    return jnp.where(mask, 1.0, 0.0).astype(jnp.bfloat16)


def pack_kernel(home_ref, table_ref, out_ref):
    rows = table_ref.shape[0]
    blocks = home_ref.shape[1]
    home = home_ref[...]
    dest = home >> 9
    dest_f = dest.astype(jnp.float32)
    dest_col = jnp.broadcast_to(dest_f, (128, blocks)).T[:, :1]
    before = (dest_col == dest_f) & (iota((blocks, blocks), 0) < iota((blocks, blocks), 1))
    rank = jnp.sum(jnp.where(before, 1.0, 0.0), axis=0, keepdims=True).astype(jnp.int32)
    line = iota((16, blocks), 0)
    parts = jnp.where(line == 2, (home & 511) >> 1, home & 1)
    parts = jnp.where(line == 0, dest, jnp.where(line == 1, rank, parts))
    twice = onehot(iota((blocks, rows), 0) == (iota((blocks, rows), 1) >> 1))
    parts = jnp.dot(
        parts.astype(jnp.float32).astype(jnp.bfloat16), twice, preferred_element_type=jnp.float32
    ).astype(jnp.int32)
    dest = parts[:1]
    rank = parts[1:2] * 2 + (iota((1, rows), 1) & 1)
    place = dest * SLOT_ROWS + rank
    outs = out_ref.shape[0]
    spread = onehot(iota((outs, rows), 0) == place)
    data = jnp.dot(spread, table_ref[...], preferred_element_type=jnp.float32)
    lane = iota((256, rows), 0)
    high = jnp.broadcast_to((parts[2:3] + 1).astype(jnp.float32), (256, rows))
    low = jnp.broadcast_to(parts[3:4].astype(jnp.float32), (256, rows))
    marks = jnp.where(lane == rank, high, jnp.where(lane == rank + 128, low, 0.0)).astype(
        jnp.bfloat16
    )
    owner = onehot(iota((128, rows), 0) == dest)
    pos_rows = lax.dot_general(
        owner, marks, (((1,), (1,)), ((), ())), preferred_element_type=jnp.float32
    ).astype(jnp.bfloat16)
    lift = onehot(iota((outs, 128), 0) == iota((outs, 128), 1) * SLOT_ROWS + POS_ROW)
    data = data + jnp.dot(lift, pos_rows, preferred_element_type=jnp.float32)
    out_ref[...] = data.astype(jnp.bfloat16)


def unpack_kernel(in_ref, out_ref):
    ins = in_ref.shape[0]
    rows = out_ref.shape[0]
    data = in_ref[...]
    drop = onehot(iota((128, ins), 1) == iota((128, ins), 0) * SLOT_ROWS + POS_ROW)
    pos_rows = jnp.dot(drop, data, preferred_element_type=jnp.float32).astype(jnp.bfloat16)
    within = onehot(iota((128, ins), 0) == (iota((128, ins), 1) & (SLOT_ROWS - 1)))
    mine = (iota((128, ins), 1) >> 4) == iota((128, ins), 0)

    def lanes(part):
        spread = jnp.dot(part, within, preferred_element_type=jnp.float32)
        return jnp.sum(jnp.where(mine, spread, 0.0), axis=0, keepdims=True).astype(jnp.int32)

    high = lanes(pos_rows[:, :128])
    low = lanes(pos_rows[:, 128:])
    target = 4 * (high - 1) + 2 * low + (iota((1, ins), 1) & 1)
    pick = onehot(iota((rows, ins), 0) == target)
    out_ref[...] = jnp.dot(pick, data, preferred_element_type=jnp.float32).astype(jnp.bfloat16)


def ring_order(step):
    return jnp.where(step == 0, 0, jnp.where(step == 3, 1, jnp.where(step == 1, 2, 3)))


def plan_kernel(where_ref, count_ref, rows_ref, cols_ref, code_ref, start_ref):
    slots = rows_ref.shape[1]
    count = count_ref[0]
    x, core, z, y = where_ref[0], where_ref[1], where_ref[2], where_ref[3]
    row = rows_ref[...]
    col = cols_ref[...]
    source = col >> 3
    order_z = ring_order(((source >> 2) - z) & 3)
    order_y = ring_order(((source & 3) - y) & 3)
    outer = jnp.where(core == 0, order_z, order_y)
    inner = jnp.where(core == 0, order_y, order_z)
    stage = jnp.where(outer == 0, 0, jnp.where(outer == 3, 3, jnp.where(inner < 2, 1, 2)))
    side = (inner & 1) * 8 + jnp.where(outer == 2, 16, 0)
    tile = jnp.where((outer == 0) | (outer == 3), inner * 8, side) + (col & 7)
    owner = row >> 3
    dx = ((owner >> 1) - x) & 3
    order_x = jnp.where(dx == 2, 0, jnp.where(dx == 1, 1, jnp.where(dx == 3, 2, 3)))
    own = (owner & 1) == core
    chunk = jnp.where(order_x == 0, jnp.where(own, 1, 0), jnp.where(own, 4, 1) + order_x)
    key = stage * 64 + chunk * 8 + (row & 7)
    slot = iota((1, slots), 1)
    key = jnp.where(slot < count, key, 511)
    code = ((chunk * 8 + (row & 7)) << 18) + (slot << 8) + tile + 1

    def column(v):
        return jnp.broadcast_to(v.astype(jnp.float32), (128, slots)).T

    key_row = key.astype(jnp.float32)
    key_col = column(key)[:, :1]
    code_col = column(code)[:, :1]
    same = (key_col == key_row) & (iota((slots, slots), 1) < iota((slots, slots), 0))
    rank = jnp.sum(jnp.where(same, 1.0, 0.0), axis=1, keepdims=True)
    bucket = iota((slots, LANES), 1).astype(jnp.float32)
    member = key_col == bucket
    cnt = jnp.sum(jnp.where(member, 1.0, 0.0), axis=0, keepdims=True).astype(jnp.int32)
    pairs = jnp.broadcast_to((cnt + 1) >> 1, (16, LANES)).astype(jnp.float32).astype(jnp.bfloat16)
    a, b = iota((LANES, LANES), 0), iota((LANES, LANES), 1)

    same_stage = (a >> 6) == (b >> 6)
    opens = ((a & 63) == 0) & ((a >> 6) < (b >> 6))
    inside = jnp.dot(pairs, onehot(same_stage & (a < b)), preferred_element_type=jnp.float32)
    total = jnp.dot(pairs, onehot(same_stage), preferred_element_type=jnp.float32)
    blocks = ((total.astype(jnp.int32) + (PAIRS - 1)) >> 3).astype(jnp.float32)
    blocks = blocks.astype(jnp.bfloat16)
    ahead = jnp.dot(
        blocks, onehot(opens), preferred_element_type=jnp.float32
    )
    begin = (ahead * BLOCK + inside * 2.0)[:1]
    base = jnp.sum(jnp.where(member, begin, 0.0), axis=1, keepdims=True)
    live = iota((slots, 1), 0) < count
    place = jnp.where(live, base + rank, -1.0)
    lists = code_ref.shape[1]
    hit = place == iota((slots, lists), 1).astype(jnp.float32)
    code_ref[...] = jnp.sum(jnp.where(hit, code_col, 0.0), axis=0, keepdims=True).astype(jnp.int32)
    start_ref[...] = ahead[:1].astype(jnp.int32)


def fetch(block, code_ref, weights, wbuf, wsem):
    slot = lax.rem(block, BUFS)
    for i in range(BLOCK):
        s = (code_ref[block * BLOCK + i] >> 8) & 1023
        pltpu.make_async_copy(weights.at[s], wbuf.at[slot, i], wsem.at[slot]).start()


def arrive(block, weights, wbuf, wsem):
    slot = lax.rem(block, BUFS)
    pltpu.make_async_copy(weights.at[pl.ds(0, BLOCK)], wbuf.at[slot], wsem.at[slot]).wait()


def open_kernel(code_ref, start_ref, weights, acc, wbuf, wsem):
    total = start_ref[64 * STAGES]
    for i in range(BUFS - 1):
        pl.when(i < total)(functools.partial(fetch, i, code_ref, weights, wbuf, wsem))

    def clear(i, _):
        acc[i] = jnp.zeros(acc.shape[1:], acc.dtype)
        return 0

    lax.fori_loop(0, acc.shape[0], clear, 0)
    for i in range(BUFS - 1):
        pl.when(i < total)(functools.partial(arrive, i, weights, wbuf, wsem))


def tiles_kernel(stage, n_pieces, outs, *refs):
    code_ref, start_ref, weights = refs[:3]
    pieces = refs[3 : 3 + n_pieces]
    k = 5 + n_pieces
    acc, wbuf = refs[k : k + 2]
    out_refs = refs[k + 2 : k + 2 + len(outs)]
    panel, wsem, psem = refs[k + 2 + len(outs) :]
    first = start_ref[64 * stage]
    last = start_ref[64 * stage + 64]
    total = start_ref[64 * STAGES]
    ahead = BUFS - 1

    copies = []
    offset = 1
    for i, piece in enumerate(pieces):
        n = piece.shape[0]
        copies.append(pltpu.make_async_copy(piece, panel.at[pl.ds(offset, n)], psem.at[i]))
        offset += n
    for c in copies:
        c.start()
    panel[0] = jnp.zeros(panel.shape[1:], panel.dtype)
    fetched = first + ahead
    for c in copies:
        c.wait()

    def run_block(block, _):
        pl.when(block + ahead < total)(functools.partial(fetch, block + ahead, code_ref, weights, wbuf, wsem))
        pl.when(block >= fetched)(functools.partial(arrive, block, weights, wbuf, wsem))
        slot = lax.rem(block, BUFS)
        for u in range(PAIRS):
            c0 = code_ref[block * BLOCK + 2 * u]
            c1 = code_ref[block * BLOCK + 2 * u + 1]
            w = jnp.concatenate([wbuf[slot, 2 * u], wbuf[slot, 2 * u + 1]], axis=1)
            f = jnp.concatenate([panel[c0 & 255], panel[c1 & 255]], axis=0)
            acc[c0 >> 18] += jnp.dot(w, f, preferred_element_type=jnp.float32)
        return 0

    lax.fori_loop(first, last, run_block, 0)
    for out, (lo, n) in zip(out_refs, outs):

        def give(i, _, out=out, lo=lo):
            out[i] = acc[lo + i].astype(out.dtype)
            return 0

        lax.fori_loop(0, n, give, 0)
    for i in range(ahead):
        pl.when((last + i < total) & (last + i >= fetched))(
            functools.partial(arrive, last + i, weights, wbuf, wsem)
        )


def round_kernel(outs, acc, *out_refs):
    for out, (lo, n) in zip(out_refs, outs):

        def give(i, _, out=out, lo=lo):
            out[i] = acc[lo + i].astype(out.dtype)
            return 0

        lax.fori_loop(0, n, give, 0)


def round_rows(acc, outs):
    vmem = pl.BlockSpec(memory_space=pltpu.VMEM)
    return pl.pallas_call(
        functools.partial(round_kernel, outs),
        out_shape=[pltpu.VMEM((n, *acc.shape[1:]), jnp.bfloat16) for _, n in outs],
        in_specs=[vmem],
        out_specs=[vmem] * len(outs),
        compiler_params=pltpu.CompilerParams(vmem_limit_bytes=VMEM_TILES),
        cost_estimate=pl.CostEstimate(flops=1 << 22, bytes_accessed=12 * MB, transcendentals=0),
        name="round_rows",
    )(acc)


def open_tiles(code, start, weights, width):
    vmem = pl.BlockSpec(memory_space=pltpu.VMEM)
    smem = pl.BlockSpec(memory_space=pltpu.SMEM)
    t = weights.shape[1]
    return pl.pallas_call(
        open_kernel,
        out_shape=[
            pltpu.VMEM((64, t, width), jnp.float32),
            pltpu.VMEM((BUFS, BLOCK, t, t), jnp.bfloat16),
        ],
        in_specs=[smem, smem, pl.BlockSpec(memory_space=pl.ANY)],
        out_specs=[vmem, vmem],
        scratch_shapes=[pltpu.SemaphoreType.DMA((BUFS,))],
        compiler_params=pltpu.CompilerParams(vmem_limit_bytes=VMEM_TILES),
        name="tiles_open",
    )(code, start, weights)


def run_tiles(stage, code, start, weights, pieces, state, outs=()):
    any_spec = pl.BlockSpec(memory_space=pl.ANY)
    vmem = pl.BlockSpec(memory_space=pltpu.VMEM)
    smem = pl.BlockSpec(memory_space=pltpu.SMEM)
    t = weights.shape[1]
    pieces = [p.reshape(-1, t, p.shape[-1]) for p in pieces]
    n = len(pieces)
    tiles = sum(p.shape[0] for p in pieces) + 1
    f = pieces[0].shape[2]
    args = [code, start, weights, *pieces]
    in_specs = [smem, smem] + [any_spec] * (n + 1)
    aliases = {len(args) + i: i for i in range(len(state))}
    out_shape = [
        pltpu.VMEM((64, t, f), jnp.float32),
        pltpu.VMEM((BUFS, BLOCK, t, t), jnp.bfloat16),
    ] + [pltpu.VMEM((k, t, f), jnp.bfloat16) for _, k in outs]
    share = 352 * (tiles - 1) // 128
    return pl.pallas_call(
        functools.partial(tiles_kernel, stage, n, outs),
        out_shape=out_shape,
        in_specs=in_specs + [vmem] * len(state),
        out_specs=[vmem] * len(out_shape),
        scratch_shapes=[
            pltpu.VMEM((tiles, t, f), jnp.bfloat16),
            pltpu.SemaphoreType.DMA((BUFS,)),
            pltpu.SemaphoreType.DMA((n,)),
        ],
        input_output_aliases=aliases,
        compiler_params=pltpu.CompilerParams(vmem_limit_bytes=VMEM_TILES),
        cost_estimate=pl.CostEstimate(
            flops=share * 4 * t * t * f, bytes_accessed=share * 4 * t * t, transcendentals=0
        ),
        name=f"tiles_{stage}",
    )(*args, *state)


def panel_perm(turn, step):
    pairs = []
    for row in range(8):
        along_y = row % 2 == turn
        for z in range(4):
            for y in range(4):
                to = z * 4 + (y + step) % 4 if along_y else (z + step) % 4 * 4 + y
                pairs.append((row * 16 + z * 4 + y, row * 16 + to))
    return pairs


def row_perm(dx, flip=0):
    return [(x * 2 + c, (x + dx) % 4 * 2 + (c ^ flip)) for x in range(4) for c in range(2)]


def per_device(
    table, home, degree, tile_rows, tile_cols, tile_count, tile_values, w_self, w_neigh, bias
):
    rows, width = table.shape
    devices = lax.axis_size("row") * lax.axis_size("col")
    slots, tile = tile_values.shape[2:4]
    row_index = lax.axis_index("row")
    col_index = lax.axis_index("col")
    where = jnp.stack([row_index // 2, row_index % 2, col_index // 4, col_index % 4]).astype(
        jnp.int32
    )
    vmem = pl.BlockSpec(memory_space=pltpu.VMEM)
    smem = pl.BlockSpec(memory_space=pltpu.SMEM)
    big = pltpu.CompilerParams(vmem_limit_bytes=48 * MB)

    outgoing = pl.pallas_call(
        pack_kernel,
        out_shape=jax.ShapeDtypeStruct((devices * SLOT_ROWS, width), jnp.bfloat16),
        in_specs=[vmem, vmem],
        out_specs=vmem,
        compiler_params=big,
        name="pack",
    )(home.reshape(1, -1), table)
    incoming = lax.all_to_all(
        outgoing.reshape(devices, SLOT_ROWS, width),
        ("row", "col"),
        split_axis=0,
        concat_axis=0,
        tiled=True,
    )
    half = rows // 2
    owned = pl.pallas_call(
        unpack_kernel,
        out_shape=jax.ShapeDtypeStruct((rows, width), jnp.bfloat16),
        in_specs=[vmem],
        out_specs=vmem,
        compiler_params=big,
        name="unpack",
    )(incoming.reshape(devices * SLOT_ROWS, width))

    code, start = pl.pallas_call(
        plan_kernel,
        out_shape=(
            jax.ShapeDtypeStruct((1, LIST), jnp.int32),
            jax.ShapeDtypeStruct((1, LANES), jnp.int32),
        ),
        in_specs=[smem, smem, vmem, vmem],
        out_specs=(vmem, vmem),
        compiler_params=big,
        name="plan",
    )(where, tile_count.reshape(1), tile_rows.reshape(1, slots), tile_cols.reshape(1, slots))
    code = code.reshape(LIST)
    start = start.reshape(LANES)
    weights = tile_values.reshape(slots, tile, tile)

    def send(v, turn, step):
        return lax.ppermute(v, ("row", "col"), panel_perm(turn, step))

    def cat(*parts):
        return jnp.concatenate(parts, axis=0)

    plus, minus = send(owned, 0, 1), send(owned, 0, -1)
    state = open_tiles(code, start, weights, width)
    plus, minus, code, start, *state = lax.optimization_barrier((plus, minus, code, start, *state))
    hi = cat(minus, send(plus[:half], 0, 1), send(minus[half:], 0, -1))
    lo = cat(owned, plus)
    lists = (code, start, weights)
    lo_p, lo_m = send(lo, 1, 1), send(lo, 1, -1)
    hi_p, hi_m = send(hi, 1, 1), send(hi, 1, -1)
    state = run_tiles(0, *lists, [lo, hi], state)
    lo_p, lo_m, *state = lax.optimization_barrier((lo_p, lo_m, *state))
    far_lo = [send(lo_p[:rows], 1, 1), send(lo_m[rows:], 1, -1)]
    state = run_tiles(1, *lists, [lo_p, lo_m], state)
    hi_p, hi_m, *state = lax.optimization_barrier((hi_p, hi_m, *state))
    far_hi = [send(hi_p[:rows], 1, 1), send(hi_m[rows:], 1, -1)]
    state = run_tiles(2, *lists, [hi_p, hi_m], state)
    sums, _, other_far, mine_far = run_tiles(
        3, *lists, far_lo + far_hi, state, ((0, 8), (8, 8))
    )
    other_rest, mine_rest = round_rows(sums, ((16, 24), (40, 24)))

    f32 = jnp.float32

    def over(v, dx, flip=0):
        return lax.ppermute(v, "row", row_perm(dx, flip))

    got_far = over(other_far.reshape(rows, width), 0, 1)
    across = (mine_far.reshape(rows, width).astype(f32) + got_far.astype(f32)).astype(jnp.bfloat16)
    across, other_rest = lax.optimization_barrier((across, other_rest))
    from_minus, from_plus = over(across[:half], 1), over(across[half:], -1)
    got_rest = over(other_rest.reshape(3, rows, width), 0, 1)
    mine_rest = mine_rest.reshape(3, rows, width)
    both = [mine_rest[i].astype(f32) + got_rest[i].astype(f32) for i in range(3)]
    low = over(both[0][half:].astype(jnp.bfloat16), 1)
    high = over(both[1][:half].astype(jnp.bfloat16), -1)
    to_plus = (both[0][:half] + from_minus.astype(f32)).astype(jnp.bfloat16)
    to_minus = (both[1][half:] + from_plus.astype(f32)).astype(jnp.bfloat16)
    top = both[2][:half] + high.astype(f32)
    bottom = both[2][half:] + low.astype(f32)
    top, bottom = lax.optimization_barrier((top, bottom))
    last_top, last_bottom = over(to_plus, 1), over(to_minus, -1)
    summed = cat(top + last_top.astype(f32), bottom + last_bottom.astype(f32))

    neighbor_mean = (summed / degree.astype(f32)[:, None]).astype(jnp.bfloat16)
    total = jnp.dot(owned, w_self, preferred_element_type=f32)
    total = total + jnp.dot(neighbor_mean, w_neigh, preferred_element_type=f32)
    total = total + bias.astype(f32)[None, :]
    return jnp.maximum(total, f32(0.0)).astype(jnp.bfloat16)


def solution(mesh):
    in_specs = (
        P(("row", "col"), None),
        P(("row", "col")),
        P(("row", "col")),
        P("row", "col", None),
        P("row", "col", None),
        P("row", "col"),
        P("row", "col", None, None, None),
        P(),
        P(),
        P(),
    )
    out_specs = P(("row", "col"), None)
    return jax.shard_map(
        per_device, mesh=mesh, in_specs=in_specs, out_specs=out_specs, check_vma=False
    )
```
